256 devices in a mesh: scan: 64 (over y, z, core), mode: 4 (over x).
Axes of the slice: x: 4, y: 4, z: 8, core: 2. Of those that a mesh axis runs over, the one named last changes fastest.
Arguments:
- object_tiles: bfloat16 [512, 2, 2, 128, 128], P('scan'), may hold values from -5 to 5
- tile_owner: int32 [512], replicated, may hold values from 0 to 63, as said below
- block_tiles: int32 [64, 64], replicated, may hold values from 0 to 511, as said below
- positions: int32 [1024, 2], P('scan'), may hold values from 0 to 3968, as said below
- counts: int32 [1024, 128, 128], P('scan'), may hold values from 0 to 5
- probe: float32 [4, 2, 128, 128], P('mode'), may hold values from -3 to 3
Outputs:
- object_grad: float32 [512, 2, 2, 128, 128], P('scan', None, None, 'mode')
- probe_grad: float32 [4, 2, 128, 128], P('mode')
The draws below stay inside these ranges and needn't reach their ends.
Inputs may be any that keep to these rules, and one draw needn't show every extreme that they name: `tile_owner`: each scan index owns exactly 8 tiles, and the 64 tiles of any one row of block_tiles have 64 different owners. `block_tiles`: row b holds the tiles of a window of 2 consecutive tile rows and 32 consecutive tile columns of an object of 32 tile columns (tile t in tile row t // 32, column t % 32); slot s is the window's tile in window row s // 32 and window column s % 32. `positions`: row offsets run from 0 to 128 and column offsets from 0 to 3968, so every patch lies inside its block's window.
All inputs are finite; a program needn't handle non-finite values.
Results may differ from the reference program's by a relative error of at most 0.00055.
Values may be sent and summed in bfloat16 or wider, within the bound.
A program may use at most 128 MiB of HBM per device.

```python
import jax
import jax.numpy as jnp
from jax import lax

PAT = 128
SLICES = 2
TILE_COLS = 32
TILE_DEV = 8
POS_DEV = 16
MODES = 4
TILES = 512
SCAN_POS = 1024
N_SCAN = 64


def draw_tile_owner(key, part):
    key = jax.random.fold_in(key, 7)
    relabel = jax.random.permutation(key, N_SCAN)
    window_span = N_SCAN // 2
    tile_index = jnp.arange(TILES)
    cyclic = tile_index // TILE_COLS % 2 * window_span + tile_index % TILE_COLS % window_span
    return relabel[cyclic].astype(jnp.int32)


def draw_block_tiles(key, part):
    key = jax.random.fold_in(key, 11)
    row_key, col_key = jax.random.split(key)
    window_span = N_SCAN // 2
    tile_rows = TILES // TILE_COLS
    anchor_row = jax.random.randint(row_key, (N_SCAN,), 0, tile_rows - 1)
    anchor_col = jax.random.randint(col_key, (N_SCAN,), 0, TILE_COLS - window_span + 1)
    blocks = jnp.arange(N_SCAN)
    anchor_row = jnp.where(blocks == 0, tile_rows - 2, jnp.where(blocks == 1, 0, anchor_row))
    anchor_col = jnp.where(blocks == 0, TILE_COLS - window_span, jnp.where(blocks == 1, 0, anchor_col))
    slot_index = jnp.arange(N_SCAN)
    listed = (anchor_row[:, None] + slot_index[None, :] // window_span) * TILE_COLS + anchor_col[:, None] + slot_index[None, :] % window_span
    return listed.astype(jnp.int32)


def draw_positions(key, part):
    key = jax.random.fold_in(key, 5)
    row_key, col_key, pick_key = jax.random.split(key, 3)
    col_most = (N_SCAN // 2 - 1) * PAT
    row_offsets = jax.random.randint(row_key, (SCAN_POS,), 0, PAT + 1)
    col_offsets = jax.random.randint(col_key, (SCAN_POS,), 0, col_most + 1)
    chosen = jax.random.randint(pick_key, (N_SCAN,), 0, POS_DEV)
    position_index = jnp.arange(SCAN_POS)
    within_block = position_index % POS_DEV
    marked = chosen[position_index // POS_DEV]
    lowest = (marked + 1) % POS_DEV
    row_offsets = jnp.where(within_block == marked, PAT, jnp.where(within_block == lowest, 0, row_offsets))
    col_offsets = jnp.where(within_block == marked, col_most, jnp.where(within_block == lowest, 0, col_offsets))
    return jnp.stack([row_offsets, col_offsets], axis=1).astype(jnp.int32)


def touch_ends(drawn, rng, low, high):
    longest = drawn.shape.index(max(drawn.shape))
    spots = []
    for shift in (0, 1):
        where = [jax.random.randint(jax.random.fold_in(rng, axis), (), 0, length) for axis, length in enumerate(drawn.shape)]
        where[longest] = (where[longest] + shift) % drawn.shape[longest]
        spots.append(tuple(where))
    return drawn.at[spots[0]].set(low).at[spots[1]].set(high)


def steps_of(stream_key, shape, shards, smallest, high):
    gain = 1.0
    for axis_at, parts in shards:
        steps = jax.random.uniform(jax.random.fold_in(jax.random.fold_in(stream_key, 6), axis_at), (parts,), jnp.float32, smallest / len(shards), high / len(shards))
        gain = gain * jnp.repeat(jnp.exp(steps), shape[axis_at] // parts).reshape((-1,) + (1,) * (len(shape) - 1 - axis_at))
    return gain


def gaussian(stream_key, extent, scale, bound, cuts=(), held_as=jnp.bfloat16):
    values = jax.random.normal(stream_key, extent, jnp.float32) * scale
    if len(cuts) > 0:
        values = steps_of(stream_key, extent, cuts, -0.22, 0.18) * values
    return jnp.clip(values, min=-bound, max=bound).astype(held_as)


def setup_inputs(seed: int = 0) -> dict:
    arg_keys = jax.random.split(jax.random.key(seed), 7)
    return {
        "object_tiles": gaussian(arg_keys[0], (TILES, SLICES, 2, PAT, PAT), 0.8, 5.0, ((0, 64),)),
        "tile_owner": draw_tile_owner(jax.random.fold_in(arg_keys[6], 71), 0),
        "block_tiles": draw_block_tiles(jax.random.fold_in(arg_keys[6], 71), 0),
        "positions": draw_positions(jax.random.fold_in(arg_keys[6], 71), 0),
        "counts": touch_ends(jax.random.randint(arg_keys[4], (SCAN_POS, PAT, PAT), 0, 6), jax.random.fold_in(arg_keys[4], 1), 0, 5).astype(jnp.int32),
        "probe": gaussian(arg_keys[5], (MODES, 2, PAT, PAT), 0.5, 3.0, ((0, 4),), jnp.float32),
    }


background = 0.25
fresnel_number = 1.0
highest = lax.Precision.HIGHEST

def tables(pattern_side):
    index_range = jnp.arange(pattern_side, dtype=jnp.int32)
    product = index_range[:, None] * index_range[None, :] % pattern_side
    angles = 2.0 * jnp.pi / pattern_side * product.astype(jnp.float32)
    scaling = 1.0 / jnp.sqrt(jnp.float32(pattern_side))
    four_re = jnp.cos(angles) * scaling
    four_im = -jnp.sin(angles) * scaling
    frequency = jnp.where(index_range < pattern_side // 2, index_range, index_range - pattern_side).astype(jnp.float32) / pattern_side
    phases = -jnp.pi * fresnel_number * frequency * frequency
    chirp_re = jnp.cos(phases)
    chirp_im = jnp.sin(phases)
    left_re = four_re * chirp_re[None, :] + four_im * chirp_im[None, :]
    left_im = four_re * chirp_im[None, :] - four_im * chirp_re[None, :]
    prop_re = jnp.dot(left_re, four_re, precision=highest) - jnp.dot(left_im, four_im, precision=highest)
    prop_im = jnp.dot(left_re, four_im, precision=highest) + jnp.dot(left_im, four_re, precision=highest)
    return (four_re, four_im, prop_re, prop_im)

def two_sided(matrix_re, matrix_im, field_re, field_im):
    half_re = jnp.einsum('jk,bkl->bjl', matrix_re, field_re, precision=highest) - jnp.einsum('jk,bkl->bjl', matrix_im, field_im, precision=highest)
    half_im = jnp.einsum('jk,bkl->bjl', matrix_re, field_im, precision=highest) + jnp.einsum('jk,bkl->bjl', matrix_im, field_re, precision=highest)
    full_re = jnp.einsum('bjk,kl->bjl', half_re, matrix_re, precision=highest) - jnp.einsum('bjk,kl->bjl', half_im, matrix_im, precision=highest)
    full_im = jnp.einsum('bjk,kl->bjl', half_re, matrix_im, precision=highest) + jnp.einsum('bjk,kl->bjl', half_im, matrix_re, precision=highest)
    return (full_re, full_im)

def forward(probe_re, probe_im, obj_re, obj_im, dft_tables):
    four_re, four_im, prop_re, prop_im = dft_tables
    batch_size = obj_re.shape[1]
    wave_re = jnp.broadcast_to(probe_re, (batch_size,) + probe_re.shape)
    wave_im = jnp.broadcast_to(probe_im, (batch_size,) + probe_im.shape)
    waves = []
    depth_count = obj_re.shape[0]
    for depth_index in range(depth_count):
        waves.append((wave_re, wave_im))
        exit_re = wave_re * obj_re[depth_index] - wave_im * obj_im[depth_index]
        exit_im = wave_re * obj_im[depth_index] + wave_im * obj_re[depth_index]
        if depth_index + 1 < depth_count:
            wave_re, wave_im = two_sided(prop_re, prop_im, exit_re, exit_im)
        else:
            far_re, far_im = two_sided(four_re, four_im, exit_re, exit_im)
    return (waves, far_re, far_im)

def backward(waves, far_re, far_im, weight, obj_re, obj_im, dft_tables):
    four_re, four_im, prop_re, prop_im = dft_tables
    depth_count = obj_re.shape[0]
    grad_re, grad_im = two_sided(four_re, -four_im, weight * far_re, weight * far_im)
    terms_re = [None] * depth_count
    terms_im = [None] * depth_count
    for depth_index in reversed(range(depth_count)):
        wave_re, wave_im = waves[depth_index]
        terms_re[depth_index] = wave_re * grad_re + wave_im * grad_im
        terms_im[depth_index] = wave_re * grad_im - wave_im * grad_re
        back_re = obj_re[depth_index] * grad_re + obj_im[depth_index] * grad_im
        back_im = obj_re[depth_index] * grad_im - obj_im[depth_index] * grad_re
        if depth_index > 0:
            grad_re, grad_im = two_sided(prop_re, -prop_im, back_re, back_im)
    return (jnp.stack(terms_re), jnp.stack(terms_im), lax.optimization_barrier(jnp.sum(back_re, axis=0)), lax.optimization_barrier(jnp.sum(back_im, axis=0)))

def reference(object_tiles, tile_owner, block_tiles, positions, counts, probe):
    dft_tables = tables(PAT)
    window_span = N_SCAN // 2
    owner_range = jnp.arange(N_SCAN, dtype=jnp.int32)
    owner_hot = (tile_owner[:, None] == owner_range[None, :]).astype(jnp.int32)
    rank_all = lax.optimization_barrier(jnp.sum((jnp.cumsum(owner_hot, axis=0) - owner_hot) * owner_hot, axis=1))
    storage_row = (tile_owner * TILE_DEV + rank_all).astype(jnp.int32)
    by_tile = object_tiles[storage_row]
    anchor_zero = jnp.int32(0)

    def block_step(carry, inputs):
        grad_store, probe_total = carry
        tile_list, offsets, block_counts = inputs
        slot_tiles = by_tile[tile_list]
        window = slot_tiles.reshape(2, window_span, SLICES, 2, PAT, PAT).transpose(2, 3, 0, 4, 1, 5).reshape(SLICES, 2, 2 * PAT, window_span * PAT)

        def cut_patch(offset):
            return lax.dynamic_slice(window, (anchor_zero, anchor_zero, offset[0], offset[1]), (SLICES, 2, PAT, PAT))
        patches = jax.vmap(cut_patch)(offsets).astype(jnp.float32)
        obj_re = jnp.transpose(patches[:, :, 0], (1, 0, 2, 3))
        obj_im = jnp.transpose(patches[:, :, 1], (1, 0, 2, 3))
        mode_runs = [forward(probe[mode_index, 0], probe[mode_index, 1], obj_re, obj_im, dft_tables) for mode_index in range(MODES)]
        intensity = jnp.full(block_counts.shape, background, jnp.float32)
        for run_entry in mode_runs:
            intensity = intensity + run_entry[1] * run_entry[1] + run_entry[2] * run_entry[2]
        weight = 1.0 - block_counts.astype(jnp.float32) / intensity
        total_re = jnp.zeros_like(obj_re)
        total_im = jnp.zeros_like(obj_im)
        probe_parts = []
        for run_entry in mode_runs:
            terms_re, terms_im, probe_re, probe_im = backward(run_entry[0], run_entry[1], run_entry[2], weight, obj_re, obj_im, dft_tables)
            total_re = total_re + terms_re
            total_im = total_im + terms_im
            probe_parts.append(jnp.stack([probe_re, probe_im]))
        terms = jnp.transpose(jnp.stack([total_re, total_im], axis=1), (2, 0, 1, 3, 4))

        def place(position, canvas):
            start = (anchor_zero, anchor_zero, offsets[position, 0], offsets[position, 1])
            current = lax.dynamic_slice(canvas, start, (SLICES, 2, PAT, PAT))
            return lax.dynamic_update_slice(canvas, current + terms[position], start)
        canvas = lax.fori_loop(0, POS_DEV, place, jnp.zeros((SLICES, 2, 2 * PAT, window_span * PAT), jnp.float32))
        slot_grads = canvas.reshape(SLICES, 2, 2, PAT, window_span, PAT).transpose(2, 4, 0, 1, 3, 5).reshape(N_SCAN, SLICES, 2, PAT, PAT)
        grad_store = grad_store.at[storage_row[tile_list]].add(slot_grads)
        return ((grad_store, probe_total + jnp.stack(probe_parts)), None)
    start_carry = (jnp.zeros((TILES, SLICES, 2, PAT, PAT), jnp.float32), jnp.zeros((MODES, 2, PAT, PAT), jnp.float32))
    inputs = (block_tiles, positions.reshape(N_SCAN, POS_DEV, 2), counts.reshape(N_SCAN, POS_DEV, PAT, PAT))
    final_carry, unused = lax.scan(block_step, start_carry, inputs)
    return (final_carry[0], final_carry[1] / SCAN_POS)
```

```python
import functools

import jax
import jax.numpy as jnp
import ml_dtypes
import numpy as np
from jax import lax
from jax.experimental import pallas as pl
from jax.experimental.pallas import tpu as pltpu
from jax.sharding import PartitionSpec as P

background = 0.25
fresnel_number = 1.0
MIB = 1024 * 1024


def split_const(matrix):
    hi = matrix.astype(ml_dtypes.bfloat16)
    lo = (matrix - hi.astype(np.float64)).astype(ml_dtypes.bfloat16)
    return hi, lo


def transform_tables(side):
    index = np.arange(side)
    four = np.exp(-2j * np.pi * (index[:, None] * index[None, :] % side) / side) / np.sqrt(side)
    frequency = np.where(index < side // 2, index, index - side) / side
    chirp = np.exp(-1j * np.pi * fresnel_number * frequency * frequency)
    prop = (four.conj() * chirp[None, :]) @ four
    blocks = []
    for matrix in (four, prop):
        re, im = matrix.real, matrix.imag
        blocks.append(np.block([[re, im], [-im, re]]))
        blocks.append(np.block([[re, -im], [im, re]]))
    parts = []
    for block in blocks:
        parts.extend(split_const(block))
    return np.stack(parts)


def split_parts(value):
    hi = value.astype(jnp.bfloat16)
    lo = (value - hi.astype(jnp.float32)).astype(jnp.bfloat16)
    return hi, lo


def dot(a, b):
    return jnp.dot(a, b, preferred_element_type=jnp.float32)


def compute_kernel(rc_ref, q_ref, x_ref, probe_ref, counts_ref, tab_ref, e_ref, pg_ref, a_hi, a_lo, c_hi, c_lo, xs, p1, es):
    side = probe_ref.shape[-1]
    modes = probe_ref.shape[0]
    npos = x_ref.shape[1]
    quarter = x_ref.shape[3]
    nq = x_ref.shape[0]

    def block(m):
        return slice(m * side, (m + 1) * side)

    def two_sided(right, left, fields):
        for m, (re, im) in enumerate(fields):
            rh, rl = split_parts(re)
            ih, il = split_parts(im)
            a_hi[block(m), 0:side] = rh
            a_hi[block(m), side : 2 * side] = ih
            a_lo[block(m), 0:side] = rl
            a_lo[block(m), side : 2 * side] = il
        for m in range(modes):
            bh, bl = tab_ref[2 * right], tab_ref[2 * right + 1]
            y = dot(a_hi[block(m)], bh) + dot(a_lo[block(m)], bh) + dot(a_hi[block(m)], bl)
            hi, lo = split_parts(y)
            c_hi[0:side, block(m)] = hi[:, 0:side]
            c_hi[side : 2 * side, block(m)] = hi[:, side : 2 * side]
            c_lo[0:side, block(m)] = lo[:, 0:side]
            c_lo[side : 2 * side, block(m)] = lo[:, side : 2 * side]
        lh, ll = tab_ref[2 * left], tab_ref[2 * left + 1]
        out = []
        for h in range(modes // 2):
            cols = slice(h * 2 * side, (h + 1) * 2 * side)
            z = dot(lh, c_hi[:, cols]) + dot(lh, c_lo[:, cols]) + dot(ll, c_hi[:, cols])
            for k in range(2):
                out.append((z[0:side, block(k)], z[side : 2 * side, block(k)]))
        return out

    pg_ref[...] = jnp.zeros_like(pg_ref)

    def position(p, carry):
        row = rc_ref[p, 0]
        col = rc_ref[p, 1]
        for plane in range(4):
            whole = jnp.concatenate([x_ref[k, p, plane].astype(jnp.float32) for k in range(nq)], axis=0)
            whole = pltpu.roll(whole, (side - row) % side, 0)
            xs[plane] = pltpu.roll(whole, (side - col) % side, 1)
        fields = []
        for m in range(modes):
            pr, pi = probe_ref[m, 0], probe_ref[m, 1]
            xr, xi = xs[0], xs[1]
            fields.append((pr * xr - pi * xi, pr * xi + pi * xr))
        waves = two_sided(2, 3, fields)
        fields = []
        for m in range(modes):
            wr, wi = waves[m]
            p1[m, 0] = wr
            p1[m, 1] = wi
            xr, xi = xs[2], xs[3]
            fields.append((wr * xr - wi * xi, wr * xi + wi * xr))
        far = two_sided(0, 1, fields)
        intensity = background
        for re, im in far:
            intensity = intensity + (re * re + im * im)
        weight = 1.0 - counts_ref[p].astype(jnp.float32) / intensity
        grads = two_sided(1, 0, [(weight * re, weight * im) for re, im in far])
        fields = []
        er = ei = 0.0
        for m in range(modes):
            gr, gi = grads[m]
            wr, wi = p1[m, 0], p1[m, 1]
            er = er + (wr * gr + wi * gi)
            ei = ei + (wr * gi - wi * gr)
            xr, xi = xs[2], xs[3]
            fields.append((xr * gr + xi * gi, xr * gi - xi * gr))
        es[2] = er
        es[3] = ei
        grads = two_sided(3, 2, fields)
        er = ei = 0.0
        for m in range(modes):
            gr, gi = grads[m]
            wr, wi = probe_ref[m, 0], probe_ref[m, 1]
            er = er + (wr * gr + wi * gi)
            ei = ei + (wr * gi - wi * gr)
            xr, xi = xs[0], xs[1]
            pg_ref[m, 0] += xr * gr + xi * gi
            pg_ref[m, 1] += xr * gi - xi * gr
        es[0] = er
        es[1] = ei
        for plane in range(4):
            whole = pltpu.roll(pltpu.roll(es[plane], row, 0), col, 1)
            for k in range(nq):
                e_ref[k, p, plane] = whole[k * quarter : (k + 1) * quarter]
        return carry

    lax.fori_loop(0, npos, position, 0)


def compute(rc, q, x, probe_all, counts, tables):
    nq, npos, planes, quarter, side = x.shape
    modes = probe_all.shape[0]
    return pl.pallas_call(
        compute_kernel,
        grid_spec=pltpu.PrefetchScalarGridSpec(
            num_scalar_prefetch=2,
            grid=(1,),
            in_specs=[
                pl.BlockSpec(x.shape, lambda i, rc, q: (0, 0, 0, 0, 0)),
                pl.BlockSpec(probe_all.shape, lambda i, rc, q: (0, 0, 0, 0)),
                pl.BlockSpec((npos, side, side), lambda i, rc, q: (q[0], 0, 0)),
                pl.BlockSpec(tables.shape, lambda i, rc, q: (0, 0, 0)),
            ],
            out_specs=[
                pl.BlockSpec(x.shape, lambda i, rc, q: (0, 0, 0, 0, 0)),
                pl.BlockSpec(probe_all.shape, lambda i, rc, q: (0, 0, 0, 0)),
            ],
            scratch_shapes=[
                pltpu.VMEM((modes * side, 2 * side), jnp.bfloat16),
                pltpu.VMEM((modes * side, 2 * side), jnp.bfloat16),
                pltpu.VMEM((2 * side, modes * side), jnp.bfloat16),
                pltpu.VMEM((2 * side, modes * side), jnp.bfloat16),
                pltpu.VMEM((4, side, side), jnp.float32),
                pltpu.VMEM((modes, 2, side, side), jnp.float32),
                pltpu.VMEM((4, side, side), jnp.float32),
            ],
        ),
        out_shape=[
            jax.ShapeDtypeStruct(x.shape, jnp.float32),
            jax.ShapeDtypeStruct(probe_all.shape, jnp.float32),
        ],
        compiler_params=pltpu.CompilerParams(vmem_limit_bytes=40 * MIB),
        name="fields",
    )(rc, q, x, probe_all, counts, tables)


def residue_masks(row, col, first_row, shape):
    rows = lax.broadcasted_iota(jnp.int32, shape, len(shape) - 2) + first_row
    cols = lax.broadcasted_iota(jnp.int32, shape, len(shape) - 1)
    return rows >= row, cols >= col


def cut_kernel(place_ref, q_ref, win_ref, out_ref):
    quarter = win_ref.shape[2]

    def position(j, carry):
        up, left = residue_masks(place_ref[j, 4], place_ref[j, 5], q_ref[0] * quarter, win_ref.shape[1:])
        tiles = [win_ref[place_ref[j, k]].astype(jnp.float32) for k in range(4)]
        upper = jnp.where(left, tiles[0], tiles[1])
        lower = jnp.where(left, tiles[2], tiles[3])
        out_ref[j] = jnp.where(up, upper, lower).astype(jnp.bfloat16)
        return carry

    lax.fori_loop(0, out_ref.shape[0], position, 0)


def cut(place, q, window):
    npos = place.shape[0]
    return pl.pallas_call(
        cut_kernel,
        in_specs=[
            pl.BlockSpec(memory_space=pltpu.SMEM),
            pl.BlockSpec(memory_space=pltpu.SMEM),
            pl.BlockSpec(memory_space=pltpu.VMEM),
        ],
        out_specs=pl.BlockSpec(memory_space=pltpu.VMEM),
        out_shape=jax.ShapeDtypeStruct((npos,) + window.shape[1:], window.dtype),
        compiler_params=pltpu.CompilerParams(vmem_limit_bytes=32 * MIB),
        name="cut",
    )(place, q, window)


def lay_kernel(place_ref, q_ref, e_ref, out_ref):
    quarter = e_ref.shape[2]
    out_ref[...] = jnp.zeros_like(out_ref)

    def position(j, carry):
        up, left = residue_masks(place_ref[j, 4], place_ref[j, 5], q_ref[0] * quarter, e_ref.shape[1:])
        term = e_ref[j]
        upper = jnp.where(up, term, 0.0)
        lower = jnp.where(up, 0.0, term)
        out_ref[place_ref[j, 0]] += jnp.where(left, upper, 0.0)
        out_ref[place_ref[j, 1]] += jnp.where(left, 0.0, upper)
        out_ref[place_ref[j, 2]] += jnp.where(left, lower, 0.0)
        out_ref[place_ref[j, 3]] += jnp.where(left, 0.0, lower)
        return carry

    lax.fori_loop(0, e_ref.shape[0], position, 0)


def lay(place, q, terms, slots):
    return pl.pallas_call(
        lay_kernel,
        in_specs=[
            pl.BlockSpec(memory_space=pltpu.SMEM),
            pl.BlockSpec(memory_space=pltpu.SMEM),
            pl.BlockSpec(memory_space=pltpu.VMEM),
        ],
        out_specs=pl.BlockSpec(memory_space=pltpu.VMEM),
        out_shape=jax.ShapeDtypeStruct((slots,) + terms.shape[1:], terms.dtype),
        compiler_params=pltpu.CompilerParams(vmem_limit_bytes=32 * MIB),
        name="lay",
    )(place, q, terms)


def land_kernel(rows_ref, in_ref, out_ref):
    out_ref[...] = jnp.zeros_like(out_ref)

    def block(b, carry):
        out_ref[rows_ref[b]] += in_ref[b]
        return carry

    lax.fori_loop(0, in_ref.shape[0], block, 0)


def land(rows, returned, tile_dev):
    return pl.pallas_call(
        land_kernel,
        in_specs=[pl.BlockSpec(memory_space=pltpu.SMEM), pl.BlockSpec(memory_space=pltpu.VMEM)],
        out_specs=pl.BlockSpec(memory_space=pltpu.VMEM),
        out_shape=jax.ShapeDtypeStruct((tile_dev,) + returned.shape[1:], returned.dtype),
        compiler_params=pltpu.CompilerParams(vmem_limit_bytes=32 * MIB),
        name="land",
    )(rows, returned)


def shards(object_tiles, tile_owner, block_tiles, positions, counts, probe):
    scan_count = lax.axis_size("scan")
    mode_count = lax.axis_size("mode")
    scan_here = lax.axis_index("scan")
    mode_here = lax.axis_index("mode")
    tile_dev, slices, parts, side = object_tiles.shape[:4]
    batch = positions.shape[0]
    span = scan_count // 2
    quarter = side // mode_count
    npos = batch // mode_count
    planes = slices * parts
    tables = jnp.asarray(transform_tables(side))

    first = block_tiles[:, 0]
    tiles = tile_owner.shape[0]
    tile_range = jnp.arange(tiles, dtype=jnp.int32)
    same = (tile_owner[:, None] == tile_owner[None, :]) & (tile_range[None, :] < tile_range[:, None])
    rank = jnp.sum(same.astype(jnp.int32), axis=1)
    listed = (tile_range[None, :] >= first[:, None]) & (tile_range[None, :] < first[:, None] + scan_count)
    mine = listed & (tile_owner == scan_here)[None, :]
    local_rows = jnp.sum(jnp.where(mine, rank[None, :], 0), axis=1)
    my_first = lax.dynamic_index_in_dim(first, scan_here, 0, keepdims=False)
    slot_owner = lax.dynamic_slice(tile_owner, (my_first,), (scan_count,))
    q = mode_here.reshape(1)
    up, left = positions[:, 0] // side, positions[:, 1] // side
    down, right = jnp.minimum(up + 1, 1), jnp.minimum(left + 1, span - 1)
    slots = jnp.stack([up * span + left, up * span + right, down * span + left, down * span + right], axis=1)
    rc = positions % side
    place = jnp.concatenate([slot_owner[slots], rc], axis=1)

    part = lax.dynamic_slice_in_dim(object_tiles, mode_here * quarter, quarter, 3).reshape(
        tile_dev, planes, quarter, side
    )
    window = lax.all_to_all(part[local_rows], "scan", split_axis=0, concat_axis=0, tiled=True)
    pieces = cut(place, q, window)
    probe_all = lax.all_gather(probe, "mode", axis=0, tiled=True)
    x = lax.all_to_all(
        pieces.reshape(mode_count, npos, planes, quarter, side), "mode", split_axis=0, concat_axis=0, tiled=True
    )
    my_rc = lax.dynamic_slice_in_dim(rc, mode_here * npos, npos, 0)
    terms, probe_terms = compute(my_rc, q, x, probe_all, counts, tables)
    probe_part = lax.psum_scatter(probe_terms, "mode", scatter_dimension=0, tiled=True)
    probe_grad = lax.psum(probe_part, "scan") / (batch * scan_count)
    back = lax.all_to_all(terms, "mode", split_axis=0, concat_axis=0, tiled=True)
    canvas = lay(place, q, back.reshape(batch, planes, quarter, side), scan_count)
    returned = lax.all_to_all(canvas, "scan", split_axis=0, concat_axis=0, tiled=True)
    summed = land(local_rows, returned, tile_dev)
    return (summed.reshape(tile_dev, slices, parts, quarter, side), probe_grad)


def solution(mesh):
    placed = (
        P("scan", None, None, None, None),
        P(),
        P(),
        P("scan", None),
        P("scan", None, None),
        P("mode", None, None, None),
    )
    return jax.shard_map(
        shards,
        mesh=mesh,
        in_specs=placed,
        out_specs=(P("scan", None, None, "mode", None), P("mode", None, None, None)),
        check_vma=False,
    )
```

```python
import functools

import jax
import jax.numpy as jnp
import ml_dtypes
import numpy as np
from jax import lax
from jax.experimental import pallas as pl
from jax.experimental.pallas import tpu as pltpu
from jax.sharding import PartitionSpec as P

background = 0.25
fresnel_number = 1.0
MIB = 1024 * 1024
RING = 8


def split_const(matrix):
    hi = matrix.astype(ml_dtypes.bfloat16)
    lo = (matrix - hi.astype(np.float64)).astype(ml_dtypes.bfloat16)
    return hi, lo


def transform_tables(side):
    index = np.arange(side)
    four = np.exp(-2j * np.pi * (index[:, None] * index[None, :] % side) / side) / np.sqrt(side)
    frequency = np.where(index < side // 2, index, index - side) / side
    chirp = np.exp(-1j * np.pi * fresnel_number * frequency * frequency)
    prop = (four.conj() * chirp[None, :]) @ four
    blocks = []
    for matrix in (four, prop):
        re, im = matrix.real, matrix.imag
        blocks.append(np.block([[re, im], [-im, re]]))
        blocks.append(np.block([[re, -im], [im, re]]))
    parts = []
    for block in blocks:
        parts.extend(split_const(block))
    return np.stack(parts)


def split_parts(value):
    hi = value.astype(jnp.bfloat16)
    lo = (value - hi.astype(jnp.float32)).astype(jnp.bfloat16)
    return hi, lo


def dot(a, b):
    return jnp.dot(a, b, preferred_element_type=jnp.float32)


def compute_kernel(rc_ref, q_ref, x_ref, probe_ref, counts_ref, tab_ref, e_ref, pg_ref, a_hi, a_lo, c_hi, c_lo, xs, p1, es):
    side = probe_ref.shape[-1]
    modes = probe_ref.shape[0]
    npos = x_ref.shape[1]
    quarter = x_ref.shape[3]
    nq = x_ref.shape[0]

    def block(m):
        return slice(m * side, (m + 1) * side)

    def two_sided(right, left, fields):
        for m, (re, im) in enumerate(fields):
            rh, rl = split_parts(re)
            ih, il = split_parts(im)
            a_hi[block(m), 0:side] = rh
            a_hi[block(m), side : 2 * side] = ih
            a_lo[block(m), 0:side] = rl
            a_lo[block(m), side : 2 * side] = il
        for m in range(modes):
            bh, bl = tab_ref[2 * right], tab_ref[2 * right + 1]
            y = dot(a_hi[block(m)], bh) + dot(a_lo[block(m)], bh) + dot(a_hi[block(m)], bl)
            hi, lo = split_parts(y)
            c_hi[0:side, block(m)] = hi[:, 0:side]
            c_hi[side : 2 * side, block(m)] = hi[:, side : 2 * side]
            c_lo[0:side, block(m)] = lo[:, 0:side]
            c_lo[side : 2 * side, block(m)] = lo[:, side : 2 * side]
        lh, ll = tab_ref[2 * left], tab_ref[2 * left + 1]
        out = []
        for h in range(modes // 2):
            cols = slice(h * 2 * side, (h + 1) * 2 * side)
            z = dot(lh, c_hi[:, cols]) + dot(lh, c_lo[:, cols]) + dot(ll, c_hi[:, cols])
            for k in range(2):
                out.append((z[0:side, block(k)], z[side : 2 * side, block(k)]))
        return out

    pg_ref[...] = jnp.zeros_like(pg_ref)

    def position(p, carry):
        row = rc_ref[q_ref[0] * npos + p, 4]
        col = rc_ref[q_ref[0] * npos + p, 5]
        for plane in range(4):
            whole = jnp.concatenate([x_ref[k, p, plane].astype(jnp.float32) for k in range(nq)], axis=0)
            whole = pltpu.roll(whole, (side - row) % side, 0)
            xs[plane] = pltpu.roll(whole, (side - col) % side, 1)
        fields = []
        for m in range(modes):
            pr, pi = probe_ref[m, 0], probe_ref[m, 1]
            xr, xi = xs[0], xs[1]
            fields.append((pr * xr - pi * xi, pr * xi + pi * xr))
        waves = two_sided(2, 3, fields)
        fields = []
        for m in range(modes):
            wr, wi = waves[m]
            p1[m, 0] = wr
            p1[m, 1] = wi
            xr, xi = xs[2], xs[3]
            fields.append((wr * xr - wi * xi, wr * xi + wi * xr))
        far = two_sided(0, 1, fields)
        intensity = background
        for re, im in far:
            intensity = intensity + (re * re + im * im)
        weight = 1.0 - counts_ref[p].astype(jnp.float32) / intensity
        grads = two_sided(1, 0, [(weight * re, weight * im) for re, im in far])
        fields = []
        er = ei = 0.0
        for m in range(modes):
            gr, gi = grads[m]
            wr, wi = p1[m, 0], p1[m, 1]
            er = er + (wr * gr + wi * gi)
            ei = ei + (wr * gi - wi * gr)
            xr, xi = xs[2], xs[3]
            fields.append((xr * gr + xi * gi, xr * gi - xi * gr))
        es[2] = er
        es[3] = ei
        grads = two_sided(3, 2, fields)
        er = ei = 0.0
        for m in range(modes):
            gr, gi = grads[m]
            wr, wi = probe_ref[m, 0], probe_ref[m, 1]
            er = er + (wr * gr + wi * gi)
            ei = ei + (wr * gi - wi * gr)
            xr, xi = xs[0], xs[1]
            pg_ref[m, 0] += xr * gr + xi * gi
            pg_ref[m, 1] += xr * gi - xi * gr
        es[0] = er
        es[1] = ei
        for plane in range(4):
            whole = pltpu.roll(pltpu.roll(es[plane], row, 0), col, 1)
            for k in range(nq):
                e_ref[k, p, plane] = whole[k * quarter : (k + 1) * quarter]
        return carry

    lax.fori_loop(0, npos, position, 0)


def compute(rc, q, x, probe_all, counts, tables):
    nq, npos, planes, quarter, side = x.shape
    modes = probe_all.shape[0]
    return pl.pallas_call(
        compute_kernel,
        grid_spec=pltpu.PrefetchScalarGridSpec(
            num_scalar_prefetch=2,
            grid=(1,),
            in_specs=[
                pl.BlockSpec(x.shape, lambda i, rc, q: (0, 0, 0, 0, 0)),
                pl.BlockSpec(probe_all.shape, lambda i, rc, q: (0, 0, 0, 0)),
                pl.BlockSpec((npos, side, side), lambda i, rc, q: (q[0], 0, 0)),
                pl.BlockSpec(tables.shape, lambda i, rc, q: (0, 0, 0)),
            ],
            out_specs=[
                pl.BlockSpec(x.shape, lambda i, rc, q: (0, 0, 0, 0, 0)),
                pl.BlockSpec(probe_all.shape, lambda i, rc, q: (0, 0, 0, 0)),
            ],
            scratch_shapes=[
                pltpu.VMEM((modes * side, 2 * side), jnp.bfloat16),
                pltpu.VMEM((modes * side, 2 * side), jnp.bfloat16),
                pltpu.VMEM((2 * side, modes * side), jnp.bfloat16),
                pltpu.VMEM((2 * side, modes * side), jnp.bfloat16),
                pltpu.VMEM((4, side, side), jnp.float32),
                pltpu.VMEM((modes, 2, side, side), jnp.float32),
                pltpu.VMEM((4, side, side), jnp.float32),
            ],
        ),
        out_shape=[
            jax.ShapeDtypeStruct(x.shape, jnp.float32),
            jax.ShapeDtypeStruct(probe_all.shape, jnp.float32),
        ],
        compiler_params=pltpu.CompilerParams(vmem_limit_bytes=40 * MIB),
        name="fields",
    )(rc, q, x, probe_all, counts, tables)


def residue_masks(row, col, first_row, shape):
    rows = lax.broadcasted_iota(jnp.int32, shape, len(shape) - 2) + first_row
    cols = lax.broadcasted_iota(jnp.int32, shape, len(shape) - 1)
    return rows >= row, cols >= col


def lay_kernel(place_ref, q_ref, e_ref, out_ref):
    quarter = e_ref.shape[2]
    out_ref[...] = jnp.zeros_like(out_ref)

    def position(j, carry):
        up, left = residue_masks(place_ref[j, 4], place_ref[j, 5], q_ref[0] * quarter, e_ref.shape[1:])
        term = e_ref[j]
        upper = jnp.where(up, term, 0.0)
        lower = jnp.where(up, 0.0, term)
        out_ref[place_ref[j, 0]] += jnp.where(left, upper, 0.0)
        out_ref[place_ref[j, 1]] += jnp.where(left, 0.0, upper)
        out_ref[place_ref[j, 2]] += jnp.where(left, lower, 0.0)
        out_ref[place_ref[j, 3]] += jnp.where(left, 0.0, lower)
        return carry

    lax.fori_loop(0, e_ref.shape[0], position, 0)


def lay(place, q, terms, slots):
    return pl.pallas_call(
        lay_kernel,
        in_specs=[
            pl.BlockSpec(memory_space=pltpu.SMEM),
            pl.BlockSpec(memory_space=pltpu.SMEM),
            pl.BlockSpec(memory_space=pltpu.VMEM),
        ],
        out_specs=pl.BlockSpec(memory_space=pltpu.VMEM),
        out_shape=jax.ShapeDtypeStruct((slots,) + terms.shape[1:], terms.dtype),
        compiler_params=pltpu.CompilerParams(vmem_limit_bytes=32 * MIB),
        name="lay",
    )(place, q, terms)


def spot(scan):
    return scan // (2 * RING), scan // 2 % RING, scan % 2


def at_spot(y, z, core):
    return (y * RING + z) * 2 + core


def plane_peers(y, z, core):
    peers = []
    for number in range(1, 8):
        there_y, there_core = (y + number // 2) % 4, (core + number % 2) % 2
        peers.append((number - 1, at_spot(there_y, z, there_core), there_y * 2 + there_core))
    return peers


def plane_sources(y, core):
    return [(y - number // 2 + 4) % 4 * 2 + (core + number % 2) % 2 for number in range(1, 8)]


def send(src, dst, send_sem, recv_sem, scan, mode):
    return pltpu.make_async_remote_copy(
        src_ref=src,
        dst_ref=dst,
        send_sem=send_sem,
        recv_sem=recv_sem,
        device_id={"scan": scan, "mode": mode},
        device_id_type=pl.DeviceIdType.MESH,
    )


def meet(partners):
    barrier = pltpu.get_barrier_semaphore()
    for scan, mode in partners:
        pl.semaphore_signal(
            barrier, inc=1, device_id={"scan": scan, "mode": mode}, device_id_type=pl.DeviceIdType.MESH
        )
    pl.semaphore_wait(barrier, len(partners))


def gather_kernel(sel_ref, place_ref, obj_ref, probe_ref, x_ref, pall_ref, a0, a1, a2, a3, b1, b2, b3, h4, win, ybuf, xbuf, own_sem, zs, zr, ys, yr, xs, xr, ps, pr):
    here, q = lax.axis_index("scan"), lax.axis_index("mode")
    y, z, core = spot(here)
    mine = y * 2 + core
    quarter = a0.shape[2]
    half = a0.shape[0] // 2
    modes, npos = x_ref.shape[:2]
    own = pltpu.make_async_copy(obj_ref.at[:, :, pl.ds(q * quarter, quarter), :], a0, own_sem)
    own.start()
    right, left = at_spot(y, (z + 1) % RING, core), at_spot(y, (z + RING - 1) % RING, core)
    peers = plane_peers(y, z, core)
    sources = plane_sources(y, core)
    others = [(q + k) % modes for k in range(1, modes)]
    meet([(right, q), (left, q)] + [(scan, q) for _, scan, _ in peers] + [(here, m) for m in others])
    own.wait()

    sends = []

    def go(copy):
        copy.start()
        sends.append(copy)
        return copy

    def offer(buf, r, zi):
        for n, scan, d in peers:
            ybuf[n, r] = buf[sel_ref[d, zi]]
            go(send(ybuf.at[n, r], win.at[mine * RING + zi], ys.at[n, r], yr.at[n, r], scan, q))
        win[mine * RING + zi] = buf[sel_ref[mine, zi]]

    to_right = go(send(a0, a1, zs.at[0, 0], zr.at[0, 0], right, q))
    to_left = go(send(a0, b1, zs.at[1, 0], zr.at[1, 0], left, q))
    shared = []
    for k, m in enumerate(others):
        shared.append(go(send(probe_ref.at[0], pall_ref.at[q], ps.at[k], pr.at[k], here, m)))
    pall_ref[q] = probe_ref[0]
    chunks = [(0, z)]
    offer(a0, 0, z)
    for step, (a, a_next, b, b_next) in enumerate(((a1, a2, b1, b2), (a2, a3, b2, b3), (a3, h4, b3, h4)), 1):
        last = step == 3
        to_right.wait_recv()
        if last:
            a, a_next = a.at[:half], a_next.at[:half]
        to_right = go(send(a, a_next, zs.at[0, step], zr.at[0, step], right, q))
        to_left.wait_recv()
        if last:
            b, b_next = b.at[half:], b_next.at[half:]
        to_left = go(send(b, b_next, zs.at[1, step], zr.at[1, step], left, q))
        behind, ahead = (z + RING - step) % RING, (z + step) % RING
        offer((a1, a2, a3)[step - 1], 2 * step - 1, behind)
        offer((b1, b2, b3)[step - 1], 2 * step, ahead)
        chunks.extend([(2 * step - 1, behind), (2 * step, ahead)])
    to_right.wait_recv()
    to_left.wait_recv()
    opposite = (z + 4) % RING
    offer(h4, 7, opposite)
    chunks.append((7, opposite))
    for r, zi in chunks:
        for n, source in enumerate(sources):
            send(ybuf.at[n, r], win.at[source * RING + zi], ys.at[n, r], yr.at[n, r], here, q).wait_recv()

    def piece(j):
        up, left_side = residue_masks(place_ref[j, 4], place_ref[j, 5], q * quarter, win.shape[1:])
        tiles = [win[place_ref[j, k]].astype(jnp.float32) for k in range(4)]
        upper = jnp.where(left_side, tiles[0], tiles[1])
        lower = jnp.where(left_side, tiles[2], tiles[3])
        return jnp.where(up, upper, lower).astype(jnp.bfloat16)

    arrivals = []
    for k, m in enumerate(others):

        def pack(i, carry, k=k, m=m):
            xbuf[k, i] = piece(m * npos + i)
            return carry

        lax.fori_loop(0, npos, pack, 0)
        go(send(xbuf.at[k], x_ref.at[q], xs.at[k], xr.at[k], here, m))

    def keep(i, carry):
        x_ref[q, i] = piece(q * npos + i)
        return carry

    lax.fori_loop(0, npos, keep, 0)
    for k in range(modes - 1):
        source = (q + modes - 1 - k) % modes
        send(xbuf.at[k], x_ref.at[source], xs.at[k], xr.at[k], here, q).wait_recv()
        send(probe_ref.at[0], pall_ref.at[source], ps.at[k], pr.at[k], here, q).wait_recv()
    for copy in sends:
        copy.wait_send()


def gather(sel, place, tiles, probe, modes):
    tile_dev, planes, side, _ = tiles.shape
    quarter = side // modes
    npos = place.shape[0] // modes
    chunk = pltpu.VMEM((tile_dev, planes, quarter, side), tiles.dtype)
    dma = pltpu.SemaphoreType.DMA
    return pl.pallas_call(
        gather_kernel,
        in_specs=[
            pl.BlockSpec(memory_space=pltpu.SMEM),
            pl.BlockSpec(memory_space=pltpu.SMEM),
            pl.BlockSpec(memory_space=pl.ANY),
            pl.BlockSpec(memory_space=pltpu.VMEM),
        ],
        out_specs=[pl.BlockSpec(memory_space=pltpu.VMEM), pl.BlockSpec(memory_space=pltpu.VMEM)],
        out_shape=[
            jax.ShapeDtypeStruct((modes, npos, planes, quarter, side), tiles.dtype),
            jax.ShapeDtypeStruct((modes,) + probe.shape[1:], probe.dtype),
        ],
        scratch_shapes=[chunk] * 8
        + [
            pltpu.VMEM((8 * RING, planes, quarter, side), tiles.dtype),
            pltpu.VMEM((7, RING, planes, quarter, side), tiles.dtype),
            pltpu.VMEM((modes - 1, npos, planes, quarter, side), tiles.dtype),
            dma(()),
            dma((2, 4)),
            dma((2, 4)),
            dma((7, 8)),
            dma((7, 8)),
            dma((modes - 1,)),
            dma((modes - 1,)),
            dma((modes - 1,)),
            dma((modes - 1,)),
        ],
        compiler_params=pltpu.CompilerParams(
            collective_id=0, has_side_effects=True, vmem_limit_bytes=40 * MIB
        ),
        name="gather",
    )(sel, place, tiles, probe)


def swap_kernel(e_ref, pg_ref, eq_ref, pr_ref, pbuf, es, er, ps, pr):
    here, q = lax.axis_index("scan"), lax.axis_index("mode")
    modes = e_ref.shape[0]
    others = [(q + k) % modes for k in range(1, modes)]
    meet([(here, m) for m in others])
    sends = []
    for k, m in enumerate(others):
        sends.append(send(pg_ref.at[m], pbuf.at[k], ps.at[k], pr.at[k], here, m))
    for k, m in enumerate(others):
        sends.append(send(e_ref.at[m], eq_ref.at[q], es.at[k], er.at[k], here, m))
    for copy in sends:
        copy.start()
    eq_ref[q] = e_ref[q]
    for k in range(modes - 1):
        sends[k].wait_recv()
    total = pg_ref[q]
    for k in range(modes - 1):
        total = total + pbuf[k]
    pr_ref[...] = total
    for k in range(modes - 1):
        source = (q + modes - 1 - k) % modes
        send(e_ref.at[q], eq_ref.at[source], es.at[k], er.at[k], here, q).wait_recv()
    for copy in sends:
        copy.wait_send()


def swap(terms, probe_terms):
    modes = terms.shape[0]
    dma = pltpu.SemaphoreType.DMA((modes - 1,))
    vmem = pl.BlockSpec(memory_space=pltpu.VMEM)
    return pl.pallas_call(
        swap_kernel,
        in_specs=[vmem, vmem],
        out_specs=[vmem, vmem],
        out_shape=[
            jax.ShapeDtypeStruct(terms.shape, terms.dtype),
            jax.ShapeDtypeStruct(probe_terms.shape[1:], probe_terms.dtype),
        ],
        scratch_shapes=[pltpu.VMEM((modes - 1,) + probe_terms.shape[1:], probe_terms.dtype), dma, dma, dma, dma],
        compiler_params=pltpu.CompilerParams(
            collective_id=1, has_side_effects=True, vmem_limit_bytes=32 * MIB
        ),
        name="swap",
    )(terms, probe_terms)


def return_kernel(hot_ref, canvas, pr_ref, out_ref, pg_ref, rbuf, sr0, sr1, sr2, sr3, sl0, sl1, sl2, sl3, rr0, rr1, rr2, rr3, rl0, rl1, rl2, rl3, pyb, pzs, pzb, zs, zr, ys, yr, p1s, p1r, p2s, p2r, p3s, p3r, scale=1.0):
    here, q = lax.axis_index("scan"), lax.axis_index("mode")
    y, z, core = spot(here)
    mine = y * 2 + core
    half = out_ref.shape[0] // 2
    tile_dev = out_ref.shape[0]
    right, left = at_spot(y, (z + 1) % RING, core), at_spot(y, (z + RING - 1) % RING, core)
    peers = plane_peers(y, z, core)
    sources = plane_sources(y, core)
    column = [at_spot(y, (z + k) % RING, core) for k in range(1, RING)]
    meet([(scan, q) for scan in column] + [(scan, q) for _, scan, _ in peers])
    sends = []

    def go(copy):
        copy.start()
        sends.append(copy)
        return copy

    def zi(offset):
        return (z + offset + RING) % RING

    def yield_up(r, offset):
        for n, scan, d in peers:
            go(send(canvas.at[d * RING + zi(offset)], rbuf.at[mine * RING + zi(offset)], ys.at[n, r], yr.at[n, r], scan, q))

    def await_up(r, offset):
        for n, source in enumerate(sources):
            at = source * RING + zi(offset)
            send(canvas.at[at], rbuf.at[at], ys.at[n, r], yr.at[n, r], here, q).wait_recv()

    def combine(offset, tiles, into, received):
        place = zi(offset)

        def plane(l, carry):
            terms = [canvas[mine * RING + place, l]]
            terms.extend(rbuf[source * RING + place, l] for source in sources)
            for at, k in enumerate(tiles):
                total = hot_ref[(mine * RING + place) * tile_dev + k] * terms[0]
                for source, term in zip(sources, terms[1:]):
                    total = total + hot_ref[(source * RING + place) * tile_dev + k] * term
                for ref, first in received:
                    if first <= k < first + ref.shape[0]:
                        total = total + ref[k - first, l]
                into[at, l] = total
            return carry

        lax.fori_loop(0, into.shape[1], plane, 0)

    for n, scan, d in peers:
        go(send(pr_ref.at[d], pyb.at[n], p1s.at[n], p1r.at[n], scan, q))
    yield_up(0, 4)
    yield_up(1, 3)
    yield_up(2, -3)
    total = pr_ref[mine]
    for n, source in enumerate(sources):
        send(pr_ref.at[source], pyb.at[n], p1s.at[n], p1r.at[n], here, q).wait_recv()
        total = total + pyb[n]
    pzs[...] = total
    for k, scan in enumerate(column):
        go(send(pzs, pzb.at[k], p2s.at[k], p2r.at[k], scan, q))
    await_up(0, 4)
    low, high = range(half), range(half, tile_dev)
    combine(4, low, sr0, [])
    to_right = go(send(sr0, rr0, zs.at[0, 0], zr.at[0, 0], right, q))
    combine(4, high, sl0, [])
    to_left = go(send(sl0, rl0, zs.at[1, 0], zr.at[1, 0], left, q))
    yield_up(3, 2)
    yield_up(4, -2)
    for k, scan in enumerate(column):
        send(pzs, pzb.at[k], p2s.at[k], p2r.at[k], here, q).wait_recv()
        total = total + pzb[k]
    pg_ref[mine] = total * scale
    for n, scan, d in peers:
        go(send(pg_ref.at[mine], pg_ref.at[mine], p3s.at[n], p3r.at[n], scan, q))
    firsts = (0, half)
    whole = range(tile_dev)
    steps = ((3, sr1, sl1, rr0, rl0, rr1, rl1), (2, sr2, sl2, rr1, rl1, rr2, rl2), (1, sr3, sl3, rr2, rl2, rr3, rl3))
    for step, (offset, sr, sl, rr, rl, rr_next, rl_next) in enumerate(steps, 1):
        await_up(2 * step - 1, offset)
        to_right.wait_recv()
        combine(offset, whole, sr, [(rr, 0)])
        to_right = go(send(sr, rr_next, zs.at[0, step], zr.at[0, step], right, q))
        await_up(2 * step, -offset)
        to_left.wait_recv()
        combine(-offset, whole, sl, [(rl, half if step == 1 else 0)])
        to_left = go(send(sl, rl_next, zs.at[1, step], zr.at[1, step], left, q))
        if step == 1:
            yield_up(5, 1)
            yield_up(6, -1)
        elif step == 2:
            yield_up(7, 0)
    await_up(7, 0)
    to_right.wait_recv()
    to_left.wait_recv()
    combine(0, whole, out_ref, [(rr3, 0), (rl3, 0)])
    for n, source in enumerate(sources):
        send(pg_ref.at[source], pg_ref.at[source], p3s.at[n], p3r.at[n], here, q).wait_recv()
    for copy in sends:
        copy.wait_send()


def give_back(hot, canvas, probe_part, tile_dev, scale):
    tile = canvas.shape[1:]
    piece = probe_part.shape[1:]
    dma = pltpu.SemaphoreType.DMA
    vmem = pl.BlockSpec(memory_space=pltpu.VMEM)
    chunk = pltpu.VMEM((tile_dev,) + tile, canvas.dtype)
    part = pltpu.VMEM((tile_dev // 2,) + tile, canvas.dtype)
    return pl.pallas_call(
        functools.partial(return_kernel, scale=scale),
        in_specs=[pl.BlockSpec(memory_space=pltpu.SMEM), vmem, vmem],
        out_specs=[vmem, vmem],
        out_shape=[
            jax.ShapeDtypeStruct((tile_dev,) + tile, canvas.dtype),
            jax.ShapeDtypeStruct(probe_part.shape, probe_part.dtype),
        ],
        scratch_shapes=[pltpu.VMEM(canvas.shape, canvas.dtype)]
        + [part, chunk, chunk, chunk] * 4
        + [
            pltpu.VMEM((7,) + piece, probe_part.dtype),
            pltpu.VMEM(piece, probe_part.dtype),
            pltpu.VMEM((RING - 1,) + piece, probe_part.dtype),
            dma((2, 4)),
            dma((2, 4)),
            dma((7, 8)),
            dma((7, 8)),
            dma((7,)),
            dma((7,)),
            dma((RING - 1,)),
            dma((RING - 1,)),
            dma((7,)),
            dma((7,)),
        ],
        compiler_params=pltpu.CompilerParams(
            collective_id=2, has_side_effects=True, vmem_limit_bytes=48 * MIB
        ),
        name="give_back",
    )(hot, canvas, probe_part)


def shards(object_tiles, tile_owner, block_tiles, positions, counts, probe):
    scan_count = lax.axis_size("scan")
    mode_count = lax.axis_size("mode")
    here = lax.axis_index("scan")
    q = lax.axis_index("mode").reshape(1)
    tile_dev, slices, parts, side = object_tiles.shape[:4]
    batch = positions.shape[0]
    span = scan_count // 2
    quarter = side // mode_count
    planes = slices * parts
    tables = jnp.asarray(transform_tables(side))

    y, z, core = spot(here)
    first = block_tiles[:, 0]
    total = tile_owner.shape[0]
    tile_range = jnp.arange(total, dtype=jnp.int32)
    same = (tile_owner[:, None] == tile_owner[None, :]) & (tile_range[None, :] < tile_range[:, None])
    rank = jnp.sum(same.astype(jnp.int32), axis=1)
    near = lax.dynamic_index_in_dim(first.reshape(4, RING, 2), z, 1, keepdims=False).reshape(8)
    ring = at_spot(y, jnp.arange(RING, dtype=jnp.int32), core)
    listed = (tile_range[None, :] >= near[:, None]) & (tile_range[None, :] < near[:, None] + scan_count)
    owned = tile_owner[None, :] == ring[:, None]
    sel = jnp.sum(jnp.where(listed[:, None, :] & owned[None, :, :], rank[None, None, :], 0), axis=2)
    hot = (sel[:, :, None] == jnp.arange(tile_dev, dtype=jnp.int32)).astype(jnp.float32).reshape(-1)
    my_first = lax.dynamic_index_in_dim(first, here, 0, keepdims=False)
    up, left = positions[:, 0] // side, positions[:, 1] // side
    down, right = jnp.minimum(up + 1, 1), jnp.minimum(left + 1, span - 1)
    slots = jnp.stack([up * span + left, up * span + right, down * span + left, down * span + right], axis=1)
    wanted = my_first + slots
    owner_y, owner_z, owner_core = spot(tile_owner)
    homes = (owner_y * 2 + owner_core) * RING + owner_z
    found = jnp.sum(jnp.where(wanted[:, :, None] == tile_range, homes, 0), axis=2)
    place = jnp.concatenate([found, positions % side], axis=1)

    x, probe_all = gather(sel, place, object_tiles.reshape(tile_dev, planes, side, side), probe, mode_count)
    terms, probe_terms = compute(place, q, x, probe_all, counts, tables)
    back, probe_part = swap(terms, probe_terms)
    canvas = lay(place, q, back.reshape(batch, planes, quarter, side), scan_count)
    summed, probe_grad = give_back(
        hot, canvas, probe_part.reshape(8, parts * side // 8, side), tile_dev, 1.0 / (batch * scan_count)
    )
    return (summed.reshape(tile_dev, slices, parts, quarter, side), probe_grad.reshape(probe.shape))


def solution(mesh):
    placed = (
        P("scan", None, None, None, None),
        P(),
        P(),
        P("scan", None),
        P("scan", None, None),
        P("mode", None, None, None),
    )
    return jax.shard_map(
        shards,
        mesh=mesh,
        in_specs=placed,
        out_specs=(P("scan", None, None, "mode", None), P("mode", None, None, None)),
        check_vma=False,
    )
```

```python
import functools

import jax
import jax.numpy as jnp
import ml_dtypes
import numpy as np
from jax import lax
from jax.experimental import pallas as pl
from jax.experimental.pallas import tpu as pltpu
from jax.sharding import PartitionSpec as P

background = 0.25
fresnel_number = 1.0
MIB = 1024 * 1024
RING = 8
STEPS = 32767.0


def split_const(matrix):
    hi = matrix.astype(ml_dtypes.bfloat16)
    lo = (matrix - hi.astype(np.float64)).astype(ml_dtypes.bfloat16)
    return hi, lo


def transform_tables(side):
    index = np.arange(side)
    four = np.exp(-2j * np.pi * (index[:, None] * index[None, :] % side) / side) / np.sqrt(side)
    frequency = np.where(index < side // 2, index, index - side) / side
    chirp = np.exp(-1j * np.pi * fresnel_number * frequency * frequency)
    prop = (four.conj() * chirp[None, :]) @ four
    blocks = []
    for matrix in (four, prop):
        re, im = matrix.real, matrix.imag
        blocks.append(np.block([[re, im], [-im, re]]))
        blocks.append(np.block([[re, -im], [im, re]]))
    parts = []
    for block in blocks:
        parts.extend(split_const(block))
    return np.stack(parts)


def split_parts(value):
    hi = value.astype(jnp.bfloat16)
    lo = (value - hi.astype(jnp.float32)).astype(jnp.bfloat16)
    return hi, lo


def dot(a, b):
    return jnp.dot(a, b, preferred_element_type=jnp.float32)


def residue_masks(row, col, first_row, shape):
    rows = lax.broadcasted_iota(jnp.int32, shape, len(shape) - 2) + first_row
    cols = lax.broadcasted_iota(jnp.int32, shape, len(shape) - 1)
    return rows >= row, cols >= col


def spot(scan):
    return scan // (2 * RING), scan // 2 % RING, scan % 2


def at_spot(y, z, core):
    return (y * RING + z) * 2 + core


def plane_peers(y, z, core):
    peers = []
    for number in range(1, 8):
        there_y, there_core = (y + number // 2) % 4, (core + number % 2) % 2
        peers.append((number - 1, at_spot(there_y, z, there_core), there_y * 2 + there_core))
    return peers


def plane_sources(y, core):
    return [(y - number // 2 + 4) % 4 * 2 + (core + number % 2) % 2 for number in range(1, 8)]


def send(src, dst, send_sem, recv_sem, scan, mode):
    return pltpu.make_async_remote_copy(
        src_ref=src,
        dst_ref=dst,
        send_sem=send_sem,
        recv_sem=recv_sem,
        device_id={"scan": scan, "mode": mode},
        device_id_type=pl.DeviceIdType.MESH,
    )


def meet(partners):
    barrier = pltpu.get_barrier_semaphore()
    for scan, mode in partners:
        pl.semaphore_signal(
            barrier, inc=1, device_id={"scan": scan, "mode": mode}, device_id_type=pl.DeviceIdType.MESH
        )
    pl.semaphore_wait(barrier, len(partners))


def front_kernel(sel_ref, place_ref, obj_ref, probe_ref, counts_any, tab_any, eq_ref, pg_ref, a0, a1, a2, a3, b1, b2, b3, h4, win, ybuf, xbuf, x_ref, pall_ref, counts_ref, tab_ref, ebuf, a_hi, a_lo, c_hi, c_lo, planes_ref, wave_ref, sum_ref, local_sem, zs, zr, ys, yr, xs, xr, ps, pr, es, er):
    here, q = lax.axis_index("scan"), lax.axis_index("mode")
    y, z, core = spot(here)
    mine = y * 2 + core
    quarter = a0.shape[2]
    half = a0.shape[0] // 2
    modes, npos = x_ref.shape[:2]
    side = pall_ref.shape[-1]
    own = pltpu.make_async_copy(obj_ref.at[:, :, pl.ds(q * quarter, quarter), :], a0, local_sem.at[0])
    own.start()
    local = [
        pltpu.make_async_copy(tab_any, tab_ref, local_sem.at[1]),
        pltpu.make_async_copy(counts_any.at[pl.ds(q * npos, npos)], counts_ref, local_sem.at[2]),
        pltpu.make_async_copy(probe_ref.at[0], pall_ref.at[q], local_sem.at[3]),
    ]
    for copy in local:
        copy.start()
    right, left = at_spot(y, (z + 1) % RING, core), at_spot(y, (z + RING - 1) % RING, core)
    peers = plane_peers(y, z, core)
    sources = plane_sources(y, core)
    others = [(q + k) % modes for k in range(1, modes)]
    meet([(right, q), (left, q)] + [(scan, q) for _, scan, _ in peers] + [(here, m) for m in others])
    own.wait()

    sends = []

    def go(copy):
        copy.start()
        sends.append(copy)
        return copy

    def offer(buf, r, zi):
        for n, scan, d in peers:
            ybuf[n, r] = buf[sel_ref[d, zi]]
            go(send(ybuf.at[n, r], win.at[mine * RING + zi], ys.at[n, r], yr.at[n, r], scan, q))
        win[mine * RING + zi] = buf[sel_ref[mine, zi]]

    parts = (slice(0, half), slice(half, 2 * half))

    def pass_on(direction, step, part, src, dst, scan):
        rows = parts[part]
        return go(send(src.at[rows], dst.at[rows], zs.at[direction, step, part], zr.at[direction, step, part], scan, q))

    to_right = [pass_on(0, 0, part, a0, a1, right) for part in range(2)]
    to_left = [pass_on(1, 0, part, a0, b1, left) for part in (1, 0)][::-1]
    for k, m in enumerate(others):
        go(send(probe_ref.at[0], pall_ref.at[q], ps.at[k], pr.at[k], here, m))
    chunks = [(0, z)]
    offer(a0, 0, z)
    for step, (a, a_next, b, b_next) in enumerate(((a1, a2, b1, b2), (a2, a3, b2, b3), (a3, h4, b3, h4)), 1):
        last = step == 3
        next_right, next_left = [None, None], [None, None]
        for turn in range(2):
            part = turn
            to_right[part].wait_recv()
            if not last or part == 0:
                next_right[part] = pass_on(0, step, part, a, a_next, right)
            part = 1 - turn
            to_left[part].wait_recv()
            if not last or part == 1:
                next_left[part] = pass_on(1, step, part, b, b_next, left)
        to_right, to_left = next_right, next_left
        behind, ahead = (z + RING - step) % RING, (z + step) % RING
        offer(a, 2 * step - 1, behind)
        offer(b, 2 * step, ahead)
        chunks.extend([(2 * step - 1, behind), (2 * step, ahead)])
    to_right[0].wait_recv()
    to_left[1].wait_recv()
    opposite = (z + 4) % RING
    offer(h4, 7, opposite)
    chunks.append((7, opposite))
    for r, zi in chunks:
        for n, source in enumerate(sources):
            send(ybuf.at[n, r], win.at[source * RING + zi], ys.at[n, r], yr.at[n, r], here, q).wait_recv()

    def piece(j):
        up, left_side = residue_masks(place_ref[j, 4], place_ref[j, 5], q * quarter, win.shape[1:])
        tiles = [win[place_ref[j, k]].astype(jnp.float32) for k in range(4)]
        upper = jnp.where(left_side, tiles[0], tiles[1])
        lower = jnp.where(left_side, tiles[2], tiles[3])
        return jnp.where(up, upper, lower).astype(jnp.bfloat16)

    def x_copy(k, i, scan_mode, target):
        return send(xbuf.at[k, i], x_ref.at[target, i], xs.at[k, i], xr.at[k, i], here, scan_mode)

    def pack(i, carry):
        for k in (1, 0, 2):
            xbuf[k, i] = piece(others[k] * npos + i)
            x_copy(k, i, others[k], q).start()
        x_ref[q, i] = piece(q * npos + i)
        return carry

    lax.fori_loop(0, npos, pack, 0)
    for copy in local:
        copy.wait()
    froms = [(q + modes - 1 - k) % modes for k in range(modes - 1)]
    for k in range(modes - 1):
        send(probe_ref.at[0], pall_ref.at[froms[k]], ps.at[k], pr.at[k], here, q).wait_recv()

    def block(m):
        return slice(m * side, (m + 1) * side)

    def two_sided(right_table, left_table, fields):
        for m, (re, im) in enumerate(fields):
            rh, rl = split_parts(re)
            ih, il = split_parts(im)
            a_hi[block(m), 0:side] = rh
            a_hi[block(m), side : 2 * side] = ih
            a_lo[block(m), 0:side] = rl
            a_lo[block(m), side : 2 * side] = il
        for m in range(modes):
            bh, bl = tab_ref[2 * right_table], tab_ref[2 * right_table + 1]
            whole = dot(a_hi[block(m)], bh) + dot(a_lo[block(m)], bh) + dot(a_hi[block(m)], bl)
            hi, lo = split_parts(whole)
            c_hi[0:side, block(m)] = hi[:, 0:side]
            c_hi[side : 2 * side, block(m)] = hi[:, side : 2 * side]
            c_lo[0:side, block(m)] = lo[:, 0:side]
            c_lo[side : 2 * side, block(m)] = lo[:, side : 2 * side]
        lh, ll = tab_ref[2 * left_table], tab_ref[2 * left_table + 1]
        out = []
        for h in range(modes // 2):
            cols = slice(h * 2 * side, (h + 1) * 2 * side)
            whole = dot(lh, c_hi[:, cols]) + dot(lh, c_lo[:, cols]) + dot(ll, c_hi[:, cols])
            for k in range(2):
                out.append((whole[0:side, block(k)], whole[side : 2 * side, block(k)]))
        return out

    pg_ref[...] = jnp.zeros_like(pg_ref)

    def e_copy(k, p, mode, target):
        return send(ebuf.at[k, p], eq_ref.at[target, p], es.at[k, p], er.at[k, p], here, mode)

    def position(p, carry):
        for k in range(modes - 1):
            x_copy(k, p, q, froms[k]).wait_recv()
        row = place_ref[q * npos + p, 4]
        col = place_ref[q * npos + p, 5]
        for plane in range(4):
            whole = jnp.concatenate([x_ref[k, p, plane].astype(jnp.float32) for k in range(modes)], axis=0)
            whole = pltpu.roll(whole, (side - row) % side, 0)
            planes_ref[plane] = pltpu.roll(whole, (side - col) % side, 1)
        fields = []
        for m in range(modes):
            wr, wi = pall_ref[m, 0], pall_ref[m, 1]
            xr_, xi_ = planes_ref[0], planes_ref[1]
            fields.append((wr * xr_ - wi * xi_, wr * xi_ + wi * xr_))
        waves = two_sided(2, 3, fields)
        fields = []
        for m in range(modes):
            wr, wi = waves[m]
            wave_ref[m, 0] = wr
            wave_ref[m, 1] = wi
            xr_, xi_ = planes_ref[2], planes_ref[3]
            fields.append((wr * xr_ - wi * xi_, wr * xi_ + wi * xr_))
        far = two_sided(0, 1, fields)
        intensity = background
        for re, im in far:
            intensity = intensity + (re * re + im * im)
        weight = 1.0 - counts_ref[p].astype(jnp.float32) / intensity
        grads = two_sided(1, 0, [(weight * re, weight * im) for re, im in far])
        fields = []
        e_re = e_im = 0.0
        for m in range(modes):
            gr, gi = grads[m]
            wr, wi = wave_ref[m, 0], wave_ref[m, 1]
            e_re = e_re + (wr * gr + wi * gi)
            e_im = e_im + (wr * gi - wi * gr)
            xr_, xi_ = planes_ref[2], planes_ref[3]
            fields.append((xr_ * gr + xi_ * gi, xr_ * gi - xi_ * gr))
        sum_ref[2] = e_re
        sum_ref[3] = e_im
        grads = two_sided(3, 2, fields)
        e_re = e_im = 0.0
        for m in range(modes):
            gr, gi = grads[m]
            wr, wi = pall_ref[m, 0], pall_ref[m, 1]
            e_re = e_re + (wr * gr + wi * gi)
            e_im = e_im + (wr * gi - wi * gr)
            xr_, xi_ = planes_ref[0], planes_ref[1]
            pg_ref[m, 0] += xr_ * gr + xi_ * gi
            pg_ref[m, 1] += xr_ * gi - xi_ * gr
        sum_ref[0] = e_re
        sum_ref[1] = e_im
        for plane in range(4):
            sum_ref[plane] = pltpu.roll(pltpu.roll(sum_ref[plane], row, 0), col, 1)
        for k in range(modes - 1):
            rows = pl.ds(pl.multiple_of(others[k] * quarter, quarter), quarter)
            for plane in range(4):
                ebuf[k, p, plane] = sum_ref[plane, rows]
            e_copy(k, p, others[k], q).start()
        rows = pl.ds(pl.multiple_of(q * quarter, quarter), quarter)
        for plane in range(4):
            eq_ref[q, p, plane] = sum_ref[plane, rows]
        return carry

    lax.fori_loop(0, npos, position, 0)

    def finish(p, carry):
        for k in range(modes - 1):
            e_copy(k, p, q, froms[k]).wait_recv()
            e_copy(k, p, others[k], q).wait_send()
            x_copy(k, p, others[k], q).wait_send()
        return carry

    lax.fori_loop(0, npos, finish, 0)
    for copy in sends:
        copy.wait_send()


def front(sel, place, tiles, probe, counts, tables, modes):
    tile_dev, planes, side, _ = tiles.shape
    quarter = side // modes
    npos = place.shape[0] // modes
    chunk = pltpu.VMEM((tile_dev, planes, quarter, side), tiles.dtype)
    dma = pltpu.SemaphoreType.DMA
    smem, anywhere, vmem = (pl.BlockSpec(memory_space=space) for space in (pltpu.SMEM, pl.ANY, pltpu.VMEM))
    pieces = (modes - 1, npos, planes, quarter, side)
    return pl.pallas_call(
        front_kernel,
        in_specs=[smem, smem, anywhere, anywhere, anywhere, anywhere],
        out_specs=[vmem, vmem],
        out_shape=[
            jax.ShapeDtypeStruct((modes, npos, planes, quarter, side), jnp.float32),
            jax.ShapeDtypeStruct((modes,) + probe.shape[1:], jnp.float32),
        ],
        scratch_shapes=[chunk] * 8
        + [
            pltpu.VMEM((8 * RING, planes, quarter, side), tiles.dtype),
            pltpu.VMEM((7, RING, planes, quarter, side), tiles.dtype),
            pltpu.VMEM(pieces, tiles.dtype),
            pltpu.VMEM((modes,) + pieces[1:], tiles.dtype),
            pltpu.VMEM((modes,) + probe.shape[1:], probe.dtype),
            pltpu.VMEM((npos, side, side), counts.dtype),
            pltpu.VMEM(tables.shape, tables.dtype),
            pltpu.VMEM(pieces, jnp.float32),
            pltpu.VMEM((modes * side, 2 * side), jnp.bfloat16),
            pltpu.VMEM((modes * side, 2 * side), jnp.bfloat16),
            pltpu.VMEM((2 * side, modes * side), jnp.bfloat16),
            pltpu.VMEM((2 * side, modes * side), jnp.bfloat16),
            pltpu.VMEM((planes, side, side), jnp.float32),
            pltpu.VMEM((modes, 2, side, side), jnp.float32),
            pltpu.VMEM((planes, side, side), jnp.float32),
            dma((4,)),
            dma((2, 4, 2)),
            dma((2, 4, 2)),
            dma((7, 8)),
            dma((7, 8)),
            dma((modes - 1, npos)),
            dma((modes - 1, npos)),
            dma((modes - 1,)),
            dma((modes - 1,)),
            dma((modes - 1, npos)),
            dma((modes - 1, npos)),
        ],
        compiler_params=pltpu.CompilerParams(
            collective_id=0, has_side_effects=True, vmem_limit_bytes=48 * MIB
        ),
        name="front",
    )(sel, place, tiles, probe, counts, tables)


def column_scale(value):
    most = jnp.max(jnp.max(jnp.abs(value), axis=0), axis=0, keepdims=True)
    return jnp.maximum(most, 1e-30) * (1.0 / STEPS)


def encode(value, scale):
    return jnp.round(value * (1.0 / scale)).astype(jnp.int32).astype(jnp.int16)


def decode(code):
    return code.astype(jnp.int32).astype(jnp.float32)


def lay_kernel(place_ref, q_ref, e_ref, code_ref, scale_ref, canvas):
    quarter = e_ref.shape[2]
    canvas[...] = jnp.zeros_like(canvas)

    def position(j, carry):
        up, left = residue_masks(place_ref[j, 4], place_ref[j, 5], q_ref[0] * quarter, e_ref.shape[1:])
        term = e_ref[j]
        upper = jnp.where(up, term, 0.0)
        lower = jnp.where(up, 0.0, term)
        canvas[place_ref[j, 0]] += jnp.where(left, upper, 0.0)
        canvas[place_ref[j, 1]] += jnp.where(left, 0.0, upper)
        canvas[place_ref[j, 2]] += jnp.where(left, lower, 0.0)
        canvas[place_ref[j, 3]] += jnp.where(left, 0.0, lower)
        return carry

    lax.fori_loop(0, e_ref.shape[0], position, 0)

    def group(d, carry):
        for k in range(RING):
            value = canvas[d * RING + k]
            scale = column_scale(value)
            scale_ref[d, k : k + 1, :] = scale
            code_ref[d * RING + k] = encode(value, scale)
        return carry

    lax.fori_loop(0, scale_ref.shape[0], group, 0)


def lay(place, q, terms, slots):
    smem, vmem = (pl.BlockSpec(memory_space=space) for space in (pltpu.SMEM, pltpu.VMEM))
    return pl.pallas_call(
        lay_kernel,
        in_specs=[smem, smem, vmem],
        out_specs=[vmem, vmem],
        out_shape=[
            jax.ShapeDtypeStruct((slots,) + terms.shape[1:], jnp.int16),
            jax.ShapeDtypeStruct((slots // RING, RING, terms.shape[-1]), jnp.float32),
        ],
        scratch_shapes=[pltpu.VMEM((slots,) + terms.shape[1:], jnp.float32)],
        compiler_params=pltpu.CompilerParams(vmem_limit_bytes=32 * MIB),
        name="lay",
    )(place, q, terms)


def return_kernel(hot_ref, canvas, cscale, pp_ref, out_ref, pg_ref, rbuf, rscale, sr0, sr1, sr2, sr3, sl0, sl1, sl2, sl3, rr0, rr1, rr2, rr3, rl0, rl1, rl2, rl3, sscale, zscale, total_ref, pxb, pxs, pyb, pzs, pzb, zs, zr, zcs, zcr, ys, yr, ycs, ycr, p0s, p0r, p1s, p1r, p2s, p2r, p3s, p3r, scale=1.0):
    here, q = lax.axis_index("scan"), lax.axis_index("mode")
    y, z, core = spot(here)
    mine = y * 2 + core
    tile_dev, planes = out_ref.shape[:2]
    half = tile_dev // 2
    modes = pp_ref.shape[0]
    right, left = at_spot(y, (z + 1) % RING, core), at_spot(y, (z + RING - 1) % RING, core)
    peers = plane_peers(y, z, core)
    sources = plane_sources(y, core)
    column = [at_spot(y, (z + k) % RING, core) for k in range(1, RING)]
    others = [(q + k) % modes for k in range(1, modes)]
    meet([(scan, q) for scan in column] + [(scan, q) for _, scan, _ in peers] + [(here, m) for m in others])
    sends = []

    def go(copy):
        copy.start()
        sends.append(copy)
        return copy

    def zi(offset):
        return (z + offset + RING) % RING

    def yield_up(r, offset):
        for n, scan, d in peers:
            go(send(canvas.at[d * RING + zi(offset)], rbuf.at[mine * RING + zi(offset)], ys.at[n, r], yr.at[n, r], scan, q))

    def await_up(r, offset):
        for n, source in enumerate(sources):
            at = source * RING + zi(offset)
            send(canvas.at[at], rbuf.at[at], ys.at[n, r], yr.at[n, r], here, q).wait_recv()

    def combine(offset, first, count, received):
        place = zi(offset)
        steps = [cscale[mine, pl.ds(place, 1)]] + [rscale[source, pl.ds(place, 1)] for source in sources]
        givers = [mine] + sources
        weights = [
            [hot_ref[(giver * RING + place) * tile_dev + first + k] for k in range(count)] for giver in givers
        ]

        def plane(l, carry):
            terms = [decode(canvas[mine * RING + place, l]) * steps[0]]
            terms.extend(
                decode(rbuf[source * RING + place, l]) * step for source, step in zip(sources, steps[1:])
            )
            for k in range(count):
                total = weights[0][k] * terms[0]
                for weight, term in zip(weights[1:], terms[1:]):
                    total = total + weight[k] * term
                for ref, ref_scale, ref_first in received:
                    at = first + k - ref_first
                    if 0 <= at < ref.shape[0]:
                        total = total + decode(ref[at, l]) * ref_scale[at : at + 1]
                total_ref[k, l] = total
            return carry

        lax.fori_loop(0, planes, plane, 0)

    def ship(direction, step, count, buf, to, scan):
        for k in range(count):
            value = total_ref[k]
            step_size = column_scale(value)
            sscale[direction, step, k : k + 1] = step_size
            buf[k] = encode(value, step_size)
        return (
            go(send(sscale.at[direction, step], zscale.at[direction, step], zcs.at[direction, step], zcr.at[direction, step], scan, q)),
            go(send(buf, to, zs.at[direction, step], zr.at[direction, step], scan, q)),
        )

    def landed(pair):
        for copy in pair:
            copy.wait_recv()

    sscale[...] = jnp.zeros_like(sscale)
    for n, scan, d in peers:
        go(send(cscale.at[d], rscale.at[mine], ycs.at[n], ycr.at[n], scan, q))
    for k, m in enumerate(others):
        go(send(pp_ref.at[m], pxb.at[k], p0s.at[k], p0r.at[k], here, m))
    yield_up(0, 4)
    yield_up(1, 3)
    yield_up(2, -3)
    for n, source in enumerate(sources):
        send(cscale.at[source], rscale.at[source], ycs.at[n], ycr.at[n], here, q).wait_recv()
    await_up(0, 4)
    combine(4, 0, half, [])
    to_right = ship(0, 0, half, sr0, rr0, right)
    combine(4, half, half, [])
    to_left = ship(1, 0, half, sl0, rl0, left)
    yield_up(3, 2)
    yield_up(4, -2)
    total = pp_ref[q]
    for k in range(modes - 1):
        send(pp_ref.at[q], pxb.at[k], p0s.at[k], p0r.at[k], here, q).wait_recv()
        total = total + pxb[k]
    pxs[...] = total
    for n, scan, d in peers:
        go(send(pxs.at[d], pyb.at[n], p1s.at[n], p1r.at[n], scan, q))
    steps = ((3, sr1, sl1, rr0, rl0, rr1, rl1), (2, sr2, sl2, rr1, rl1, rr2, rl2), (1, sr3, sl3, rr2, rl2, rr3, rl3))
    for step, (offset, sr, sl, rr, rl, rr_next, rl_next) in enumerate(steps, 1):
        await_up(2 * step - 1, offset)
        landed(to_right)
        combine(offset, 0, tile_dev, [(rr, zscale.at[0, step - 1], 0)])
        to_right = ship(0, step, tile_dev, sr, rr_next, right)
        await_up(2 * step, -offset)
        landed(to_left)
        combine(-offset, 0, tile_dev, [(rl, zscale.at[1, step - 1], half if step == 1 else 0)])
        to_left = ship(1, step, tile_dev, sl, rl_next, left)
        if step == 1:
            yield_up(5, 1)
            yield_up(6, -1)
            total = pxs[mine]
            for n, source in enumerate(sources):
                send(pxs.at[source], pyb.at[n], p1s.at[n], p1r.at[n], here, q).wait_recv()
                total = total + pyb[n]
            pzs[...] = total
            for k, scan in enumerate(column):
                go(send(pzs, pzb.at[k], p2s.at[k], p2r.at[k], scan, q))
        elif step == 2:
            yield_up(7, 0)
            total = pzs[...]
            for k, scan in enumerate(column):
                send(pzs, pzb.at[k], p2s.at[k], p2r.at[k], here, q).wait_recv()
                total = total + pzb[k]
            pg_ref[mine] = total * scale
            for n, scan, d in peers:
                go(send(pg_ref.at[mine], pg_ref.at[mine], p3s.at[n], p3r.at[n], scan, q))
    await_up(7, 0)
    landed(to_right)
    landed(to_left)
    combine(0, 0, tile_dev, [(rr3, zscale.at[0, 3], 0), (rl3, zscale.at[1, 3], 0)])
    out_ref[...] = total_ref[...]
    for n, source in enumerate(sources):
        send(pg_ref.at[source], pg_ref.at[source], p3s.at[n], p3r.at[n], here, q).wait_recv()
    for copy in sends:
        copy.wait_send()


def give_back(hot, codes, scales, probe_terms, tile_dev, scale):
    tile = codes.shape[1:]
    modes, pieces, rows, columns = probe_terms.shape
    piece = (rows, columns)
    dma = pltpu.SemaphoreType.DMA
    smem, vmem = (pl.BlockSpec(memory_space=space) for space in (pltpu.SMEM, pltpu.VMEM))
    chunk = pltpu.VMEM((tile_dev,) + tile, codes.dtype)
    part = pltpu.VMEM((tile_dev // 2,) + tile, codes.dtype)
    ring_scale = pltpu.VMEM((2, 4, tile_dev, columns), jnp.float32)
    return pl.pallas_call(
        functools.partial(return_kernel, scale=scale),
        in_specs=[smem, vmem, vmem, vmem],
        out_specs=[vmem, vmem],
        out_shape=[
            jax.ShapeDtypeStruct((tile_dev,) + tile, jnp.float32),
            jax.ShapeDtypeStruct((pieces,) + piece, jnp.float32),
        ],
        scratch_shapes=[pltpu.VMEM(codes.shape, codes.dtype), pltpu.VMEM(scales.shape, jnp.float32)]
        + [part, chunk, chunk, chunk] * 4
        + [
            ring_scale,
            ring_scale,
            pltpu.VMEM((tile_dev,) + tile, jnp.float32),
            pltpu.VMEM((modes - 1, pieces) + piece, jnp.float32),
            pltpu.VMEM((pieces,) + piece, jnp.float32),
            pltpu.VMEM((7,) + piece, jnp.float32),
            pltpu.VMEM(piece, jnp.float32),
            pltpu.VMEM((RING - 1,) + piece, jnp.float32),
            dma((2, 4)),
            dma((2, 4)),
            dma((2, 4)),
            dma((2, 4)),
            dma((7, 8)),
            dma((7, 8)),
            dma((7,)),
            dma((7,)),
            dma((modes - 1,)),
            dma((modes - 1,)),
            dma((7,)),
            dma((7,)),
            dma((RING - 1,)),
            dma((RING - 1,)),
            dma((7,)),
            dma((7,)),
        ],
        compiler_params=pltpu.CompilerParams(
            collective_id=2, has_side_effects=True, vmem_limit_bytes=48 * MIB
        ),
        name="give_back",
    )(hot, codes, scales, probe_terms)


def shards(object_tiles, tile_owner, block_tiles, positions, counts, probe):
    scan_count = lax.axis_size("scan")
    mode_count = lax.axis_size("mode")
    here = lax.axis_index("scan")
    q = lax.axis_index("mode").reshape(1)
    tile_dev, slices, parts, side = object_tiles.shape[:4]
    batch = positions.shape[0]
    span = scan_count // 2
    quarter = side // mode_count
    planes = slices * parts
    tables = jnp.asarray(transform_tables(side))

    y, z, core = spot(here)
    first = block_tiles[:, 0]
    total = tile_owner.shape[0]
    tile_range = jnp.arange(total, dtype=jnp.int32)
    same = (tile_owner[:, None] == tile_owner[None, :]) & (tile_range[None, :] < tile_range[:, None])
    rank = jnp.sum(same.astype(jnp.int32), axis=1)
    near = lax.dynamic_index_in_dim(first.reshape(4, RING, 2), z, 1, keepdims=False).reshape(8)
    ring = at_spot(y, jnp.arange(RING, dtype=jnp.int32), core)
    listed = (tile_range[None, :] >= near[:, None]) & (tile_range[None, :] < near[:, None] + scan_count)
    owned = tile_owner[None, :] == ring[:, None]
    sel = jnp.sum(jnp.where(listed[:, None, :] & owned[None, :, :], rank[None, None, :], 0), axis=2)
    hot = (sel[:, :, None] == jnp.arange(tile_dev, dtype=jnp.int32)).astype(jnp.float32).reshape(-1)
    my_first = lax.dynamic_index_in_dim(first, here, 0, keepdims=False)
    up, left = positions[:, 0] // side, positions[:, 1] // side
    down, right = jnp.minimum(up + 1, 1), jnp.minimum(left + 1, span - 1)
    slots = jnp.stack([up * span + left, up * span + right, down * span + left, down * span + right], axis=1)
    wanted = my_first + slots
    owner_y, owner_z, owner_core = spot(tile_owner)
    homes = (owner_y * 2 + owner_core) * RING + owner_z
    found = jnp.sum(jnp.where(wanted[:, :, None] == tile_range, homes, 0), axis=2)
    place = jnp.concatenate([found, positions % side], axis=1)

    terms, probe_terms = front(
        sel, place, object_tiles.reshape(tile_dev, planes, side, side), probe, counts, tables, mode_count
    )
    codes, scales = lay(place, q, terms.reshape(batch, planes, quarter, side), scan_count)
    summed, probe_grad = give_back(
        hot, codes, scales, probe_terms.reshape(mode_count, 8, parts * side // 8, side), tile_dev, 1.0 / (batch * scan_count)
    )
    return (summed.reshape(tile_dev, slices, parts, quarter, side), probe_grad.reshape(probe.shape))


def solution(mesh):
    placed = (
        P("scan", None, None, None, None),
        P(),
        P(),
        P("scan", None),
        P("scan", None, None),
        P("mode", None, None, None),
    )
    return jax.shard_map(
        shards,
        mesh=mesh,
        in_specs=placed,
        out_specs=(P("scan", None, None, "mode", None), P("mode", None, None, None)),
        check_vma=False,
    )
```

```python
import functools

import jax
import jax.numpy as jnp
import ml_dtypes
import numpy as np
from jax import lax
from jax.experimental import pallas as pl
from jax.experimental.pallas import tpu as pltpu
from jax.sharding import PartitionSpec as P

background = 0.25
fresnel_number = 1.0
MIB = 1024 * 1024
RING = 8
STEPS = 32767.0


def split_const(matrix):
    hi = matrix.astype(ml_dtypes.bfloat16)
    lo = (matrix - hi.astype(np.float64)).astype(ml_dtypes.bfloat16)
    return hi, lo


def transform_tables(side):
    index = np.arange(side)
    four = np.exp(-2j * np.pi * (index[:, None] * index[None, :] % side) / side) / np.sqrt(side)
    frequency = np.where(index < side // 2, index, index - side) / side
    chirp = np.exp(-1j * np.pi * fresnel_number * frequency * frequency)
    prop = (four.conj() * chirp[None, :]) @ four
    blocks = []
    for matrix in (four, prop):
        re, im = matrix.real, matrix.imag
        blocks.append(np.block([[re, im], [-im, re]]))
        blocks.append(np.block([[re, -im], [im, re]]))
    parts = []
    for block in blocks:
        parts.extend(split_const(block))
    return np.stack(parts)


def split_parts(value):
    hi = value.astype(jnp.bfloat16)
    lo = (value - hi.astype(jnp.float32)).astype(jnp.bfloat16)
    return hi, lo


def dot(a, b):
    return jnp.dot(a, b, preferred_element_type=jnp.float32)


def spot(scan):
    return scan // (2 * RING), scan // 2 % RING, scan % 2


def at_spot(y, z, core):
    return (y * RING + z) * 2 + core


def plane_peers(y, z, core):
    peers = []
    for number in range(1, 8):
        there_y, there_core = (y + number // 2) % 4, (core + number % 2) % 2
        peers.append((number - 1, at_spot(there_y, z, there_core), there_y * 2 + there_core))
    return peers


def plane_sources(y, core):
    return [(y - number // 2 + 4) % 4 * 2 + (core + number % 2) % 2 for number in range(1, 8)]


def send(src, dst, send_sem, recv_sem, scan, mode):
    return pltpu.make_async_remote_copy(
        src_ref=src,
        dst_ref=dst,
        send_sem=send_sem,
        recv_sem=recv_sem,
        device_id={"scan": scan, "mode": mode},
        device_id_type=pl.DeviceIdType.MESH,
    )


def meet(partners):
    barrier = pltpu.get_barrier_semaphore()
    for scan, mode in partners:
        pl.semaphore_signal(
            barrier, inc=1, device_id={"scan": scan, "mode": mode}, device_id_type=pl.DeviceIdType.MESH
        )
    pl.semaphore_wait(barrier, len(partners))


def home(owner):
    y, z, core = owner >> 4, (owner >> 1) & (RING - 1), owner & 1
    return (y * 2 + core) * RING + z


def front_kernel(owner_ref, first_ref, pos_ref, owner_rows, obj_ref, probe_ref, counts_any, tab_any, eq_ref, pg_ref, sel_out, *scratch):
    rings, (win0, win1, ybuf, xbuf, x_ref, pall_ref, counts_ref, tab_ref, ebuf, a_hi, a_lo, b_hi, b_lo, c_hi, c_lo, planes_ref, xroll, wave_ref, sum_ref, sel_ref, local_sem, zs, zr, ys, yr, xs, xr, ps, pr, es, er) = scratch[:16], scratch[16:]
    chunk = [rings[8 * l : 8 * l + 8] for l in range(2)]
    win = (win0, win1)
    here, q = lax.axis_index("scan"), lax.axis_index("mode")
    y, z, core = spot(here)
    mine = y * 2 + core
    tile_dev, _, quarter, side = chunk[0][0].shape
    modes, npos = x_ref.shape[1:3]
    local = [
        pltpu.make_async_copy(
            obj_ref.at[:, l, :, pl.ds(q * quarter, quarter), :], chunk[l][0], local_sem.at[l]
        )
        for l in range(2)
    ]
    local.extend(
        [
            pltpu.make_async_copy(probe_ref.at[0], pall_ref.at[q], local_sem.at[2]),
            pltpu.make_async_copy(tab_any, tab_ref, local_sem.at[3]),
            pltpu.make_async_copy(counts_any.at[pl.ds(q * npos, npos)], counts_ref, local_sem.at[4]),
        ]
    )
    for copy in local:
        copy.start()
    right, left = at_spot(y, (z + 1) % RING, core), at_spot(y, (z + RING - 1) % RING, core)
    peers = plane_peers(y, z, core)
    sources = plane_sources(y, core)
    others = [(q + k) % modes for k in range(1, modes)]
    froms = [(q + modes - 1 - k) % modes for k in range(modes - 1)]
    meet([(right, q), (left, q)] + [(scan, q) for _, scan, _ in peers] + [(here, m) for m in others])

    sends = []

    def go(copy):
        copy.start()
        sends.append(copy)
        return copy

    def pass_on(l, direction, step):
        if step == 3 and direction != l:
            return None
        rightward = chunk[l][0:4] + chunk[l][7:8]
        leftward = chunk[l][0:1] + chunk[l][4:8]
        lane = (rightward, leftward)[direction]
        scan = (right, left)[direction]
        return go(send(lane[step], lane[step + 1], zs.at[l, direction, step], zr.at[l, direction, step], scan, q))

    moving = {}

    def step_on(l, step):
        for direction in (0, 1):
            if step > 0:
                moving[l, direction].wait_recv()
            moving[l, direction] = pass_on(l, direction, step)

    for l in range(2):
        local[l].wait()
        if l == 0:
            step_on(0, 0)
    for k, m in enumerate(others):
        go(send(probe_ref.at[0], pall_ref.at[q], ps.at[k], pr.at[k], here, m))

    lanes = lax.broadcasted_iota(jnp.int32, (RING, side), 1)
    ring = at_spot(y, lax.broadcasted_iota(jnp.int32, (RING, side), 0), core)
    owned = [(owner_rows[n : n + 1, :] == ring).astype(jnp.int32) for n in range(owner_rows.shape[0])]
    table = jnp.zeros((RING, side), jnp.int32)
    for d in range(8):
        first = first_ref[at_spot(d // 2, z, d % 2), 0]
        before = jnp.zeros((RING, side), jnp.int32)
        for n, hit in enumerate(owned):
            before = before + jnp.where(lanes + n * side < first, hit, 0)
        table = jnp.where(lanes == d, jnp.sum(before, axis=1, keepdims=True), table)
    sel_out[...] = table
    sel_copy = pltpu.make_async_copy(sel_out, sel_ref, local_sem.at[5])
    sel_copy.start()
    sel_copy.wait()

    rounds = [0, -1, 1, -2, 2, -3, 3, 4]

    def offer(l, r):
        zi = (z + rounds[r] + RING) % RING
        buf = chunk[l][(0, 1, 4, 2, 5, 3, 6, 7)[r]]
        for n, scan, d in peers:
            ybuf[l, n, r] = buf[sel_ref[zi, d]]
            go(send(ybuf.at[l, n, r], win[l].at[mine * RING + zi], ys.at[l, n, r], yr.at[l, n, r], scan, q))
        win[l][mine * RING + zi] = buf[sel_ref[zi, mine]]

    def await_window(l):
        for r in range(RING):
            zi = (z + rounds[r] + RING) % RING
            for n, source in enumerate(sources):
                send(ybuf.at[l, n, r], win[l].at[source * RING + zi], ys.at[l, n, r], yr.at[l, n, r], here, q).wait_recv()

    my_first = first_ref[here, 0]
    span = first_ref.shape[0] // 2
    shape = (2, quarter, side)
    rows = lax.broadcasted_iota(jnp.int32, shape, 1) + q * quarter
    cols = lax.broadcasted_iota(jnp.int32, shape, 2)

    def piece(l, j):
        row, col = pos_ref[j, 0], pos_ref[j, 1]
        near = my_first + (col >> 7)
        far = my_first + jnp.minimum((col >> 7) + 1, span - 1)
        tiles = [win[l][home(owner_ref[t])].astype(jnp.float32) for t in (near, far, near + span, far + span)]
        kept = cols >= (col & (side - 1))
        upper = jnp.where(kept, tiles[0], tiles[1])
        lower = jnp.where(kept, tiles[2], tiles[3])
        return jnp.where(rows >= row, upper, lower).astype(jnp.bfloat16)

    def x_copy(l, k, i, mode, target):
        return send(xbuf.at[l, k, i], x_ref.at[l, target, i], xs.at[l, k, i], xr.at[l, k, i], here, mode)

    def share(l):
        def pack(i, carry):
            for k in (1, 0, 2):
                xbuf[l, k, i] = piece(l, others[k] * npos + i)
                x_copy(l, k, i, others[k], q).start()
            x_ref[l, q, i] = piece(l, q * npos + i)
            return carry

        lax.fori_loop(0, npos, pack, 0)

    offer(0, 0)
    step_on(0, 1)
    step_on(1, 0)
    offer(0, 1)
    offer(0, 2)
    step_on(0, 2)
    step_on(1, 1)
    offer(0, 3)
    offer(0, 4)
    offer(1, 0)
    step_on(0, 3)
    step_on(1, 2)
    offer(0, 5)
    offer(0, 6)
    offer(1, 1)
    offer(1, 2)
    moving[0, 0].wait_recv()
    offer(0, 7)
    step_on(1, 3)
    offer(1, 3)
    offer(1, 4)
    offer(1, 5)
    offer(1, 6)
    await_window(0)
    share(0)
    moving[1, 1].wait_recv()
    offer(1, 7)
    for copy in local[2:]:
        copy.wait()
    for k in range(modes - 1):
        send(probe_ref.at[0], pall_ref.at[froms[k]], ps.at[k], pr.at[k], here, q).wait_recv()

    def block(m):
        return slice(m * side, (m + 1) * side)

    def load(hi_ref, lo_ref, fields):
        for m, (re, im) in enumerate(fields):
            rh, rl = split_parts(re)
            ih, il = split_parts(im)
            hi_ref[block(m), 0:side] = rh
            hi_ref[block(m), side : 2 * side] = ih
            lo_ref[block(m), 0:side] = rl
            lo_ref[block(m), side : 2 * side] = il

    def two_sided(right_table, left_table, hi_ref, lo_ref):
        for m in range(modes):
            bh, bl = tab_ref[2 * right_table], tab_ref[2 * right_table + 1]
            whole = dot(hi_ref[block(m)], bh) + dot(lo_ref[block(m)], bh) + dot(hi_ref[block(m)], bl)
            hi, lo = split_parts(whole)
            c_hi[0:side, block(m)] = hi[:, 0:side]
            c_hi[side : 2 * side, block(m)] = hi[:, side : 2 * side]
            c_lo[0:side, block(m)] = lo[:, 0:side]
            c_lo[side : 2 * side, block(m)] = lo[:, side : 2 * side]
        lh, ll = tab_ref[2 * left_table], tab_ref[2 * left_table + 1]
        out = []
        for h in range(modes // 2):
            cut = slice(h * 2 * side, (h + 1) * 2 * side)
            whole = dot(lh, c_hi[:, cut]) + dot(lh, c_lo[:, cut]) + dot(ll, c_hi[:, cut])
            for k in range(2):
                out.append((whole[0:side, block(k)], whole[side : 2 * side, block(k)]))
        return out

    def patch(l, p):
        for k in range(modes - 1):
            x_copy(l, k, p, q, froms[k]).wait_recv()
        row, col = pos_ref[q * npos + p, 0], pos_ref[q * npos + p, 1]
        for part in range(2):
            whole = jnp.concatenate([x_ref[l, k, p, part].astype(jnp.float32) for k in range(modes)], axis=0)
            whole = pltpu.roll(whole, (side - row) & (side - 1), 0)
            planes_ref[part] = pltpu.roll(whole, (side - (col & (side - 1))) & (side - 1), 1)

    def times(wave, field):
        (wr, wi), (fr, fi) = wave, field
        return wr * fr - wi * fi, wr * fi + wi * fr

    def conj_times(wave, field):
        (wr, wi), (fr, fi) = wave, field
        return wr * fr + wi * fi, wr * fi - wi * fr

    def e_copy(l, k, p, mode, target):
        return send(ebuf.at[l, k, p], eq_ref.at[l, target, p], es.at[l, k, p], er.at[l, k, p], here, mode)

    def hand_out(l, p, total):
        row, col = pos_ref[q * npos + p, 0], pos_ref[q * npos + p, 1]
        for part in range(2):
            sum_ref[part] = pltpu.roll(pltpu.roll(total[part], row & (side - 1), 0), col & (side - 1), 1)
        for k in range(modes - 1):
            cut = pl.ds(pl.multiple_of(others[k] * quarter, quarter), quarter)
            for part in range(2):
                ebuf[l, k, p, part] = sum_ref[part, cut]
            e_copy(l, k, p, others[k], q).start()
        cut = pl.ds(pl.multiple_of(q * quarter, quarter), quarter)
        for part in range(2):
            eq_ref[l, q, p, part] = sum_ref[part, cut]

    def enter(p, carry):
        patch(0, p)
        for part in range(2):
            xroll[p, part] = planes_ref[part]
        load(a_hi, a_lo, [times((pall_ref[m, 0], pall_ref[m, 1]), (planes_ref[0], planes_ref[1])) for m in range(modes)])
        for m, (re, im) in enumerate(two_sided(2, 3, a_hi, a_lo)):
            wave_ref[p, m, 0] = re
            wave_ref[p, m, 1] = im
        return carry

    lax.fori_loop(0, npos, enter, 0)
    await_window(1)
    share(1)

    def detect(p, carry):
        patch(1, p)
        load(a_hi, a_lo, [times((wave_ref[p, m, 0], wave_ref[p, m, 1]), (planes_ref[0], planes_ref[1])) for m in range(modes)])
        far = two_sided(0, 1, a_hi, a_lo)
        intensity = background
        for re, im in far:
            intensity = intensity + (re * re + im * im)
        weight = 1.0 - counts_ref[p].astype(jnp.float32) / intensity
        load(a_hi, a_lo, [(weight * re, weight * im) for re, im in far])
        grads = two_sided(1, 0, a_hi, a_lo)
        load(b_hi.at[p], b_lo.at[p], [conj_times((planes_ref[0], planes_ref[1]), grad) for grad in grads])
        terms = [conj_times((wave_ref[p, m, 0], wave_ref[p, m, 1]), grad) for m, grad in enumerate(grads)]
        hand_out(1, p, [functools.reduce(jnp.add, part) for part in zip(*terms)])
        return carry

    lax.fori_loop(0, npos, detect, 0)
    pg_ref[...] = jnp.zeros_like(pg_ref)

    def leave(p, carry):
        grads = two_sided(3, 2, b_hi.at[p], b_lo.at[p])
        for m, grad in enumerate(grads):
            re, im = conj_times((xroll[p, 0], xroll[p, 1]), grad)
            pg_ref[m, 0] += re
            pg_ref[m, 1] += im
        terms = [conj_times((pall_ref[m, 0], pall_ref[m, 1]), grad) for m, grad in enumerate(grads)]
        hand_out(0, p, [functools.reduce(jnp.add, part) for part in zip(*terms)])
        return carry

    lax.fori_loop(0, npos, leave, 0)

    def finish(p, carry):
        for l in (1, 0):
            for k in range(modes - 1):
                e_copy(l, k, p, q, froms[k]).wait_recv()
                e_copy(l, k, p, others[k], q).wait_send()
                x_copy(l, k, p, others[k], q).wait_send()
        return carry

    lax.fori_loop(0, npos, finish, 0)
    for copy in sends:
        copy.wait_send()


def front(tile_owner, block_tiles, positions, tiles, probe, counts, tables, modes):
    tile_dev, slices, parts, side, _ = tiles.shape
    quarter = side // modes
    npos = positions.shape[0] // modes
    dma = pltpu.SemaphoreType.DMA
    smem, anywhere, vmem = (pl.BlockSpec(memory_space=space) for space in (pltpu.SMEM, pl.ANY, pltpu.VMEM))
    tile = (parts, quarter, side)
    field = pltpu.VMEM((modes * side, 2 * side), jnp.bfloat16)
    saved = pltpu.VMEM((npos, modes * side, 2 * side), jnp.bfloat16)
    column = pltpu.VMEM((2 * side, modes * side), jnp.bfloat16)
    plane = pltpu.VMEM((parts, side, side), jnp.float32)
    return pl.pallas_call(
        front_kernel,
        in_specs=[smem, smem, smem, vmem, anywhere, anywhere, anywhere, anywhere],
        out_specs=[vmem, vmem, vmem],
        out_shape=[
            jax.ShapeDtypeStruct((slices, modes, npos) + tile, jnp.float32),
            jax.ShapeDtypeStruct((modes,) + probe.shape[1:], jnp.float32),
            jax.ShapeDtypeStruct((RING, side), jnp.int32),
        ],
        scratch_shapes=[pltpu.VMEM((tile_dev,) + tile, tiles.dtype)] * 16
        + [
            pltpu.VMEM((8 * RING,) + tile, tiles.dtype),
            pltpu.VMEM((8 * RING,) + tile, tiles.dtype),
            pltpu.VMEM((slices, 7, RING) + tile, tiles.dtype),
            pltpu.VMEM((slices, modes - 1, npos) + tile, tiles.dtype),
            pltpu.VMEM((slices, modes, npos) + tile, tiles.dtype),
            pltpu.VMEM((modes,) + probe.shape[1:], probe.dtype),
            pltpu.VMEM((npos, side, side), counts.dtype),
            pltpu.VMEM(tables.shape, tables.dtype),
            pltpu.VMEM((slices, modes - 1, npos) + tile, jnp.float32),
            field,
            field,
            saved,
            saved,
            column,
            column,
            plane,
            pltpu.VMEM((npos, parts, side, side), jnp.float32),
            pltpu.VMEM((npos, modes, parts, side, side), jnp.float32),
            plane,
            pltpu.SMEM((RING, side), jnp.int32),
            dma((6,)),
            dma((slices, 2, 4)),
            dma((slices, 2, 4)),
            dma((slices, 7, RING)),
            dma((slices, 7, RING)),
            dma((slices, modes - 1, npos)),
            dma((slices, modes - 1, npos)),
            dma((modes - 1,)),
            dma((modes - 1,)),
            dma((slices, modes - 1, npos)),
            dma((slices, modes - 1, npos)),
        ],
        compiler_params=pltpu.CompilerParams(
            collective_id=0, has_side_effects=True, vmem_limit_bytes=60 * MIB
        ),
        name="front",
    )(tile_owner, block_tiles, positions, tile_owner.reshape(-1, side), tiles, probe, counts, tables)


def column_scale(value):
    most = jnp.max(jnp.max(jnp.abs(value), axis=0), axis=0, keepdims=True)
    return jnp.maximum(most, 1e-30) * (1.0 / STEPS)


def encode(value, scale):
    return jnp.round(value * (1.0 / scale)).astype(jnp.int32).astype(jnp.int16)


def decode(code):
    return code.astype(jnp.int32).astype(jnp.float32)


def lay_kernel(owner_ref, first_ref, pos_ref, at_ref, e_ref, code_ref, scale_ref, canvas):
    slices, batch, _, quarter, side = e_ref.shape
    here, q = at_ref[0], at_ref[1]
    my_first = first_ref[here, 0]
    span = first_ref.shape[0] // 2
    canvas[...] = jnp.zeros_like(canvas)
    shape = e_ref.shape[2:]
    rows = lax.broadcasted_iota(jnp.int32, shape, 1) + q * quarter
    cols = lax.broadcasted_iota(jnp.int32, shape, 2)

    def position(j, carry):
        row, col = pos_ref[j, 0], pos_ref[j, 1]
        near = my_first + (col >> 7)
        far = my_first + jnp.minimum((col >> 7) + 1, span - 1)
        spots = [home(owner_ref[t]) for t in (near, far, near + span, far + span)]
        up = rows >= row
        kept = cols >= (col & (side - 1))
        for l in range(slices):
            term = e_ref[l, j]
            upper = jnp.where(up, term, 0.0)
            lower = jnp.where(up, 0.0, term)
            canvas[l, spots[0]] += jnp.where(kept, upper, 0.0)
            canvas[l, spots[1]] += jnp.where(kept, 0.0, upper)
            canvas[l, spots[2]] += jnp.where(kept, lower, 0.0)
            canvas[l, spots[3]] += jnp.where(kept, 0.0, lower)
        return carry

    lax.fori_loop(0, batch, position, 0)

    def group(d, carry):
        for l in range(slices):
            for k in range(RING):
                value = canvas[l, d * RING + k]
                scale = column_scale(value)
                scale_ref[l, d, k : k + 1, :] = scale
                code_ref[l, d * RING + k] = encode(value, scale)
        return carry

    lax.fori_loop(0, scale_ref.shape[1], group, 0)


def lay(tile_owner, block_tiles, positions, at, terms, slots):
    smem, vmem = (pl.BlockSpec(memory_space=space) for space in (pltpu.SMEM, pltpu.VMEM))
    slices, tile = terms.shape[0], terms.shape[2:]
    return pl.pallas_call(
        lay_kernel,
        in_specs=[smem, smem, smem, smem, vmem],
        out_specs=[vmem, vmem],
        out_shape=[
            jax.ShapeDtypeStruct((slices, slots) + tile, jnp.int16),
            jax.ShapeDtypeStruct((slices, slots // RING, RING, terms.shape[-1]), jnp.float32),
        ],
        scratch_shapes=[pltpu.VMEM((slices, slots) + tile, jnp.float32)],
        compiler_params=pltpu.CompilerParams(vmem_limit_bytes=32 * MIB),
        name="lay",
    )(tile_owner, block_tiles, positions, at, terms)


def return_kernel(sel_ref, canvas, cscale, pp_ref, out_ref, pg_ref, *scratch, scale=1.0):
    rings, (rbuf, rscale, sscale, zscale, total_ref, pxb, pxs, pyb, pzs, pzb, zs, zr, zcs, zcr, ys, yr, ycs, ycr, p0s, p0r, p1s, p1r, p2s, p2r, p3s, p3r) = scratch[:32], scratch[32:]
    out_of = [[rings[16 * l + 4 * direction : 16 * l + 4 * direction + 4] for direction in range(2)] for l in range(2)]
    into = [[rings[16 * l + 8 + 4 * direction : 16 * l + 12 + 4 * direction] for direction in range(2)] for l in range(2)]
    here, q = lax.axis_index("scan"), lax.axis_index("mode")
    y, z, core = spot(here)
    mine = y * 2 + core
    tile_dev = out_ref.shape[0]
    modes = pp_ref.shape[0]
    right, left = at_spot(y, (z + 1) % RING, core), at_spot(y, (z + RING - 1) % RING, core)
    peers = plane_peers(y, z, core)
    sources = plane_sources(y, core)
    column = [at_spot(y, (z + k) % RING, core) for k in range(1, RING)]
    others = [(q + k) % modes for k in range(1, modes)]
    meet([(scan, q) for scan in column] + [(scan, q) for _, scan, _ in peers] + [(here, m) for m in others])
    sends = []

    def go(copy):
        copy.start()
        sends.append(copy)
        return copy

    rounds = [4, 3, -3, 2, -2, 1, -1, 0]

    def zi(r):
        return (z + rounds[r] + RING) % RING

    def yield_up(l, r):
        for n, scan, d in peers:
            go(send(canvas.at[l, d * RING + zi(r)], rbuf.at[l, mine * RING + zi(r)], ys.at[l, n, r], yr.at[l, n, r], scan, q))

    def await_up(l, r):
        for n, source in enumerate(sources):
            at = source * RING + zi(r)
            send(canvas.at[l, at], rbuf.at[l, at], ys.at[l, n, r], yr.at[l, n, r], here, q).wait_recv()

    def combine(l, r, received):
        place = zi(r)
        steps = [cscale[l, mine, pl.ds(place, 1)]] + [rscale[l, source, pl.ds(place, 1)] for source in sources]
        chosen = [sel_ref[place, giver] for giver in [mine] + sources]
        weights = [[jnp.where(pick == k, 1.0, 0.0) for k in range(tile_dev)] for pick in chosen]

        def plane(part, carry):
            terms = [decode(canvas[l, mine * RING + place, part]) * steps[0]]
            terms.extend(
                decode(rbuf[l, source * RING + place, part]) * step for source, step in zip(sources, steps[1:])
            )
            for k in range(tile_dev):
                total = weights[0][k] * terms[0]
                for weight, term in zip(weights[1:], terms[1:]):
                    total = total + weight[k] * term
                for ref, ref_scale in received:
                    total = total + decode(ref[k, part]) * ref_scale[k : k + 1]
                total_ref[k, part] = total
            return carry

        lax.fori_loop(0, total_ref.shape[1], plane, 0)

    def ship(l, direction, step):
        buf, to = out_of[l][direction][step], into[l][direction][step]
        for k in range(tile_dev):
            value = total_ref[k]
            step_size = column_scale(value)
            sscale[l, direction, step, k : k + 1] = step_size
            buf[k] = encode(value, step_size)
        at = (l, direction, step)
        scan = (right, left)[direction]
        return (
            go(send(sscale.at[at], zscale.at[at], zcs.at[at], zcr.at[at], scan, q)),
            go(send(buf, to, zs.at[at], zr.at[at], scan, q)),
        )

    moving = {}

    def arrived(l, direction, step):
        if step == 0 or (l, direction) not in moving:
            return []
        for copy in moving[l, direction]:
            copy.wait_recv()
        return [(into[l][direction][step - 1], zscale.at[l, direction, step - 1])]

    def turn(l, step):
        if step == 0:
            await_up(l, 0)
            combine(l, 0, [])
            moving[l, l] = ship(l, l, 0)
            return
        for direction in (l, 1 - l):
            r = 2 * step - 1 + direction
            await_up(l, r)
            combine(l, r, arrived(l, direction, step))
            moving[l, direction] = ship(l, direction, step)

    for n, scan, d in peers:
        for l in range(2):
            go(send(cscale.at[l, d], rscale.at[l, mine], ycs.at[l, n], ycr.at[l, n], scan, q))
    for r in range(3):
        for l in range(2):
            yield_up(l, r)
    for k, m in enumerate(others):
        go(send(pp_ref.at[m], pxb.at[k], p0s.at[k], p0r.at[k], here, m))
    for n, source in enumerate(sources):
        for l in range(2):
            send(cscale.at[l, source], rscale.at[l, source], ycs.at[l, n], ycr.at[l, n], here, q).wait_recv()
    turn(0, 0)
    turn(1, 0)
    for r in (3, 4):
        for l in range(2):
            yield_up(l, r)
    total = pp_ref[q]
    for k in range(modes - 1):
        send(pp_ref.at[q], pxb.at[k], p0s.at[k], p0r.at[k], here, q).wait_recv()
        total = total + pxb[k]
    pxs[...] = total
    for n, scan, d in peers:
        go(send(pxs.at[d], pyb.at[n], p1s.at[n], p1r.at[n], scan, q))
    turn(0, 1)
    turn(1, 1)
    for r in (5, 6):
        for l in range(2):
            yield_up(l, r)
    total = pxs[mine]
    for n, source in enumerate(sources):
        send(pxs.at[source], pyb.at[n], p1s.at[n], p1r.at[n], here, q).wait_recv()
        total = total + pyb[n]
    pzs[...] = total
    for k, scan in enumerate(column):
        go(send(pzs, pzb.at[k], p2s.at[k], p2r.at[k], scan, q))
    turn(0, 2)
    turn(1, 2)
    for l in range(2):
        yield_up(l, 7)
    for k, scan in enumerate(column):
        send(pzs, pzb.at[k], p2s.at[k], p2r.at[k], here, q).wait_recv()
        total = total + pzb[k]
    pg_ref[mine] = total * scale
    for n, scan, d in peers:
        go(send(pg_ref.at[mine], pg_ref.at[mine], p3s.at[n], p3r.at[n], scan, q))
    turn(0, 3)
    turn(1, 3)
    for l in range(2):
        await_up(l, 7)
        combine(l, 7, arrived(l, 0, 4) + arrived(l, 1, 4))
        out_ref[:, l] = total_ref[...]
    for n, source in enumerate(sources):
        send(pg_ref.at[source], pg_ref.at[source], p3s.at[n], p3r.at[n], here, q).wait_recv()
    for copy in sends:
        copy.wait_send()


def give_back(sel, codes, scales, probe_terms, tile_dev, scale):
    slices, tile = codes.shape[0], codes.shape[2:]
    modes, pieces, rows, columns = probe_terms.shape
    piece = (rows, columns)
    dma = pltpu.SemaphoreType.DMA
    smem, vmem = (pl.BlockSpec(memory_space=space) for space in (pltpu.SMEM, pltpu.VMEM))
    ring_scale = pltpu.VMEM((slices, 2, 4, tile_dev, columns), jnp.float32)
    return pl.pallas_call(
        functools.partial(return_kernel, scale=scale),
        in_specs=[smem, vmem, vmem, vmem],
        out_specs=[vmem, vmem],
        out_shape=[
            jax.ShapeDtypeStruct((tile_dev, slices) + tile, jnp.float32),
            jax.ShapeDtypeStruct((pieces,) + piece, jnp.float32),
        ],
        scratch_shapes=[pltpu.VMEM((tile_dev,) + tile, codes.dtype)] * 32
        + [
            pltpu.VMEM(codes.shape, codes.dtype),
            pltpu.VMEM(scales.shape, jnp.float32),
            ring_scale,
            ring_scale,
            pltpu.VMEM((tile_dev,) + tile, jnp.float32),
            pltpu.VMEM((modes - 1, pieces) + piece, jnp.float32),
            pltpu.VMEM((pieces,) + piece, jnp.float32),
            pltpu.VMEM((7,) + piece, jnp.float32),
            pltpu.VMEM(piece, jnp.float32),
            pltpu.VMEM((RING - 1,) + piece, jnp.float32),
            dma((slices, 2, 4)),
            dma((slices, 2, 4)),
            dma((slices, 2, 4)),
            dma((slices, 2, 4)),
            dma((slices, 7, RING)),
            dma((slices, 7, RING)),
            dma((slices, 7)),
            dma((slices, 7)),
            dma((modes - 1,)),
            dma((modes - 1,)),
            dma((7,)),
            dma((7,)),
            dma((RING - 1,)),
            dma((RING - 1,)),
            dma((7,)),
            dma((7,)),
        ],
        compiler_params=pltpu.CompilerParams(
            collective_id=2, has_side_effects=True, vmem_limit_bytes=60 * MIB
        ),
        name="give_back",
    )(sel, codes, scales, probe_terms)


def shards(object_tiles, tile_owner, block_tiles, positions, counts, probe):
    scan_count = lax.axis_size("scan")
    mode_count = lax.axis_size("mode")
    at = jnp.stack([lax.axis_index("scan"), lax.axis_index("mode")])
    tile_dev, slices, parts, side = object_tiles.shape[:4]
    batch = positions.shape[0]
    quarter = side // mode_count
    tables = jnp.asarray(transform_tables(side))
    terms, probe_terms, sel = front(tile_owner, block_tiles, positions, object_tiles, probe, counts, tables, mode_count)
    terms = terms.reshape(slices, batch, parts, quarter, side)
    codes, scales = lay(tile_owner, block_tiles, positions, at, terms, scan_count)
    summed, probe_grad = give_back(
        sel, codes, scales, probe_terms.reshape(mode_count, 8, parts * side // 8, side), tile_dev, 1.0 / (batch * scan_count)
    )
    return (summed, probe_grad.reshape(probe.shape))


def solution(mesh):
    placed = (
        P("scan", None, None, None, None),
        P(),
        P(),
        P("scan", None),
        P("scan", None, None),
        P("mode", None, None, None),
    )
    return jax.shard_map(
        shards,
        mesh=mesh,
        in_specs=placed,
        out_specs=(P("scan", None, None, "mode", None), P("mode", None, None, None)),
        check_vma=False,
    )
```

```python
import functools

import jax
import jax.numpy as jnp
import ml_dtypes
import numpy as np
from jax import lax
from jax.experimental import pallas as pl
from jax.experimental.pallas import tpu as pltpu
from jax.sharding import PartitionSpec as P

background = 0.25
fresnel_number = 1.0
MIB = 1024 * 1024
RING = 8
STEPS = 32767.0


def split_const(matrix):
    hi = matrix.astype(ml_dtypes.bfloat16)
    lo = (matrix - hi.astype(np.float64)).astype(ml_dtypes.bfloat16)
    return hi, lo


def transform_tables(side):
    index = np.arange(side)
    four = np.exp(-2j * np.pi * (index[:, None] * index[None, :] % side) / side) / np.sqrt(side)
    frequency = np.where(index < side // 2, index, index - side) / side
    chirp = np.exp(-1j * np.pi * fresnel_number * frequency * frequency)
    prop = (four.conj() * chirp[None, :]) @ four
    blocks = []
    for matrix in (four, prop):
        re, im = matrix.real, matrix.imag
        blocks.append(np.block([[re, im], [-im, re]]))
        blocks.append(np.block([[re, -im], [im, re]]))
    parts = []
    for block in blocks:
        parts.extend(split_const(block))
    return np.stack(parts)


def split_parts(value):
    hi = value.astype(jnp.bfloat16)
    lo = (value - hi.astype(jnp.float32)).astype(jnp.bfloat16)
    return hi, lo


def dot(a, b):
    return jnp.dot(a, b, preferred_element_type=jnp.float32)


def spot(scan):
    return scan // (2 * RING), scan // 2 % RING, scan % 2


def at_spot(y, z, core):
    return (y * RING + z) * 2 + core


def plane_peers(y, z, core):
    peers = []
    for number in range(1, 8):
        there_y, there_core = (y + number // 2) % 4, (core + number % 2) % 2
        peers.append((number - 1, at_spot(there_y, z, there_core), there_y * 2 + there_core))
    return peers


def plane_sources(y, core):
    return [(y - number // 2 + 4) % 4 * 2 + (core + number % 2) % 2 for number in range(1, 8)]


def send(src, dst, send_sem, recv_sem, scan, mode):
    return pltpu.make_async_remote_copy(
        src_ref=src,
        dst_ref=dst,
        send_sem=send_sem,
        recv_sem=recv_sem,
        device_id={"scan": scan, "mode": mode},
        device_id_type=pl.DeviceIdType.MESH,
    )


def meet(partners):
    barrier = pltpu.get_barrier_semaphore()
    for scan, mode in partners:
        pl.semaphore_signal(
            barrier, inc=1, device_id={"scan": scan, "mode": mode}, device_id_type=pl.DeviceIdType.MESH
        )
    pl.semaphore_wait(barrier, len(partners))


def home(owner):
    y, z, core = owner >> 4, (owner >> 1) & (RING - 1), owner & 1
    return (y * 2 + core) * RING + z


def column_scale(value):
    most = jnp.max(jnp.max(jnp.abs(value), axis=0), axis=0, keepdims=True)
    return jnp.maximum(most, 1e-30) * (1.0 / STEPS)


def encode(value, scale):
    return jnp.round(value * (1.0 / scale)).astype(jnp.int32).astype(jnp.int16)


def decode(code):
    return code.astype(jnp.int32).astype(jnp.float32)


def kernel_body(owner_ref, first_ref, pos_ref, owner_rows, obj_ref, probe_ref, counts_any, tab_any, out_ref, pg_ref, *scratch, scale=1.0):
    names = iter(scratch)

    def several(count):
        return [next(names) for _ in range(count)]

    chunk = [several(8) for _ in range(2)]
    win = several(2)
    ybuf, xbuf, x_ref, pall_ref, counts_ref, tab_ref, ebuf = several(7)
    eq_ref = several(2)
    pp_ref = next(names)
    a_hi, a_lo, b_hi, b_lo, c_hi, c_lo, planes_ref, xroll, wave_ref, sum_ref = several(10)
    left_sum, right_sum = several(2), several(2)
    rbuf = [several(8) for _ in range(2)]
    rscale = several(2)
    out_of = [[several(4) for _ in range(2)] for _ in range(2)]
    into = [[several(4) for _ in range(2)] for _ in range(2)]
    codes, cscale, sscale, zscale, given, pxb, pxs, pyb, pzs, pzb, table_ref, pick_ref = several(12)
    local_sem, zs, zr, ys, yr, xs, xr, ps, pr, es, er = several(11)
    ts, tr, tcs, tcr, us, ur, ucs, ucr, p0s, p0r, p1s, p1r, p2s, p2r, p3s, p3r = several(16)

    here, q = lax.axis_index("scan"), lax.axis_index("mode")
    y, z, core = spot(here)
    mine = y * 2 + core
    tile_dev, _, quarter, side = chunk[0][0].shape
    modes, npos = x_ref.shape[1:3]
    batch = modes * npos
    local = [
        pltpu.make_async_copy(
            obj_ref.at[:, l, :, pl.ds(q * quarter, quarter), :], chunk[l][0], local_sem.at[l]
        )
        for l in range(2)
    ]
    local.extend(
        [
            pltpu.make_async_copy(probe_ref.at[0], pall_ref.at[q], local_sem.at[2]),
            pltpu.make_async_copy(tab_any, tab_ref, local_sem.at[3]),
            pltpu.make_async_copy(counts_any.at[pl.ds(q * npos, npos)], counts_ref, local_sem.at[4]),
        ]
    )
    for copy in local:
        copy.start()
    right, left = at_spot(y, (z + 1) % RING, core), at_spot(y, (z + RING - 1) % RING, core)
    peers = plane_peers(y, z, core)
    sources = plane_sources(y, core)
    column = [at_spot(y, (z + k) % RING, core) for k in range(1, RING)]
    others = [(q + k) % modes for k in range(1, modes)]
    froms = [(q + modes - 1 - k) % modes for k in range(modes - 1)]
    meet([(scan, q) for scan in column] + [(scan, q) for _, scan, _ in peers] + [(here, m) for m in others])

    sends = []

    def go(copy):
        copy.start()
        sends.append(copy)
        return copy


    def pass_on(l, direction, step):
        if step == 3 and direction != l:
            return None
        rightward = chunk[l][0:4] + chunk[l][7:8]
        leftward = chunk[l][0:1] + chunk[l][4:8]
        lane = (rightward, leftward)[direction]
        scan = (right, left)[direction]
        return go(send(lane[step], lane[step + 1], zs.at[l, direction, step], zr.at[l, direction, step], scan, q))

    moving = {}

    def step_on(l, step):
        for direction in (0, 1):
            if step > 0:
                moving[l, direction].wait_recv()
            moving[l, direction] = pass_on(l, direction, step)

    for l in range(2):
        local[l].wait()
        step_on(l, 0)
    for k, m in enumerate(others):
        go(send(probe_ref.at[0], pall_ref.at[q], ps.at[k], pr.at[k], here, m))

    lanes = lax.broadcasted_iota(jnp.int32, (RING, side), 1)
    depth = lax.broadcasted_iota(jnp.int32, (RING, side), 0)
    zero = jnp.zeros((RING, side), jnp.int32)
    owners = [owner_rows[n : n + 1, :] for n in range(owner_rows.shape[0])]
    my_first = first_ref[here, 0]
    span = first_ref.shape[0] // 2
    ring = at_spot(y, depth, core)
    owned = [jnp.where(row == ring, 1, 0) for row in owners]
    picks = []
    slots = zero
    for d in range(8):
        first = first_ref[at_spot(d // 2, z, d % 2), 0]
        before, slot = zero, zero
        ring = at_spot(d // 2, depth, d % 2)
        for n, row in enumerate(owners):
            tile = lanes + n * side
            before = before + jnp.where(tile < first, owned[n], 0)
            inside = (tile >= my_first) & (tile < my_first + 2 * span) & (row == ring)
            slot = jnp.maximum(slot, jnp.where(inside, tile - my_first, 0))
        picks.append(jnp.sum(before, axis=1, keepdims=True))
        slots = jnp.where(lanes == d, jnp.max(slot, axis=1, keepdims=True), slots)
    chosen, order, ends = zero, zero, zero
    for d in range(8):
        ahead = jnp.zeros_like(picks[d])
        for e in range(8):
            if e != d:
                ahead = ahead + jnp.where(picks[e] <= picks[d] if e < d else picks[e] < picks[d], 1, 0)
        chosen = jnp.where(lanes == d, picks[d], chosen)
        order = order + jnp.where(lanes == ahead, d, 0)
        ends = ends + jnp.where(picks[d] <= lanes, 1, 0)
    places = [pos_ref[j, 1] >> 7 for j in range(batch)]
    ranks = [jnp.int32(0)] * batch
    for j in range(batch):
        for k in range(j):
            earlier = jnp.where(places[k] <= places[j], 1, 0)
            ranks[j] = ranks[j] + earlier
            ranks[k] = ranks[k] + (1 - earlier)
    queue, counted = zero, zero
    for j in range(batch):
        queue = queue + jnp.where(lanes == ranks[j], j, 0)
        counted = counted + jnp.where(places[j] < lanes - 1, 1, 0)
    for n, table in enumerate((chosen, order, ends, slots, jnp.where(depth == 0, queue, counted))):
        table_ref[n] = table
    pick_copy = pltpu.make_async_copy(table_ref, pick_ref, local_sem.at[5])
    pick_copy.start()
    pick_copy.wait()

    rounds = [0, -1, 1, -2, 2, -3, 3, 4]

    def offer(l, r):
        zi = (z + rounds[r] + RING) % RING
        buf = chunk[l][(0, 1, 4, 2, 5, 3, 6, 7)[r]]
        for n, scan, d in peers:
            ybuf[l, n, r] = buf[pick_ref[0, zi, d]]
            go(send(ybuf.at[l, n, r], win[l].at[mine * RING + zi], ys.at[l, n, r], yr.at[l, n, r], scan, q))
        win[l][mine * RING + zi] = buf[pick_ref[0, zi, mine]]

    def await_window(l):
        for r in range(RING):
            zi = (z + rounds[r] + RING) % RING
            for n, source in enumerate(sources):
                send(ybuf.at[l, n, r], win[l].at[source * RING + zi], ys.at[l, n, r], yr.at[l, n, r], here, q).wait_recv()

    shape = (2, quarter, side)
    rows = lax.broadcasted_iota(jnp.int32, shape, 1) + q * quarter
    cols = lax.broadcasted_iota(jnp.int32, shape, 2)

    def piece(l, j):
        row, col = pos_ref[j, 0], pos_ref[j, 1]
        near = my_first + (col >> 7)
        far = my_first + jnp.minimum((col >> 7) + 1, span - 1)
        tiles = [win[l][home(owner_ref[t])].astype(jnp.float32) for t in (near, far, near + span, far + span)]
        kept = cols >= (col & (side - 1))
        upper = jnp.where(kept, tiles[0], tiles[1])
        lower = jnp.where(kept, tiles[2], tiles[3])
        return jnp.where(rows >= row, upper, lower).astype(jnp.bfloat16)

    def x_copy(l, k, i, mode, target):
        return send(xbuf.at[l, k, i], x_ref.at[l, target, i], xs.at[l, k, i], xr.at[l, k, i], here, mode)

    def share(l):
        def pack(i, carry):
            for k in (1, 0, 2):
                xbuf[l, k, i] = piece(l, others[k] * npos + i)
                x_copy(l, k, i, others[k], q).start()
            x_ref[l, q, i] = piece(l, q * npos + i)
            return carry

        lax.fori_loop(0, npos, pack, 0)

    for l in range(2):
        offer(l, 0)
    for step in range(1, 4):
        for l in range(2):
            step_on(l, step)
            offer(l, 2 * step - 1)
            offer(l, 2 * step)
    for l in range(2):
        moving[l, l].wait_recv()
        offer(l, 7)
    for l in range(2):
        await_window(l)
        share(l)
    for copy in local[2:]:
        copy.wait()
    for k in range(modes - 1):
        send(probe_ref.at[0], pall_ref.at[froms[k]], ps.at[k], pr.at[k], here, q).wait_recv()


    def block(m):
        return slice(m * side, (m + 1) * side)

    def load(hi_ref, lo_ref, fields):
        for m, (re, im) in enumerate(fields):
            rh, rl = split_parts(re)
            ih, il = split_parts(im)
            hi_ref[block(m), 0:side] = rh
            hi_ref[block(m), side : 2 * side] = ih
            lo_ref[block(m), 0:side] = rl
            lo_ref[block(m), side : 2 * side] = il

    def two_sided(right_table, left_table, hi_ref, lo_ref):
        for m in range(modes):
            bh, bl = tab_ref[2 * right_table], tab_ref[2 * right_table + 1]
            whole = dot(hi_ref[block(m)], bh) + dot(lo_ref[block(m)], bh) + dot(hi_ref[block(m)], bl)
            hi, lo = split_parts(whole)
            c_hi[0:side, block(m)] = hi[:, 0:side]
            c_hi[side : 2 * side, block(m)] = hi[:, side : 2 * side]
            c_lo[0:side, block(m)] = lo[:, 0:side]
            c_lo[side : 2 * side, block(m)] = lo[:, side : 2 * side]
        lh, ll = tab_ref[2 * left_table], tab_ref[2 * left_table + 1]
        out = []
        for h in range(modes // 2):
            cut = slice(h * 2 * side, (h + 1) * 2 * side)
            whole = dot(lh, c_hi[:, cut]) + dot(lh, c_lo[:, cut]) + dot(ll, c_hi[:, cut])
            for k in range(2):
                out.append((whole[0:side, block(k)], whole[side : 2 * side, block(k)]))
        return out

    def patch(l, p):
        for k in range(modes - 1):
            x_copy(l, k, p, q, froms[k]).wait_recv()
        row, col = pos_ref[q * npos + p, 0], pos_ref[q * npos + p, 1]
        for part in range(2):
            whole = jnp.concatenate([x_ref[l, k, p, part].astype(jnp.float32) for k in range(modes)], axis=0)
            whole = pltpu.roll(whole, (side - row) & (side - 1), 0)
            planes_ref[part] = pltpu.roll(whole, (side - (col & (side - 1))) & (side - 1), 1)

    def times(wave, field):
        (wr, wi), (fr, fi) = wave, field
        return wr * fr - wi * fi, wr * fi + wi * fr

    def conj_times(wave, field):
        (wr, wi), (fr, fi) = wave, field
        return wr * fr + wi * fi, wr * fi - wi * fr

    def e_copy(l, k, p, mode, target):
        return send(ebuf.at[l, k, p], eq_ref[l].at[target, p], es.at[l, k, p], er.at[l, k, p], here, mode)

    def hand_out(l, p, total):
        row, col = pos_ref[q * npos + p, 0], pos_ref[q * npos + p, 1]
        for part in range(2):
            sum_ref[part] = pltpu.roll(pltpu.roll(total[part], row & (side - 1), 0), col & (side - 1), 1)
        for k in range(modes - 1):
            cut = pl.ds(pl.multiple_of(others[k] * quarter, quarter), quarter)
            for part in range(2):
                ebuf[l, k, p, part] = sum_ref[part, cut]
            e_copy(l, k, p, others[k], q).start()
        cut = pl.ds(pl.multiple_of(q * quarter, quarter), quarter)
        for part in range(2):
            eq_ref[l][q, p, part] = sum_ref[part, cut]

    def enter(p, carry):
        patch(0, p)
        for part in range(2):
            xroll[p, part] = planes_ref[part]
        load(a_hi, a_lo, [times((pall_ref[m, 0], pall_ref[m, 1]), (planes_ref[0], planes_ref[1])) for m in range(modes)])
        for m, (re, im) in enumerate(two_sided(2, 3, a_hi, a_lo)):
            wave_ref[p, m, 0] = re
            wave_ref[p, m, 1] = im
        return carry

    lax.fori_loop(0, npos, enter, 0)

    def detect(p, carry):
        patch(1, p)
        load(a_hi, a_lo, [times((wave_ref[p, m, 0], wave_ref[p, m, 1]), (planes_ref[0], planes_ref[1])) for m in range(modes)])
        far = two_sided(0, 1, a_hi, a_lo)
        intensity = background
        for re, im in far:
            intensity = intensity + (re * re + im * im)
        weight = 1.0 - counts_ref[p].astype(jnp.float32) / intensity
        load(a_hi, a_lo, [(weight * re, weight * im) for re, im in far])
        grads = two_sided(1, 0, a_hi, a_lo)
        load(b_hi.at[p], b_lo.at[p], [conj_times((planes_ref[0], planes_ref[1]), grad) for grad in grads])
        terms = [conj_times((wave_ref[p, m, 0], wave_ref[p, m, 1]), grad) for m, grad in enumerate(grads)]
        hand_out(1, p, [functools.reduce(jnp.add, part) for part in zip(*terms)])
        return carry

    lax.fori_loop(0, npos, detect, 0)
    pp_ref[...] = jnp.zeros_like(pp_ref)

    def leave(p, carry):
        grads = two_sided(3, 2, b_hi.at[p], b_lo.at[p])
        for m, grad in enumerate(grads):
            for part, term in enumerate(conj_times((xroll[p, 0], xroll[p, 1]), grad)):
                pp_ref[m, part * side : (part + 1) * side] += term
        terms = [conj_times((pall_ref[m, 0], pall_ref[m, 1]), grad) for m, grad in enumerate(grads)]
        hand_out(0, p, [functools.reduce(jnp.add, part) for part in zip(*terms)])
        return carry

    lax.fori_loop(0, npos, leave, 0)


    def gather_e(l):
        def take(p, carry):
            for k in range(modes - 1):
                e_copy(l, k, p, q, froms[k]).wait_recv()
            return carry

        lax.fori_loop(0, npos, take, 0)

    def lay(l):
        blank = jnp.zeros(shape, jnp.float32)
        for u in range(2):
            left_sum[l][u, 0] = blank
            right_sum[l][u, 0] = blank

        def add(n, carry):
            j = pick_ref[4, 0, n]
            kept = cols >= (pos_ref[j, 1] & (side - 1))
            upper = rows >= pos_ref[j, 0]
            term = eq_ref[l][j // npos, j % npos]
            lefts, rights = jnp.where(kept, term, 0.0), jnp.where(kept, 0.0, term)
            for sums, part in ((left_sum[l], lefts), (right_sum[l], rights)):
                sums[0, n + 1] = sums[0, n] + jnp.where(upper, part, 0.0)
                sums[1, n + 1] = sums[1, n] + jnp.where(upper, 0.0, part)
            return carry

        lax.fori_loop(0, batch, add, 0)

    back = [4, 3, -3, 2, -2, 1, -1, 0]

    def zi(r):
        return (z + back[r] + RING) % RING

    def code(l):
        def one(place, carry):
            for d in range(8):
                slot = pick_ref[3, place, d]
                u, w = slot >> 5, slot & (span - 1)
                low, middle, high = pick_ref[4, 1, w], pick_ref[4, 1, w + 1], pick_ref[4, 1, w + 2]
                value = (left_sum[l][u, high] - left_sum[l][u, middle]) + (right_sum[l][u, middle] - right_sum[l][u, low])
                step = column_scale(value)
                cscale[l, d, pl.ds(place, 1)] = step
                codes[l, d, place] = encode(value, step)
            return carry

        lax.fori_loop(0, RING, one, 0)
        for n, scan, d in peers:
            go(send(cscale.at[l, d], rscale[l].at[mine], tcs.at[l, n], tcr.at[l, n], scan, q))
        rscale[l][mine] = cscale[l, mine]

    def yield_up(l, r):
        for n, scan, d in peers:
            go(send(codes.at[l, d, zi(r)], rbuf[l][r].at[mine], ts.at[l, n, r], tr.at[l, n, r], scan, q))
        rbuf[l][r][mine] = codes[l, mine, zi(r)]

    def await_up(l, r):
        for n, source in enumerate(sources):
            send(codes.at[l, source, zi(r)], rbuf[l][r].at[source], ts.at[l, n, r], tr.at[l, n, r], here, q).wait_recv()

    def await_scales(l):
        for n, source in enumerate(sources):
            send(cscale.at[l, source], rscale[l].at[source], tcs.at[l, n], tcr.at[l, n], here, q).wait_recv()

    given[0] = jnp.zeros(shape, jnp.float32)

    def combine(l, r, received, use):
        place = zi(r)
        total = jnp.zeros(shape, jnp.float32)
        for n in range(8):
            giver = pick_ref[1, place, n]
            total = total + decode(rbuf[l][r][giver]) * rscale[l][giver, pl.ds(place, 1)]
            given[n + 1] = total
        start = 0
        for k in range(tile_dev):
            end = pick_ref[2, place, k]
            value = given[end] - given[start]
            for ref, ref_scale in received:
                value = value + decode(ref[k]) * ref_scale[k : k + 1]
            use(k, value)
            start = end

    def ship(l, direction, step, r, received):
        at = (l, direction, step)
        buf, to = out_of[l][direction][step], into[l][direction][step]

        def pack(k, value):
            step_size = column_scale(value)
            sscale[l, direction, step, k : k + 1] = step_size
            buf[k] = encode(value, step_size)

        combine(l, r, received, pack)
        scan = (right, left)[direction]
        return (
            go(send(sscale.at[at], zscale.at[at], ucs.at[at], ucr.at[at], scan, q)),
            go(send(buf, to, us.at[at], ur.at[at], scan, q)),
        )

    flying = {}

    def arrived(l, direction, step):
        if (l, direction) not in flying:
            return []
        for copy in flying[l, direction]:
            copy.wait_recv()
        return [(into[l][direction][step - 1], zscale.at[l, direction, step - 1])]

    def turn(l, step):
        if step == 0:
            await_scales(l)
            await_up(l, 0)
            flying[l, l] = ship(l, l, 0, 0, [])
            return
        for direction in (l, 1 - l):
            r = 2 * step - 1 + direction
            await_up(l, r)
            flying[l, direction] = ship(l, direction, step, r, arrived(l, direction, step))

    gather_e(1)
    lay(1)
    code(1)
    for r in range(3):
        yield_up(1, r)
    for k, m in enumerate(others):
        go(send(pp_ref.at[m], pxb.at[k], p0s.at[k], p0r.at[k], here, m))
    gather_e(0)
    lay(0)
    code(0)
    for r in range(3):
        yield_up(0, r)
    turn(1, 0)
    yield_up(1, 3)
    yield_up(1, 4)
    turn(0, 0)
    yield_up(0, 3)
    yield_up(0, 4)
    turn(1, 1)
    yield_up(1, 5)
    yield_up(1, 6)
    turn(0, 1)
    yield_up(0, 5)
    yield_up(0, 6)
    total = pp_ref[q]
    for k in range(modes - 1):
        send(pp_ref.at[q], pxb.at[k], p0s.at[k], p0r.at[k], here, q).wait_recv()
        total = total + pxb[k]
    pxs[...] = total.reshape(pxs.shape)
    for n, scan, d in peers:
        go(send(pxs.at[d], pyb.at[n], p1s.at[n], p1r.at[n], scan, q))
    turn(1, 2)
    yield_up(1, 7)
    turn(0, 2)
    yield_up(0, 7)
    total = pxs[mine]
    for n, source in enumerate(sources):
        send(pxs.at[source], pyb.at[n], p1s.at[n], p1r.at[n], here, q).wait_recv()
        total = total + pyb[n]
    pzs[...] = total
    for k, scan in enumerate(column):
        go(send(pzs, pzb.at[k], p2s.at[k], p2r.at[k], scan, q))
    turn(1, 3)
    turn(0, 3)
    for k, scan in enumerate(column):
        send(pzs, pzb.at[k], p2s.at[k], p2r.at[k], here, q).wait_recv()
        total = total + pzb[k]
    pg_ref[mine] = total * scale
    for n, scan, d in peers:
        go(send(pg_ref.at[mine], pg_ref.at[mine], p3s.at[n], p3r.at[n], scan, q))
    for l in (1, 0):
        await_up(l, 7)

        def keep(k, value, l=l):
            out_ref[k, l] = value

        combine(l, 7, arrived(l, 0, 4) + arrived(l, 1, 4), keep)
    for n, source in enumerate(sources):
        send(pg_ref.at[source], pg_ref.at[source], p3s.at[n], p3r.at[n], here, q).wait_recv()

    def finish(p, carry):
        for l in (1, 0):
            for k in range(modes - 1):
                e_copy(l, k, p, others[k], q).wait_send()
                x_copy(l, k, p, others[k], q).wait_send()
        return carry

    lax.fori_loop(0, npos, finish, 0)
    for copy in sends:
        copy.wait_send()


def gradients(tile_owner, block_tiles, positions, tiles, probe, counts, tables, modes, scale):
    tile_dev, slices, parts, side, _ = tiles.shape
    quarter = side // modes
    batch = positions.shape[0]
    npos = batch // modes
    dma = pltpu.SemaphoreType.DMA
    smem, anywhere, vmem = (pl.BlockSpec(memory_space=space) for space in (pltpu.SMEM, pl.ANY, pltpu.VMEM))
    tile = (parts, quarter, side)

    def wide(*dims):
        return pltpu.VMEM(dims, jnp.float32)

    def half(*dims):
        return pltpu.VMEM(dims, jnp.bfloat16)

    def short(*dims):
        return pltpu.VMEM(dims, jnp.int16)

    piece = (parts * side // 8, side)
    scratch = [half(tile_dev, *tile)] * 16 + [half(8 * RING, *tile)] * 2
    scratch += [
        half(slices, 7, RING, *tile),
        half(slices, modes - 1, npos, *tile),
        half(slices, modes, npos, *tile),
        wide(modes, parts, side, side),
        pltpu.VMEM((npos, side, side), counts.dtype),
        half(*tables.shape),
        wide(slices, modes - 1, npos, *tile),
        wide(modes, npos, *tile),
        wide(modes, npos, *tile),
        wide(modes, parts * side, side),
        half(modes * side, 2 * side),
        half(modes * side, 2 * side),
        half(npos, modes * side, 2 * side),
        half(npos, modes * side, 2 * side),
        half(2 * side, modes * side),
        half(2 * side, modes * side),
        wide(parts, side, side),
        wide(npos, parts, side, side),
        wide(npos, modes, parts, side, side),
        wide(parts, side, side),
    ]
    scratch += [wide(2, batch + 1, *tile)] * 4
    scratch += [short(8, *tile)] * 16 + [wide(8, RING, side)] * 2
    scratch += [short(tile_dev, *tile)] * 32
    scratch += [
        short(slices, 8, RING, *tile),
        wide(slices, 8, RING, side),
        wide(slices, 2, 4, tile_dev, side),
        wide(slices, 2, 4, tile_dev, side),
        wide(9, *tile),
        wide(modes - 1, parts * side, side),
        wide(8, *piece),
        wide(7, *piece),
        wide(*piece),
        wide(RING - 1, *piece),
        pltpu.VMEM((5, RING, side), jnp.int32),
        pltpu.SMEM((5, RING, side), jnp.int32),
    ]
    sizes = [(6,)] + [(slices, 2, 4)] * 2 + [(slices, 7, RING)] * 2 + [(slices, modes - 1, npos)] * 2
    sizes += [(modes - 1,)] * 2 + [(slices, modes - 1, npos)] * 2
    sizes += [(slices, 7, RING)] * 2 + [(slices, 7)] * 2 + [(slices, 2, 4)] * 4
    sizes += [(modes - 1,)] * 2 + [(7,)] * 2 + [(RING - 1,)] * 2 + [(7,)] * 2
    scratch += [dma(size) for size in sizes]
    return pl.pallas_call(
        functools.partial(kernel_body, scale=scale),
        in_specs=[smem, smem, smem, vmem, anywhere, anywhere, anywhere, anywhere],
        out_specs=[vmem, vmem],
        out_shape=[
            jax.ShapeDtypeStruct((tile_dev, slices) + tile, jnp.float32),
            jax.ShapeDtypeStruct((8,) + piece, jnp.float32),
        ],
        scratch_shapes=scratch,
        compiler_params=pltpu.CompilerParams(
            collective_id=0, has_side_effects=True, vmem_limit_bytes=60 * MIB
        ),
        name="gradients",
    )(tile_owner, block_tiles, positions, tile_owner.reshape(-1, side), tiles, probe, counts, tables)


def shards(object_tiles, tile_owner, block_tiles, positions, counts, probe):
    scan_count = lax.axis_size("scan")
    mode_count = lax.axis_size("mode")
    batch = positions.shape[0]
    tables = jnp.asarray(transform_tables(object_tiles.shape[3]))
    object_grad, probe_grad = gradients(
        tile_owner, block_tiles, positions, object_tiles, probe, counts, tables, mode_count, 1.0 / (batch * scan_count)
    )
    return (object_grad, probe_grad.reshape(probe.shape))


def solution(mesh):
    placed = (
        P("scan", None, None, None, None),
        P(),
        P(),
        P("scan", None),
        P("scan", None, None),
        P("mode", None, None, None),
    )
    return jax.shard_map(
        shards,
        mesh=mesh,
        in_specs=placed,
        out_specs=(P("scan", None, None, "mode", None), P("mode", None, None, None)),
        check_vma=False,
    )
```

```python
import functools

import jax
import jax.numpy as jnp
import ml_dtypes
import numpy as np
from jax import lax
from jax.experimental import pallas as pl
from jax.experimental.pallas import tpu as pltpu
from jax.sharding import PartitionSpec as P

background = 0.25
fresnel_number = 1.0
MIB = 1024 * 1024
RING = 8
STEPS = 32767.0


def split_const(matrix):
    hi = matrix.astype(ml_dtypes.bfloat16)
    lo = (matrix - hi.astype(np.float64)).astype(ml_dtypes.bfloat16)
    return hi, lo


def transform_tables(side):
    index = np.arange(side)
    four = np.exp(-2j * np.pi * (index[:, None] * index[None, :] % side) / side) / np.sqrt(side)
    frequency = np.where(index < side // 2, index, index - side) / side
    chirp = np.exp(-1j * np.pi * fresnel_number * frequency * frequency)
    prop = (four.conj() * chirp[None, :]) @ four
    blocks = []
    for matrix in (four, prop):
        re, im = matrix.real, matrix.imag
        blocks.append(np.block([[re, im], [-im, re]]))
        blocks.append(np.block([[re, -im], [im, re]]))
    parts = []
    for block in blocks:
        parts.extend(split_const(block))
    return np.stack(parts)


def split_parts(value):
    hi = value.astype(jnp.bfloat16)
    lo = (value - hi.astype(jnp.float32)).astype(jnp.bfloat16)
    return hi, lo


def dot(a, b):
    return jnp.dot(a, b, preferred_element_type=jnp.float32)


def spot(scan):
    return scan // (2 * RING), scan // 2 % RING, scan % 2


def at_spot(y, z, core):
    return (y * RING + z) * 2 + core


def plane_peers(y, z, core):
    peers = []
    for number in range(1, 8):
        there_y, there_core = (y + number // 2) % 4, (core + number % 2) % 2
        peers.append((number - 1, at_spot(there_y, z, there_core), there_y * 2 + there_core))
    return peers


def send(src, dst, send_sem, recv_sem, scan, mode):
    return pltpu.make_async_remote_copy(
        src_ref=src,
        dst_ref=dst,
        send_sem=send_sem,
        recv_sem=recv_sem,
        device_id={"scan": scan, "mode": mode},
        device_id_type=pl.DeviceIdType.MESH,
    )


def received(ref, sem, scan, mode):
    send(ref, ref, sem, sem, scan, mode).wait_recv()


def meet(partners):
    barrier = pltpu.get_barrier_semaphore()
    for scan, mode in partners:
        pl.semaphore_signal(
            barrier, inc=1, device_id={"scan": scan, "mode": mode}, device_id_type=pl.DeviceIdType.MESH
        )
    pl.semaphore_wait(barrier, len(partners))


def home(owner):
    y, z, core = owner >> 4, (owner >> 1) & (RING - 1), owner & 1
    return (y * 2 + core) * RING + z


def column_scale(value):
    most = jnp.max(jnp.max(jnp.abs(value), axis=0), axis=0, keepdims=True)
    return jnp.maximum(most, 1e-30) * (1.0 / STEPS)


def encode(value, scale):
    return jnp.round(value * (1.0 / scale)).astype(jnp.int32).astype(jnp.int16)


def decode(code):
    return code.astype(jnp.int32).astype(jnp.float32)


def kernel_body(owner_ref, first_ref, pos_ref, owner_rows, obj_ref, probe_ref, counts_any, tab_any, out_ref, pg_ref, *scratch, scale=1.0):
    names = iter(scratch)

    def several(count):
        return [next(names) for _ in range(count)]

    chunk = [several(8) for _ in range(2)]
    win = several(2)
    ybuf, xbuf, x_ref, pall_ref, counts_ref, tab_ref, ebuf = several(7)
    eq_ref = several(2)
    pp_ref = next(names)
    a_hi, a_lo, b_hi, b_lo, c_hi, c_lo, planes_ref, xroll, wave_ref, sum_ref = several(10)
    left_sum, right_sum = several(2), several(2)
    rbuf = [several(8) for _ in range(2)]
    rscale = several(2)
    out_of = [[several(4) for _ in range(2)] for _ in range(2)]
    into = [[several(4) for _ in range(2)] for _ in range(2)]
    codes, cscale, sscale, zscale, given, pxb, pxs, pyb, pzs, pzb, table_ref, pick_ref = several(12)
    local_sem, zs, zr, ys, yr, xs, xr, ps, pr, es, er = several(11)
    ts, tr, tcs, tcr, us, ur, ucs, ucr, p0s, p0r, p1s, p1r, p2s, p2r, p3s, p3r = several(16)

    here, q = lax.axis_index("scan"), lax.axis_index("mode")
    y, z, core = spot(here)
    mine = y * 2 + core
    tile_dev, _, quarter, side = chunk[0][0].shape
    modes, npos = x_ref.shape[1:3]
    batch = modes * npos
    local = [
        pltpu.make_async_copy(
            obj_ref.at[:, l, :, pl.ds(q * quarter, quarter), :], chunk[l][0], local_sem.at[l]
        )
        for l in range(2)
    ]
    local.extend(
        [
            pltpu.make_async_copy(probe_ref.at[0], pall_ref.at[q], local_sem.at[2]),
            pltpu.make_async_copy(tab_any, tab_ref, local_sem.at[3]),
            pltpu.make_async_copy(counts_any.at[pl.ds(q * npos, npos)], counts_ref, local_sem.at[4]),
        ]
    )
    for copy in local:
        copy.start()
    right, left = at_spot(y, (z + 1) % RING, core), at_spot(y, (z + RING - 1) % RING, core)
    peers = plane_peers(y, z, core)
    column = [at_spot(y, (z + k) % RING, core) for k in range(1, RING)]
    others = [(q + k) % modes for k in range(1, modes)]
    meet([(scan, q) for scan in column] + [(scan, q) for _, scan, _ in peers] + [(here, m) for m in others])

    def go(copy):
        copy.start()
        return copy

    def arrive(ref, sem):
        received(ref, sem, here, q)


    def pass_on(l, direction, step):
        rightward = chunk[l][0:4] + chunk[l][7:8]
        leftward = chunk[l][0:1] + chunk[l][4:8]
        lane = (rightward, leftward)[direction]
        scan = (right, left)[direction]
        src, dst = lane[step], lane[step + 1]
        if step == 3:
            part = pl.ds(direction * (tile_dev // 2), tile_dev // 2)
            src, dst = src.at[part], dst.at[part]
        return go(send(src, dst, zs.at[l], zr.at[l, direction, step], scan, q))

    moving = {}

    def step_on(l, step):
        for direction in (0, 1):
            if step > 0:
                moving[l, direction].wait_recv()
            moving[l, direction] = pass_on(l, direction, step)

    for l in range(2):
        local[l].wait()
        step_on(l, 0)
    for k, m in enumerate(others):
        go(send(probe_ref.at[0], pall_ref.at[q], ps.at[0], pr.at[0], here, m))

    lanes = lax.broadcasted_iota(jnp.int32, (RING, side), 1)
    depth = lax.broadcasted_iota(jnp.int32, (RING, side), 0)
    zero = jnp.zeros((RING, side), jnp.int32)
    owners = [owner_rows[n : n + 1, :] for n in range(owner_rows.shape[0])]
    my_first = first_ref[here, 0]
    span = first_ref.shape[0] // 2
    ring = at_spot(y, depth, core)
    owned = [jnp.where(row == ring, 1, 0) for row in owners]
    picks = []
    slots = zero
    for d in range(8):
        first = first_ref[at_spot(d // 2, z, d % 2), 0]
        before, slot = zero, zero
        ring = at_spot(d // 2, depth, d % 2)
        for n, row in enumerate(owners):
            tile = lanes + n * side
            before = before + jnp.where(tile < first, owned[n], 0)
            inside = (tile >= my_first) & (tile < my_first + 2 * span) & (row == ring)
            slot = jnp.maximum(slot, jnp.where(inside, tile - my_first, 0))
        picks.append(jnp.sum(before, axis=1, keepdims=True))
        slots = jnp.where(lanes == d, jnp.max(slot, axis=1, keepdims=True), slots)
    chosen, order, ends = zero, zero, zero
    for d in range(8):
        ahead = jnp.zeros_like(picks[d])
        for e in range(8):
            if e != d:
                ahead = ahead + jnp.where(picks[e] <= picks[d] if e < d else picks[e] < picks[d], 1, 0)
        chosen = jnp.where(lanes == d, picks[d], chosen)
        order = order + jnp.where(lanes == ahead, d, 0)
        ends = ends + jnp.where(picks[d] <= lanes, 1, 0)
    places = [pos_ref[1, j] >> 7 for j in range(batch)]
    ranks = [jnp.int32(0)] * batch
    for j in range(batch):
        for k in range(j):
            earlier = jnp.where(places[k] <= places[j], 1, 0)
            ranks[j] = ranks[j] + earlier
            ranks[k] = ranks[k] + (1 - earlier)
    queue, counted = zero, zero
    for j in range(batch):
        queue = queue + jnp.where(lanes == ranks[j], j, 0)
        counted = counted + jnp.where(places[j] < lanes - 1, 1, 0)
    for n, table in enumerate((chosen, order, ends, slots, jnp.where(depth == 0, queue, counted))):
        table_ref[n] = table
    pick_copy = pltpu.make_async_copy(table_ref, pick_ref, local_sem.at[5])
    pick_copy.start()
    pick_copy.wait()

    rounds = [0, -1, 1, -2, 2, -3, 3, 4]

    def offer(l, r):
        zi = (z + rounds[r] + RING) % RING
        buf = chunk[l][(0, 1, 4, 2, 5, 3, 6, 7)[r]]
        for n, scan, d in peers:
            ybuf[l, n, r] = buf[pick_ref[0, zi, d]]
            go(send(ybuf.at[l, n, r], win[l].at[mine * RING + zi], ys.at[l], yr.at[l], scan, q))
        win[l][mine * RING + zi] = buf[pick_ref[0, zi, mine]]

    shape = (2, quarter, side)
    rows = lax.broadcasted_iota(jnp.int32, shape, 1) + q * quarter
    cols = lax.broadcasted_iota(jnp.int32, shape, 2)

    def piece(l, j):
        row, col = pos_ref[0, j], pos_ref[1, j]
        near = my_first + (col >> 7)
        far = my_first + jnp.minimum((col >> 7) + 1, span - 1)
        tiles = [win[l][home(owner_ref[t])].astype(jnp.float32) for t in (near, far, near + span, far + span)]
        kept = cols >= (col & (side - 1))
        upper = jnp.where(kept, tiles[0], tiles[1])
        lower = jnp.where(kept, tiles[2], tiles[3])
        return jnp.where(rows >= row, upper, lower).astype(jnp.bfloat16)

    def x_copy(l, k, i, mode, target):
        return send(xbuf.at[l, k, i], x_ref.at[l, target, i], xs.at[l], xr.at[l, i], here, mode)

    def share(l):
        def pack(i, carry):
            for k in (1, 0, 2):
                xbuf[l, k, i] = piece(l, others[k] * npos + i)
                x_copy(l, k, i, others[k], q).start()
            x_ref[l, q, i] = piece(l, q * npos + i)
            return carry

        lax.fori_loop(0, npos, pack, 0)

    for l in range(2):
        offer(l, 0)
    for step in range(1, 4):
        for l in range(2):
            step_on(l, step)
            offer(l, 2 * step - 1)
            offer(l, 2 * step)
    for l in range(2):
        for direction in (0, 1):
            moving[l, direction].wait_recv()
        offer(l, 7)
    for l in range(2):
        arrive(ybuf.at[l], yr.at[l])
        share(l)
    for copy in local[2:]:
        copy.wait()
    arrive(pall_ref.at[pl.ds(0, modes - 1)], pr.at[0])


    def block(m):
        return slice(m * side, (m + 1) * side)

    def load(hi_ref, lo_ref, fields):
        for m, (re, im) in enumerate(fields):
            rh, rl = split_parts(re)
            ih, il = split_parts(im)
            hi_ref[block(m), 0:side] = rh
            hi_ref[block(m), side : 2 * side] = ih
            lo_ref[block(m), 0:side] = rl
            lo_ref[block(m), side : 2 * side] = il

    def two_sided(right_table, left_table, hi_ref, lo_ref):
        for m in range(modes):
            bh, bl = tab_ref[2 * right_table], tab_ref[2 * right_table + 1]
            whole = dot(hi_ref[block(m)], bh) + dot(lo_ref[block(m)], bh) + dot(hi_ref[block(m)], bl)
            hi, lo = split_parts(whole)
            c_hi[0:side, block(m)] = hi[:, 0:side]
            c_hi[side : 2 * side, block(m)] = hi[:, side : 2 * side]
            c_lo[0:side, block(m)] = lo[:, 0:side]
            c_lo[side : 2 * side, block(m)] = lo[:, side : 2 * side]
        lh, ll = tab_ref[2 * left_table], tab_ref[2 * left_table + 1]
        out = []
        for h in range(modes // 2):
            cut = slice(h * 2 * side, (h + 1) * 2 * side)
            whole = dot(lh, c_hi[:, cut]) + dot(lh, c_lo[:, cut]) + dot(ll, c_hi[:, cut])
            for k in range(2):
                out.append((whole[0:side, block(k)], whole[side : 2 * side, block(k)]))
        return out

    def patch(l, p):
        arrive(x_ref.at[l, pl.ds(0, modes - 1), p], xr.at[l, p])
        row, col = pos_ref[0, q * npos + p], pos_ref[1, q * npos + p]
        for part in range(2):
            whole = jnp.concatenate([x_ref[l, k, p, part].astype(jnp.float32) for k in range(modes)], axis=0)
            whole = pltpu.roll(whole, (side - row) & (side - 1), 0)
            planes_ref[part] = pltpu.roll(whole, (side - (col & (side - 1))) & (side - 1), 1)

    def times(wave, field):
        (wr, wi), (fr, fi) = wave, field
        return wr * fr - wi * fi, wr * fi + wi * fr

    def conj_times(wave, field):
        (wr, wi), (fr, fi) = wave, field
        return wr * fr + wi * fi, wr * fi - wi * fr

    def e_copy(l, k, p, mode, target):
        return send(ebuf.at[l, k, p], eq_ref[l].at[target, p], es.at[l], er.at[l], here, mode)

    def hand_out(l, p, total):
        row, col = pos_ref[0, q * npos + p], pos_ref[1, q * npos + p]
        for part in range(2):
            sum_ref[part] = pltpu.roll(pltpu.roll(total[part], row & (side - 1), 0), col & (side - 1), 1)
        for k in range(modes - 1):
            cut = pl.ds(pl.multiple_of(others[k] * quarter, quarter), quarter)
            for part in range(2):
                ebuf[l, k, p, part] = sum_ref[part, cut]
            e_copy(l, k, p, others[k], q).start()
        cut = pl.ds(pl.multiple_of(q * quarter, quarter), quarter)
        for part in range(2):
            eq_ref[l][q, p, part] = sum_ref[part, cut]

    def enter(p, carry):
        patch(0, p)
        for part in range(2):
            xroll[p, part] = planes_ref[part]
        load(a_hi, a_lo, [times((pall_ref[m, 0], pall_ref[m, 1]), (planes_ref[0], planes_ref[1])) for m in range(modes)])
        for m, (re, im) in enumerate(two_sided(2, 3, a_hi, a_lo)):
            wave_ref[p, m, 0] = re
            wave_ref[p, m, 1] = im
        return carry

    lax.fori_loop(0, npos, enter, 0)

    def detect(p, carry):
        patch(1, p)
        load(a_hi, a_lo, [times((wave_ref[p, m, 0], wave_ref[p, m, 1]), (planes_ref[0], planes_ref[1])) for m in range(modes)])
        far = two_sided(0, 1, a_hi, a_lo)
        intensity = background
        for re, im in far:
            intensity = intensity + (re * re + im * im)
        weight = 1.0 - counts_ref[p].astype(jnp.float32) / intensity
        load(a_hi, a_lo, [(weight * re, weight * im) for re, im in far])
        grads = two_sided(1, 0, a_hi, a_lo)
        load(b_hi.at[p], b_lo.at[p], [conj_times((planes_ref[0], planes_ref[1]), grad) for grad in grads])
        terms = [conj_times((wave_ref[p, m, 0], wave_ref[p, m, 1]), grad) for m, grad in enumerate(grads)]
        hand_out(1, p, [functools.reduce(jnp.add, part) for part in zip(*terms)])
        return carry

    lax.fori_loop(0, npos, detect, 0)
    pp_ref[...] = jnp.zeros_like(pp_ref)

    def leave(p, carry):
        grads = two_sided(3, 2, b_hi.at[p], b_lo.at[p])
        for m, grad in enumerate(grads):
            for part, term in enumerate(conj_times((xroll[p, 0], xroll[p, 1]), grad)):
                pp_ref[m, part * side : (part + 1) * side] += term
        terms = [conj_times((pall_ref[m, 0], pall_ref[m, 1]), grad) for m, grad in enumerate(grads)]
        hand_out(0, p, [functools.reduce(jnp.add, part) for part in zip(*terms)])
        return carry

    lax.fori_loop(0, npos, leave, 0)


    def gather_e(l):
        arrive(eq_ref[l].at[pl.ds(0, modes - 1)], er.at[l])

    def lay(l):
        blank = jnp.zeros(shape, jnp.float32)
        for u in range(2):
            left_sum[l][u, 0] = blank
            right_sum[l][u, 0] = blank

        def add(n, carry):
            j = pick_ref[4, 0, n]
            kept = cols >= (pos_ref[1, j] & (side - 1))
            upper = rows >= pos_ref[0, j]
            term = eq_ref[l][j // npos, j % npos]
            lefts, rights = jnp.where(kept, term, 0.0), jnp.where(kept, 0.0, term)
            for sums, part in ((left_sum[l], lefts), (right_sum[l], rights)):
                sums[0, n + 1] = sums[0, n] + jnp.where(upper, part, 0.0)
                sums[1, n + 1] = sums[1, n] + jnp.where(upper, 0.0, part)
            return carry

        lax.fori_loop(0, batch, add, 0)

    back = [4, 3, -3, 2, -2, 1, -1, 0]

    def zi(r):
        return (z + back[r] + RING) % RING

    def code(l):
        def one(place, carry):
            for d in range(8):
                slot = pick_ref[3, place, d]
                u, w = slot >> 5, slot & (span - 1)
                low, middle, high = pick_ref[4, 1, w], pick_ref[4, 1, w + 1], pick_ref[4, 1, w + 2]
                value = (left_sum[l][u, high] - left_sum[l][u, middle]) + (right_sum[l][u, middle] - right_sum[l][u, low])
                step = column_scale(value)
                cscale[l, d, pl.ds(place, 1)] = step
                codes[l, d, place] = encode(value, step)
            return carry

        lax.fori_loop(0, RING, one, 0)
        for n, scan, d in peers:
            go(send(cscale.at[l, d], rscale[l].at[mine], tcs.at[l], tcr.at[l], scan, q))
        rscale[l][mine] = cscale[l, mine]

    def yield_up(l, r):
        for n, scan, d in peers:
            go(send(codes.at[l, d, zi(r)], rbuf[l][r].at[mine], ts.at[l], tr.at[l, r], scan, q))
        rbuf[l][r][mine] = codes[l, mine, zi(r)]

    def await_up(l, r):
        arrive(rbuf[l][r].at[pl.ds(0, 7)], tr.at[l, r])

    def await_scales(l):
        arrive(rscale[l].at[pl.ds(0, 7)], tcr.at[l])

    given[0] = jnp.zeros(shape, jnp.float32)

    def combine(l, r, received, use):
        place = zi(r)
        total = jnp.zeros(shape, jnp.float32)
        for n in range(8):
            giver = pick_ref[1, place, n]
            total = total + decode(rbuf[l][r][giver]) * rscale[l][giver, pl.ds(place, 1)]
            given[n + 1] = total
        start = 0
        for k in range(tile_dev):
            end = pick_ref[2, place, k]
            value = given[end] - given[start]
            for ref, ref_scale in received:
                value = value + decode(ref[k]) * ref_scale[k : k + 1]
            use(k, value)
            start = end

    def ship(l, direction, step, r, received):
        at = (l, direction, step)
        buf, to = out_of[l][direction][step], into[l][direction][step]

        def pack(k, value):
            step_size = column_scale(value)
            sscale[l, direction, step, k : k + 1] = step_size
            buf[k] = encode(value, step_size)

        combine(l, r, received, pack)
        scan = (right, left)[direction]
        return (
            go(send(sscale.at[at], zscale.at[at], ucs.at[l], ucr.at[at], scan, q)),
            go(send(buf, to, us.at[l], ur.at[at], scan, q)),
        )

    flying = {}

    def arrived(l, direction, step):
        if (l, direction) not in flying:
            return []
        for copy in flying[l, direction]:
            copy.wait_recv()
        return [(into[l][direction][step - 1], zscale.at[l, direction, step - 1])]

    def turn(l, step):
        if step == 0:
            await_scales(l)
            await_up(l, 0)
            flying[l, l] = ship(l, l, 0, 0, [])
            return
        for direction in (l, 1 - l):
            r = 2 * step - 1 + direction
            await_up(l, r)
            flying[l, direction] = ship(l, direction, step, r, arrived(l, direction, step))

    gather_e(1)
    lay(1)
    code(1)
    for r in range(3):
        yield_up(1, r)
    for k, m in enumerate(others):
        go(send(pp_ref.at[m], pxb.at[k], p0s.at[0], p0r.at[0], here, m))
    gather_e(0)
    lay(0)
    code(0)
    for r in range(3):
        yield_up(0, r)
    turn(1, 0)
    yield_up(1, 3)
    yield_up(1, 4)
    turn(0, 0)
    yield_up(0, 3)
    yield_up(0, 4)
    turn(1, 1)
    yield_up(1, 5)
    yield_up(1, 6)
    turn(0, 1)
    yield_up(0, 5)
    yield_up(0, 6)
    total = pp_ref[q]
    arrive(pxb, p0r.at[0])
    for k in range(modes - 1):
        total = total + pxb[k]
    pxs[...] = total.reshape(pxs.shape)
    for n, scan, d in peers:
        go(send(pxs.at[d], pyb.at[n], p1s.at[0], p1r.at[0], scan, q))
    turn(1, 2)
    yield_up(1, 7)
    turn(0, 2)
    yield_up(0, 7)
    total = pxs[mine]
    arrive(pyb, p1r.at[0])
    for n in range(7):
        total = total + pyb[n]
    pzs[...] = total
    for k, scan in enumerate(column):
        go(send(pzs, pzb.at[k], p2s.at[0], p2r.at[0], scan, q))
    turn(1, 3)
    turn(0, 3)
    arrive(pzb, p2r.at[0])
    for k in range(RING - 1):
        total = total + pzb[k]
    pg_ref[mine] = total * scale
    for n, scan, d in peers:
        go(send(pg_ref.at[mine], pg_ref.at[mine], p3s.at[0], p3r.at[0], scan, q))
    for l in (1, 0):
        await_up(l, 7)

        def keep(k, value, l=l):
            out_ref[k, l] = value

        combine(l, 7, arrived(l, 0, 4) + arrived(l, 1, 4), keep)
    arrive(pg_ref.at[pl.ds(0, 7)], p3r.at[0])

    def departed(ref, sem):
        send(ref, ref, sem, sem, here, q).wait_send()

    for l in range(2):
        departed(ybuf.at[l], zs.at[l])
        departed(ybuf.at[l], ys.at[l])
        departed(xbuf.at[l], xs.at[l])
        departed(ebuf.at[l], es.at[l])
        departed(codes.at[l, pl.ds(0, 7)], ts.at[l])
        departed(cscale.at[l, pl.ds(0, 7)], tcs.at[l])
        departed(codes.at[l, pl.ds(0, 7)], us.at[l])
        departed(cscale.at[l, pl.ds(0, 7)], ucs.at[l])
    departed(pall_ref.at[pl.ds(0, modes - 1)], ps.at[0])
    departed(pxb, p0s.at[0])
    departed(pyb, p1s.at[0])
    departed(pzb, p2s.at[0])
    departed(pg_ref.at[pl.ds(0, 7)], p3s.at[0])


def gradients(tile_owner, block_tiles, positions, tiles, probe, counts, tables, modes, scale):
    tile_dev, slices, parts, side, _ = tiles.shape
    quarter = side // modes
    batch = positions.shape[0]
    npos = batch // modes
    dma = pltpu.SemaphoreType.DMA
    smem, anywhere, vmem = (pl.BlockSpec(memory_space=space) for space in (pltpu.SMEM, pl.ANY, pltpu.VMEM))
    tile = (parts, quarter, side)

    def wide(*dims):
        return pltpu.VMEM(dims, jnp.float32)

    def half(*dims):
        return pltpu.VMEM(dims, jnp.bfloat16)

    def short(*dims):
        return pltpu.VMEM(dims, jnp.int16)

    piece = (parts * side // 8, side)
    scratch = [half(tile_dev, *tile)] * 16 + [half(8 * RING, *tile)] * 2
    scratch += [
        half(slices, 7, RING, *tile),
        half(slices, modes - 1, npos, *tile),
        half(slices, modes, npos, *tile),
        wide(modes, parts, side, side),
        pltpu.VMEM((npos, side, side), counts.dtype),
        half(*tables.shape),
        wide(slices, modes - 1, npos, *tile),
        wide(modes, npos, *tile),
        wide(modes, npos, *tile),
        wide(modes, parts * side, side),
        half(modes * side, 2 * side),
        half(modes * side, 2 * side),
        half(npos, modes * side, 2 * side),
        half(npos, modes * side, 2 * side),
        half(2 * side, modes * side),
        half(2 * side, modes * side),
        wide(parts, side, side),
        wide(npos, parts, side, side),
        wide(npos, modes, parts, side, side),
        wide(parts, side, side),
    ]
    scratch += [wide(2, batch + 1, *tile)] * 4
    scratch += [short(8, *tile)] * 16 + [wide(8, RING, side)] * 2
    scratch += [short(tile_dev, *tile)] * 32
    scratch += [
        short(slices, 8, RING, *tile),
        wide(slices, 8, RING, side),
        wide(slices, 2, 4, tile_dev, side),
        wide(slices, 2, 4, tile_dev, side),
        wide(9, *tile),
        wide(modes - 1, parts * side, side),
        wide(8, *piece),
        wide(7, *piece),
        wide(*piece),
        wide(RING - 1, *piece),
        pltpu.VMEM((5, RING, side), jnp.int32),
        pltpu.SMEM((5, RING, side), jnp.int32),
    ]
    sizes = [(6,), (slices,), (slices, 2, 4), (slices,), (slices,), (slices,), (slices, npos)]
    sizes += [(1,), (1,), (slices,), (slices,)]
    sizes += [(slices,), (slices, RING), (slices,), (slices,), (slices,), (slices, 2, 4), (slices,), (slices, 2, 4)]
    sizes += [(1,)] * 8
    scratch += [dma(size) for size in sizes]
    return pl.pallas_call(
        functools.partial(kernel_body, scale=scale),
        in_specs=[smem, smem, smem, vmem, anywhere, anywhere, anywhere, anywhere],
        out_specs=[vmem, vmem],
        out_shape=[
            jax.ShapeDtypeStruct((tile_dev, slices) + tile, jnp.float32),
            jax.ShapeDtypeStruct((8,) + piece, jnp.float32),
        ],
        scratch_shapes=scratch,
        compiler_params=pltpu.CompilerParams(
            collective_id=0, has_side_effects=True, vmem_limit_bytes=60 * MIB
        ),
        name="gradients",
    )(tile_owner, block_tiles, positions.T, tile_owner.reshape(-1, side), tiles, probe, counts, tables)


def shards(object_tiles, tile_owner, block_tiles, positions, counts, probe):
    scan_count = lax.axis_size("scan")
    mode_count = lax.axis_size("mode")
    batch = positions.shape[0]
    tables = jnp.asarray(transform_tables(object_tiles.shape[3]))
    object_grad, probe_grad = gradients(
        tile_owner, block_tiles, positions, object_tiles, probe, counts, tables, mode_count, 1.0 / (batch * scan_count)
    )
    return (object_grad, probe_grad.reshape(probe.shape))


def solution(mesh):
    placed = (
        P("scan", None, None, None, None),
        P(),
        P(),
        P("scan", None),
        P("scan", None, None),
        P("mode", None, None, None),
    )
    return jax.shard_map(
        shards,
        mesh=mesh,
        in_specs=placed,
        out_specs=(P("scan", None, None, "mode", None), P("mode", None, None, None)),
        check_vma=False,
    )
```

```python
import functools

import jax
import jax.numpy as jnp
import ml_dtypes
import numpy as np
from jax import lax
from jax.experimental import pallas as pl
from jax.experimental.pallas import tpu as pltpu
from jax.sharding import PartitionSpec as P

background = 0.25
fresnel_number = 1.0
MIB = 1024 * 1024
RING = 8
STEPS = 32767.0


def split_const(matrix):
    hi = matrix.astype(ml_dtypes.bfloat16)
    lo = (matrix - hi.astype(np.float64)).astype(ml_dtypes.bfloat16)
    return hi, lo


def transform_tables(side):
    index = np.arange(side)
    four = np.exp(-2j * np.pi * (index[:, None] * index[None, :] % side) / side) / np.sqrt(side)
    frequency = np.where(index < side // 2, index, index - side) / side
    chirp = np.exp(-1j * np.pi * fresnel_number * frequency * frequency)
    prop = (four.conj() * chirp[None, :]) @ four
    blocks = []
    for matrix in (four, prop):
        re, im = matrix.real, matrix.imag
        blocks.append(np.block([[re, im], [-im, re]]))
        blocks.append(np.block([[re, -im], [im, re]]))
    parts = []
    for block in blocks:
        parts.extend(split_const(block))
    return np.stack(parts)


def split_parts(value):
    hi = value.astype(jnp.bfloat16)
    lo = (value - hi.astype(jnp.float32)).astype(jnp.bfloat16)
    return hi, lo


def dot(a, b):
    return jnp.dot(a, b, preferred_element_type=jnp.float32)


def spot(scan):
    return scan // (2 * RING), scan // 2 % RING, scan % 2


def at_spot(y, z, core):
    return (y * RING + z) * 2 + core


def plane_peers(y, z, core):
    peers = []
    for number in range(1, 8):
        there_y, there_core = (y + number // 2) % 4, (core + number % 2) % 2
        peers.append((number - 1, at_spot(there_y, z, there_core), there_y * 2 + there_core))
    return peers


def send(src, dst, send_sem, recv_sem, scan, mode):
    return pltpu.make_async_remote_copy(
        src_ref=src,
        dst_ref=dst,
        send_sem=send_sem,
        recv_sem=recv_sem,
        device_id={"scan": scan, "mode": mode},
        device_id_type=pl.DeviceIdType.MESH,
    )


def received(ref, sem, scan, mode):
    send(ref, ref, sem, sem, scan, mode).wait_recv()


def meet(partners):
    barrier = pltpu.get_barrier_semaphore()
    for scan, mode in partners:
        pl.semaphore_signal(
            barrier, inc=1, device_id={"scan": scan, "mode": mode}, device_id_type=pl.DeviceIdType.MESH
        )
    pl.semaphore_wait(barrier, len(partners))


def home(owner):
    y, z, core = owner >> 4, (owner >> 1) & (RING - 1), owner & 1
    return (y * 2 + core) * RING + z


def column_scale(value):
    most = jnp.max(jnp.max(jnp.abs(value), axis=0), axis=0, keepdims=True)
    return jnp.maximum(most, 1e-30) * (1.0 / STEPS)


def encode(value, scale):
    return jnp.round(value * (1.0 / scale)).astype(jnp.int32).astype(jnp.int16)


def decode(code):
    return code.astype(jnp.int32).astype(jnp.float32)


def kernel_body(owner_ref, first_ref, pos_ref, owner_rows, obj_ref, probe_ref, counts_any, tab_any, out_ref, pg_ref, *scratch, scale=1.0):
    names = iter(scratch)

    def several(count):
        return [next(names) for _ in range(count)]

    chunk = [several(8) for _ in range(2)]
    win = several(2)
    ybuf, xbuf, x_ref, pall_ref, counts_ref, tab_ref, ebuf = several(7)
    eq_ref, e_steps = several(2), several(2)
    e_out, pp_ref = several(2)
    a_hi, a_lo, b_hi, b_lo, c_hi, c_lo, planes_ref, xroll, wave_ref, sum_ref = several(10)
    left_sum, right_sum = several(2), several(2)
    rbuf = [several(8) for _ in range(2)]
    rscale = several(2)
    out_of = [[several(4) for _ in range(2)] for _ in range(2)]
    into = [[several(4) for _ in range(2)] for _ in range(2)]
    codes, cscale, sscale, zscale, given, pxb, pxs, pyb, pzs, pzb, table_ref, pick_ref = several(12)
    local_sem, zs, zr, ys, yr, xs, xr, ps, pr, es, er, ess, esr = several(13)
    ts, tr, tcs, tcr, us, ur, ucs, ucr, p0s, p0r, p1s, p1r, p2s, p2r, p3s, p3r = several(16)

    here, q = lax.axis_index("scan"), lax.axis_index("mode")
    y, z, core = spot(here)
    mine = y * 2 + core
    tile_dev, _, quarter, side = chunk[0][0].shape
    modes, npos = x_ref.shape[1:3]
    batch = modes * npos
    local = [
        pltpu.make_async_copy(
            obj_ref.at[:, l, :, pl.ds(q * quarter, quarter), :], chunk[l][0], local_sem.at[l]
        )
        for l in range(2)
    ]
    local.extend(
        [
            pltpu.make_async_copy(probe_ref.at[0], pall_ref.at[q], local_sem.at[2]),
            pltpu.make_async_copy(tab_any, tab_ref, local_sem.at[3]),
            pltpu.make_async_copy(counts_any.at[pl.ds(q * npos, npos)], counts_ref, local_sem.at[4]),
        ]
    )
    for copy in local:
        copy.start()
    right, left = at_spot(y, (z + 1) % RING, core), at_spot(y, (z + RING - 1) % RING, core)
    peers = plane_peers(y, z, core)
    column = [at_spot(y, (z + k) % RING, core) for k in range(1, RING)]
    others = [(q + k) % modes for k in range(1, modes)]
    meet([(scan, q) for scan in column] + [(scan, q) for _, scan, _ in peers] + [(here, m) for m in others])

    def go(copy):
        copy.start()
        return copy

    def arrive(ref, sem):
        received(ref, sem, here, q)


    def pass_on(l, direction, step):
        rightward = chunk[l][0:4] + chunk[l][7:8]
        leftward = chunk[l][0:1] + chunk[l][4:8]
        lane = (rightward, leftward)[direction]
        scan = (right, left)[direction]
        src, dst = lane[step], lane[step + 1]
        if step == 3:
            part = pl.ds(direction * (tile_dev // 2), tile_dev // 2)
            src, dst = src.at[part], dst.at[part]
        return go(send(src, dst, zs.at[l], zr.at[l, direction, step], scan, q))

    moving = {}

    def step_on(l, step):
        for direction in (0, 1):
            if step > 0:
                moving[l, direction].wait_recv()
            moving[l, direction] = pass_on(l, direction, step)

    for l in range(2):
        local[l].wait()
        step_on(l, 0)
    for k, m in enumerate(others):
        go(send(probe_ref.at[0], pall_ref.at[q], ps.at[0], pr.at[0], here, m))

    lanes = lax.broadcasted_iota(jnp.int32, (RING, side), 1)
    depth = lax.broadcasted_iota(jnp.int32, (RING, side), 0)
    zero = jnp.zeros((RING, side), jnp.int32)
    owners = [owner_rows[n : n + 1, :] for n in range(owner_rows.shape[0])]
    my_first = first_ref[here, 0]
    span = first_ref.shape[0] // 2
    ring = at_spot(y, depth, core)
    owned = [jnp.where(row == ring, 1, 0) for row in owners]
    picks = []
    slots = zero
    for d in range(8):
        first = first_ref[at_spot(d // 2, z, d % 2), 0]
        before, slot = zero, zero
        ring = at_spot(d // 2, depth, d % 2)
        for n, row in enumerate(owners):
            tile = lanes + n * side
            before = before + jnp.where(tile < first, owned[n], 0)
            inside = (tile >= my_first) & (tile < my_first + 2 * span) & (row == ring)
            slot = jnp.maximum(slot, jnp.where(inside, tile - my_first, 0))
        picks.append(jnp.sum(before, axis=1, keepdims=True))
        slots = jnp.where(lanes == d, jnp.max(slot, axis=1, keepdims=True), slots)
    chosen, order, ends = zero, zero, zero
    for d in range(8):
        ahead = jnp.zeros_like(picks[d])
        for e in range(8):
            if e != d:
                ahead = ahead + jnp.where(picks[e] <= picks[d] if e < d else picks[e] < picks[d], 1, 0)
        chosen = jnp.where(lanes == d, picks[d], chosen)
        order = order + jnp.where(lanes == ahead, d, 0)
        ends = ends + jnp.where(picks[d] <= lanes, 1, 0)
    places = [pos_ref[1, j] >> 7 for j in range(batch)]
    ranks = [jnp.int32(0)] * batch
    for j in range(batch):
        for k in range(j):
            earlier = jnp.where(places[k] <= places[j], 1, 0)
            ranks[j] = ranks[j] + earlier
            ranks[k] = ranks[k] + (1 - earlier)
    queue, counted = zero, zero
    for j in range(batch):
        queue = queue + jnp.where(lanes == ranks[j], j, 0)
        counted = counted + jnp.where(places[j] < lanes - 1, 1, 0)
    for n, table in enumerate((chosen, order, ends, slots, jnp.where(depth == 0, queue, counted))):
        table_ref[n] = table
    pick_copy = pltpu.make_async_copy(table_ref, pick_ref, local_sem.at[5])
    pick_copy.start()
    pick_copy.wait()

    rounds = [0, -1, 1, -2, 2, -3, 3, 4]

    def offer(l, r):
        zi = (z + rounds[r] + RING) % RING
        buf = chunk[l][(0, 1, 4, 2, 5, 3, 6, 7)[r]]
        for n, scan, d in peers:
            ybuf[l, n, r] = buf[pick_ref[0, zi, d]]
            go(send(ybuf.at[l, n, r], win[l].at[mine * RING + zi], ys.at[l], yr.at[l], scan, q))
        win[l][mine * RING + zi] = buf[pick_ref[0, zi, mine]]

    shape = (2, quarter, side)
    rows = lax.broadcasted_iota(jnp.int32, shape, 1) + q * quarter
    cols = lax.broadcasted_iota(jnp.int32, shape, 2)

    def piece(l, j):
        row, col = pos_ref[0, j], pos_ref[1, j]
        near = my_first + (col >> 7)
        far = my_first + jnp.minimum((col >> 7) + 1, span - 1)
        tiles = [win[l][home(owner_ref[t])].astype(jnp.float32) for t in (near, far, near + span, far + span)]
        kept = cols >= (col & (side - 1))
        upper = jnp.where(kept, tiles[0], tiles[1])
        lower = jnp.where(kept, tiles[2], tiles[3])
        return jnp.where(rows >= row, upper, lower).astype(jnp.bfloat16)

    def x_copy(l, k, i, mode, target):
        return send(xbuf.at[l, k, i], x_ref.at[l, target, i], xs.at[l], xr.at[l, i], here, mode)

    def share(l):
        def pack(i, carry):
            for k in (1, 0, 2):
                xbuf[l, k, i] = piece(l, others[k] * npos + i)
                x_copy(l, k, i, others[k], q).start()
            x_ref[l, q, i] = piece(l, q * npos + i)
            return carry

        lax.fori_loop(0, npos, pack, 0)

    for l in range(2):
        offer(l, 0)
    step_on(0, 1)
    offer(0, 1)
    offer(0, 2)
    step_on(1, 1)
    offer(1, 1)
    offer(1, 2)
    step_on(0, 2)
    offer(0, 3)
    offer(0, 4)
    step_on(1, 2)
    offer(1, 3)
    step_on(0, 3)
    offer(0, 5)
    offer(0, 6)
    step_on(1, 3)
    offer(1, 4)
    for direction in (0, 1):
        moving[0, direction].wait_recv()
    offer(0, 7)
    offer(1, 5)
    for direction in (0, 1):
        moving[1, direction].wait_recv()
    offer(1, 6)
    offer(1, 7)
    for l in range(2):
        arrive(ybuf.at[l], yr.at[l])
        share(l)
    for copy in local[2:]:
        copy.wait()
    arrive(pall_ref.at[pl.ds(0, modes - 1)], pr.at[0])


    pair = 2
    count = pair * modes

    def block(m):
        return slice(m * side, (m + 1) * side)

    def load(hi_ref, lo_ref, fields):
        for m, (re, im) in enumerate(fields):
            rh, rl = split_parts(re)
            ih, il = split_parts(im)
            hi_ref[block(m), 0:side] = rh
            hi_ref[block(m), side : 2 * side] = ih
            lo_ref[block(m), 0:side] = rl
            lo_ref[block(m), side : 2 * side] = il

    def two_sided(right_table, left_table, hi_ref, lo_ref):
        for m in range(count):
            bh, bl = tab_ref[2 * right_table], tab_ref[2 * right_table + 1]
            whole = dot(hi_ref[block(m)], bh) + dot(lo_ref[block(m)], bh) + dot(hi_ref[block(m)], bl)
            hi, lo = split_parts(whole)
            c_hi[0:side, block(m)] = hi[:, 0:side]
            c_hi[side : 2 * side, block(m)] = hi[:, side : 2 * side]
            c_lo[0:side, block(m)] = lo[:, 0:side]
            c_lo[side : 2 * side, block(m)] = lo[:, side : 2 * side]
        lh, ll = tab_ref[2 * left_table], tab_ref[2 * left_table + 1]
        out = []
        for h in range(count // 2):
            cut = slice(h * 2 * side, (h + 1) * 2 * side)
            whole = dot(lh, c_hi[:, cut]) + dot(lh, c_lo[:, cut]) + dot(ll, c_hi[:, cut])
            for k in range(2):
                out.append((whole[0:side, block(k)], whole[side : 2 * side, block(k)]))
        return out

    def patch(l, p, n):
        arrive(x_ref.at[l, pl.ds(0, modes - 1), p], xr.at[l, p])
        row, col = pos_ref[0, q * npos + p], pos_ref[1, q * npos + p]
        for part in range(2):
            whole = jnp.concatenate([x_ref[l, k, p, part].astype(jnp.float32) for k in range(modes)], axis=0)
            whole = pltpu.roll(whole, (side - row) & (side - 1), 0)
            planes_ref[n, part] = pltpu.roll(whole, (side - (col & (side - 1))) & (side - 1), 1)

    def plane(n):
        return planes_ref[n, 0], planes_ref[n, 1]

    def wave(p, m):
        return wave_ref[p, m, 0], wave_ref[p, m, 1]

    def shone(m):
        return pall_ref[m, 0], pall_ref[m, 1]

    def times(wave, field):
        (wr, wi), (fr, fi) = wave, field
        return wr * fr - wi * fi, wr * fi + wi * fr

    def conj_times(wave, field):
        (wr, wi), (fr, fi) = wave, field
        return wr * fr + wi * fi, wr * fi - wi * fr

    def e_copy(l, k, p, mode, target):
        return send(ebuf.at[l, k, p], eq_ref[l].at[target, p], es.at[l], er.at[l], here, mode)

    def hand_out(l, p, n, total):
        row, col = pos_ref[0, q * npos + p], pos_ref[1, q * npos + p]
        for part in range(2):
            sum_ref[n, part] = pltpu.roll(pltpu.roll(total[part], row & (side - 1), 0), col & (side - 1), 1)
        def coded(mode):
            value = sum_ref[n, :, pl.ds(pl.multiple_of(mode * quarter, quarter), quarter)]
            step = column_scale(value)
            return encode(value, step), step

        for k in range(modes - 1):
            ebuf[l, k, p], e_out[l, k, pl.ds(p, 1)] = coded(others[k])
            e_copy(l, k, p, others[k], q).start()
        eq_ref[l][q, p], e_steps[l][q, pl.ds(p, 1)] = coded(q)

    def hand_out_steps(l):
        for k, m in enumerate(others):
            go(send(e_out.at[l, k], e_steps[l].at[q], ess.at[l], esr.at[l], here, m))

    def each(i):
        return [(n, i * pair + n, m) for n in range(pair) for m in range(modes)]

    def enter(i, carry):
        for n in range(pair):
            patch(0, i * pair + n, n)
            for part in range(2):
                xroll[i * pair + n, part] = planes_ref[n, part]
        load(a_hi, a_lo, [times(shone(m), plane(n)) for n, p, m in each(i)])
        for (n, p, m), (re, im) in zip(each(i), two_sided(2, 3, a_hi, a_lo)):
            wave_ref[p, m, 0] = re
            wave_ref[p, m, 1] = im
        return carry

    def summed(terms):
        return [functools.reduce(jnp.add, part) for part in zip(*terms)]

    def detect(i, carry):
        for n in range(pair):
            patch(1, i * pair + n, n)
        load(a_hi, a_lo, [times(wave(p, m), plane(n)) for n, p, m in each(i)])
        far = two_sided(0, 1, a_hi, a_lo)
        weighted = []
        for n in range(pair):
            mine_far = far[n * modes : (n + 1) * modes]
            intensity = background
            for re, im in mine_far:
                intensity = intensity + (re * re + im * im)
            weight = 1.0 - counts_ref[i * pair + n].astype(jnp.float32) / intensity
            weighted.extend((weight * re, weight * im) for re, im in mine_far)
        load(a_hi, a_lo, weighted)
        grads = two_sided(1, 0, a_hi, a_lo)
        load(b_hi.at[i], b_lo.at[i], [conj_times(plane(n), grad) for (n, p, m), grad in zip(each(i), grads)])
        terms = [conj_times(wave(p, m), grad) for (n, p, m), grad in zip(each(i), grads)]
        for n in range(pair):
            hand_out(1, i * pair + n, n, summed(terms[n * modes : (n + 1) * modes]))
        return carry

    def leave(i, carry):
        grads = two_sided(3, 2, b_hi.at[i], b_lo.at[i])
        for m in range(modes):
            terms = [conj_times((xroll[p, 0], xroll[p, 1]), grad) for (n, p, k), grad in zip(each(i), grads) if k == m]
            for part, term in enumerate(summed(terms)):
                pp_ref[m, part * side : (part + 1) * side] += term
        terms = [conj_times(shone(m), grad) for (n, p, m), grad in zip(each(i), grads)]
        for n in range(pair):
            hand_out(0, i * pair + n, n, summed(terms[n * modes : (n + 1) * modes]))
        return carry

    lax.fori_loop(0, npos // pair, enter, 0)
    e_out[...] = jnp.zeros_like(e_out)
    lax.fori_loop(0, npos // pair, detect, 0)
    hand_out_steps(1)
    pp_ref[...] = jnp.zeros_like(pp_ref)
    lax.fori_loop(0, npos // pair, leave, 0)
    hand_out_steps(0)


    def gather_e(l):
        arrive(eq_ref[l].at[pl.ds(0, modes - 1)], er.at[l])
        arrive(e_steps[l].at[pl.ds(0, modes - 1)], esr.at[l])

    def lay(l):
        blank = jnp.zeros(shape, jnp.float32)
        for u in range(2):
            left_sum[l][u, 0] = blank
            right_sum[l][u, 0] = blank

        def add(n, carry):
            j = pick_ref[4, 0, n]
            kept = cols >= (pos_ref[1, j] & (side - 1))
            upper = rows >= pos_ref[0, j]
            term = decode(eq_ref[l][j // npos, j % npos]) * e_steps[l][j // npos, pl.ds(j % npos, 1)]
            lefts, rights = jnp.where(kept, term, 0.0), jnp.where(kept, 0.0, term)
            for sums, part in ((left_sum[l], lefts), (right_sum[l], rights)):
                sums[0, n + 1] = sums[0, n] + jnp.where(upper, part, 0.0)
                sums[1, n + 1] = sums[1, n] + jnp.where(upper, 0.0, part)
            return carry

        lax.fori_loop(0, batch, add, 0)

    back = [4, 3, -3, 2, -2, 1, -1, 0]

    def zi(r):
        return (z + back[r] + RING) % RING

    def code(l):
        def one(place, carry):
            for d in range(8):
                slot = pick_ref[3, place, d]
                u, w = slot >> 5, slot & (span - 1)
                low, middle, high = pick_ref[4, 1, w], pick_ref[4, 1, w + 1], pick_ref[4, 1, w + 2]
                value = (left_sum[l][u, high] - left_sum[l][u, middle]) + (right_sum[l][u, middle] - right_sum[l][u, low])
                step = column_scale(value)
                cscale[l, d, pl.ds(place, 1)] = step
                codes[l, d, place] = encode(value, step)
            return carry

        lax.fori_loop(0, RING, one, 0)
        for n, scan, d in peers:
            go(send(cscale.at[l, d], rscale[l].at[mine], tcs.at[l], tcr.at[l], scan, q))
        rscale[l][mine] = cscale[l, mine]

    def yield_up(l, r):
        for n, scan, d in peers:
            go(send(codes.at[l, d, zi(r)], rbuf[l][r].at[mine], ts.at[l], tr.at[l, r], scan, q))
        rbuf[l][r][mine] = codes[l, mine, zi(r)]

    def await_up(l, r):
        arrive(rbuf[l][r].at[pl.ds(0, 7)], tr.at[l, r])

    def await_scales(l):
        arrive(rscale[l].at[pl.ds(0, 7)], tcr.at[l])

    given[0] = jnp.zeros(shape, jnp.float32)

    def combine(l, r, received, use):
        place = zi(r)
        total = jnp.zeros(shape, jnp.float32)
        for n in range(8):
            giver = pick_ref[1, place, n]
            total = total + decode(rbuf[l][r][giver]) * rscale[l][giver, pl.ds(place, 1)]
            given[n + 1] = total
        received = received()
        start = 0
        for k in range(tile_dev):
            end = pick_ref[2, place, k]
            value = given[end] - given[start]
            for ref, ref_scale, held in received:
                if k in held:
                    value = value + decode(ref[k]) * ref_scale[k : k + 1]
            use(k, value)
            start = end

    def ship(l, direction, step, tiles):
        at = (l, direction, step)
        buf, to = out_of[l][direction][step].at[tiles], into[l][direction][step].at[tiles]
        scan = (right, left)[direction]
        return (
            go(send(sscale.at[at], zscale.at[at], ucs.at[l], ucr.at[at], scan, q)),
            go(send(buf, to, us.at[l], ur.at[at], scan, q)),
        )

    def packer(l, direction, step):
        def pack(k, value):
            side_of = (k // half_dev) if direction is None else direction
            step_size = column_scale(value)
            sscale[l, side_of, step, k : k + 1] = step_size
            out_of[l][side_of][step][k] = encode(value, step_size)

        return pack

    flying = {}
    half_dev = tile_dev // 2
    halves = (pl.ds(0, half_dev), pl.ds(half_dev, half_dev))

    def arrived(l, direction, step):
        for copy in flying[l, direction]:
            copy.wait_recv()
        held = range(direction * half_dev, (direction + 1) * half_dev) if step == 1 else range(tile_dev)
        return [(into[l][direction][step - 1], zscale.at[l, direction, step - 1], held)]

    def turn(l, step):
        if step == 0:
            await_scales(l)
            await_up(l, 0)
            for scan_side in range(2):
                sscale[l, scan_side, 0] = jnp.zeros_like(sscale[l, scan_side, 0])
            combine(l, 0, lambda: [], packer(l, None, 0))
            for direction in (0, 1):
                flying[l, direction] = ship(l, direction, 0, halves[direction])
            return
        for direction in (0, 1):
            r = 2 * step - 1 + direction
            await_up(l, r)
            combine(l, r, lambda: arrived(l, direction, step), packer(l, direction, step))
            flying[l, direction] = ship(l, direction, step, pl.ds(0, tile_dev))

    def probe_over_modes():
        arrive(pxb, p0r.at[0])
        total = pp_ref[q]
        for k in range(modes - 1):
            total = total + pxb[k]
        pxs[...] = total.reshape(pxs.shape)
        for n, scan, d in peers:
            go(send(pxs.at[d], pyb.at[n], p1s.at[0], p1r.at[0], scan, q))

    def probe_over_plane():
        arrive(pyb, p1r.at[0])
        total = pxs[mine]
        for n in range(7):
            total = total + pyb[n]
        pzs[...] = total
        for k, scan in enumerate(column):
            go(send(pzs, pzb.at[k], p2s.at[0], p2r.at[0], scan, q))

    def probe_over_ring():
        arrive(pzb, p2r.at[0])
        total = pzs[...]
        for k in range(RING - 1):
            total = total + pzb[k]
        pg_ref[mine] = total * scale
        for n, scan, d in peers:
            go(send(pg_ref.at[mine], pg_ref.at[mine], p3s.at[0], p3r.at[0], scan, q))

    def keep(l):
        def put(k, value):
            out_ref[k, l] = value

        return put

    gather_e(1)
    lay(1)
    code(1)
    for r in range(5):
        yield_up(1, r)
    for k, m in enumerate(others):
        go(send(pp_ref.at[m], pxb.at[k], p0s.at[0], p0r.at[0], here, m))
    gather_e(0)
    lay(0)
    turn(1, 0)
    code(0)
    for r in range(5):
        yield_up(0, r)
    turn(1, 1)
    turn(0, 0)
    yield_up(1, 5)
    yield_up(1, 6)
    probe_over_modes()
    turn(0, 1)
    yield_up(0, 5)
    yield_up(0, 6)
    turn(1, 2)
    yield_up(1, 7)
    probe_over_plane()
    turn(0, 2)
    yield_up(0, 7)
    turn(1, 3)
    probe_over_ring()
    turn(0, 3)
    for l in (1, 0):
        await_up(l, 7)
        combine(l, 7, lambda: arrived(l, 0, 4) + arrived(l, 1, 4), keep(l))
    arrive(pg_ref.at[pl.ds(0, 7)], p3r.at[0])

    def departed(ref, sem):
        send(ref, ref, sem, sem, here, q).wait_send()

    for l in range(2):
        departed(ybuf.at[l], zs.at[l])
        departed(ybuf.at[l], ys.at[l])
        departed(xbuf.at[l], xs.at[l])
        departed(ebuf.at[l], es.at[l])
        departed(e_out.at[l], ess.at[l])
        departed(codes.at[l, pl.ds(0, 7)], ts.at[l])
        departed(cscale.at[l, pl.ds(0, 7)], tcs.at[l])
        departed(codes.at[l, pl.ds(0, 7)], us.at[l])
        departed(cscale.at[l], ucs.at[l])
    departed(pall_ref.at[pl.ds(0, modes - 1)], ps.at[0])
    departed(pxb, p0s.at[0])
    departed(pyb, p1s.at[0])
    departed(pzb, p2s.at[0])
    departed(pg_ref.at[pl.ds(0, 7)], p3s.at[0])


def gradients(tile_owner, block_tiles, positions, tiles, probe, counts, tables, modes, scale):
    tile_dev, slices, parts, side, _ = tiles.shape
    quarter = side // modes
    batch = positions.shape[0]
    npos = batch // modes
    dma = pltpu.SemaphoreType.DMA
    smem, anywhere, vmem = (pl.BlockSpec(memory_space=space) for space in (pltpu.SMEM, pl.ANY, pltpu.VMEM))
    tile = (parts, quarter, side)

    def wide(*dims):
        return pltpu.VMEM(dims, jnp.float32)

    def half(*dims):
        return pltpu.VMEM(dims, jnp.bfloat16)

    def short(*dims):
        return pltpu.VMEM(dims, jnp.int16)

    piece = (parts * side // 8, side)
    scratch = [half(tile_dev, *tile)] * 16 + [half(8 * RING, *tile)] * 2
    scratch += [
        half(slices, 7, RING, *tile),
        half(slices, modes - 1, npos, *tile),
        half(slices, modes, npos, *tile),
        wide(modes, parts, side, side),
        pltpu.VMEM((npos, side, side), counts.dtype),
        half(*tables.shape),
        short(slices, modes - 1, npos, *tile),
        short(modes, npos, *tile),
        short(modes, npos, *tile),
        wide(modes, 8, side),
        wide(modes, 8, side),
        wide(slices, modes - 1, 8, side),
        wide(modes, parts * side, side),
        half(2 * modes * side, 2 * side),
        half(2 * modes * side, 2 * side),
        half(npos // 2, 2 * modes * side, 2 * side),
        half(npos // 2, 2 * modes * side, 2 * side),
        half(2 * side, 2 * modes * side),
        half(2 * side, 2 * modes * side),
        wide(2, parts, side, side),
        wide(npos, parts, side, side),
        wide(npos, modes, parts, side, side),
        wide(2, parts, side, side),
    ]
    scratch += [wide(2, batch + 1, *tile)] * 4
    scratch += [short(8, *tile)] * 16 + [wide(8, RING, side)] * 2
    scratch += [short(tile_dev, *tile)] * 32
    scratch += [
        short(slices, 8, RING, *tile),
        wide(slices, 8, RING, side),
        wide(slices, 2, 4, tile_dev, side),
        wide(slices, 2, 4, tile_dev, side),
        wide(9, *tile),
        wide(modes - 1, parts * side, side),
        wide(8, *piece),
        wide(7, *piece),
        wide(*piece),
        wide(RING - 1, *piece),
        pltpu.VMEM((5, RING, side), jnp.int32),
        pltpu.SMEM((5, RING, side), jnp.int32),
    ]
    sizes = [(6,), (slices,), (slices, 2, 4), (slices,), (slices,), (slices,), (slices, npos)]
    sizes += [(1,), (1,), (slices,), (slices,), (slices,), (slices,)]
    sizes += [(slices,), (slices, RING), (slices,), (slices,), (slices,), (slices, 2, 4), (slices,), (slices, 2, 4)]
    sizes += [(1,)] * 8
    scratch += [dma(size) for size in sizes]
    return pl.pallas_call(
        functools.partial(kernel_body, scale=scale),
        in_specs=[smem, smem, smem, vmem, anywhere, anywhere, anywhere, anywhere],
        out_specs=[vmem, vmem],
        out_shape=[
            jax.ShapeDtypeStruct((tile_dev, slices) + tile, jnp.float32),
            jax.ShapeDtypeStruct((8,) + piece, jnp.float32),
        ],
        scratch_shapes=scratch,
        compiler_params=pltpu.CompilerParams(
            collective_id=0, has_side_effects=True, vmem_limit_bytes=60 * MIB
        ),
        name="gradients",
    )(tile_owner, block_tiles, positions.T, tile_owner.reshape(-1, side), tiles, probe, counts, tables)


def shards(object_tiles, tile_owner, block_tiles, positions, counts, probe):
    scan_count = lax.axis_size("scan")
    mode_count = lax.axis_size("mode")
    batch = positions.shape[0]
    tables = jnp.asarray(transform_tables(object_tiles.shape[3]))
    object_grad, probe_grad = gradients(
        tile_owner, block_tiles, positions, object_tiles, probe, counts, tables, mode_count, 1.0 / (batch * scan_count)
    )
    return (object_grad, probe_grad.reshape(probe.shape))


def solution(mesh):
    placed = (
        P("scan", None, None, None, None),
        P(),
        P(),
        P("scan", None),
        P("scan", None, None),
        P("mode", None, None, None),
    )
    return jax.shard_map(
        shards,
        mesh=mesh,
        in_specs=placed,
        out_specs=(P("scan", None, None, "mode", None), P("mode", None, None, None)),
        check_vma=False,
    )
```

```python
import functools

import jax
import jax.numpy as jnp
import ml_dtypes
import numpy as np
from jax import lax
from jax.experimental import pallas as pl
from jax.experimental.pallas import tpu as pltpu
from jax.sharding import PartitionSpec as P

background = 0.25
fresnel_number = 1.0
MIB = 1024 * 1024
RING = 8
STEPS = 32767.0


def split_const(matrix):
    hi = matrix.astype(ml_dtypes.bfloat16)
    lo = (matrix - hi.astype(np.float64)).astype(ml_dtypes.bfloat16)
    return hi, lo


def transform_tables(side):
    index = np.arange(side)
    four = np.exp(-2j * np.pi * (index[:, None] * index[None, :] % side) / side) / np.sqrt(side)
    frequency = np.where(index < side // 2, index, index - side) / side
    chirp = np.exp(-1j * np.pi * fresnel_number * frequency * frequency)
    prop = (four.conj() * chirp[None, :]) @ four
    blocks = []
    for matrix in (four, prop):
        re, im = matrix.real, matrix.imag
        blocks.append(np.block([[re, im], [-im, re]]))
        blocks.append(np.block([[re, -im], [im, re]]))
    parts = []
    for block in blocks:
        parts.extend(split_const(block))
    return np.stack(parts)


def split_parts(value):
    hi = value.astype(jnp.bfloat16)
    lo = (value - hi.astype(jnp.float32)).astype(jnp.bfloat16)
    return hi, lo


def dot(a, b):
    return jnp.dot(a, b, preferred_element_type=jnp.float32)


def spot(scan):
    return scan // (2 * RING), scan // 2 % RING, scan % 2


def at_spot(y, z, core):
    return (y * RING + z) * 2 + core


def plane_peers(y, z, core):
    peers = []
    for number in range(1, 8):
        there_y, there_core = (y + number // 2) % 4, (core + number % 2) % 2
        peers.append((number - 1, at_spot(there_y, z, there_core), there_y * 2 + there_core))
    return peers


def send(src, dst, send_sem, recv_sem, scan, mode):
    return pltpu.make_async_remote_copy(
        src_ref=src,
        dst_ref=dst,
        send_sem=send_sem,
        recv_sem=recv_sem,
        device_id={"scan": scan, "mode": mode},
        device_id_type=pl.DeviceIdType.MESH,
    )


def received(ref, sem, scan, mode):
    send(ref, ref, sem, sem, scan, mode).wait_recv()


def meet(partners):
    barrier = pltpu.get_barrier_semaphore()
    for scan, mode in partners:
        pl.semaphore_signal(
            barrier, inc=1, device_id={"scan": scan, "mode": mode}, device_id_type=pl.DeviceIdType.MESH
        )
    pl.semaphore_wait(barrier, len(partners))


def home(owner):
    y, z, core = owner >> 4, (owner >> 1) & (RING - 1), owner & 1
    return (y * 2 + core) * RING + z


def column_scale(value):
    most = jnp.max(jnp.max(jnp.abs(value), axis=0), axis=0, keepdims=True)
    return jnp.maximum(most, 1e-30) * (1.0 / STEPS)


def encode(value, scale):
    return jnp.round(value * (1.0 / scale)).astype(jnp.int32).astype(jnp.int16)


def decode(code):
    return code.astype(jnp.int32).astype(jnp.float32)


def kernel_body(owner_ref, first_ref, pos_ref, owner_rows, obj_ref, probe_ref, counts_any, tab_any, out_ref, pg_ref, *scratch, scale=1.0):
    names = iter(scratch)

    def several(count):
        return [next(names) for _ in range(count)]

    chunk = [several(8) for _ in range(2)]
    win = several(2)
    ybuf, xbuf, x_ref, pall_ref, counts_ref, tab_ref, ebuf = several(7)
    eq_ref, e_steps = several(2), several(2)
    e_out, pp_ref = several(2)
    a_hi, a_lo, b_hi, b_lo, c_hi, c_lo, planes_ref, xroll, wave_ref, sum_ref = several(10)
    left_sum, right_sum = several(2), several(2)
    rbuf = [several(8) for _ in range(2)]
    rscale = several(2)
    out_of = [[several(4) for _ in range(2)] for _ in range(2)]
    into = [[several(4) for _ in range(2)] for _ in range(2)]
    codes, cscale, sscale, zscale, given, pxb, pxs, pyb, pzs, pzb, table_ref, pick_ref = several(12)
    local_sem, zs, zr, ys, yr, xs, xr, ps, pr, es, er, ess, esr = several(13)
    ts, tr, tcs, tcr, us, ur, ucs, ucr, p0s, p0r, p1s, p1r, p2s, p2r, p3s, p3r = several(16)

    here, q = lax.axis_index("scan"), lax.axis_index("mode")
    y, z, core = spot(here)
    mine = y * 2 + core
    tile_dev, _, quarter, side = chunk[0][0].shape
    modes, npos = x_ref.shape[1:3]
    batch = modes * npos
    local = [
        pltpu.make_async_copy(
            obj_ref.at[:, l, :, pl.ds(q * quarter, quarter), :], chunk[l][0], local_sem.at[l]
        )
        for l in range(2)
    ]
    local.extend(
        [
            pltpu.make_async_copy(probe_ref.at[0], pall_ref.at[q], local_sem.at[2]),
            pltpu.make_async_copy(tab_any, tab_ref, local_sem.at[3]),
            pltpu.make_async_copy(counts_any.at[pl.ds(q * npos, npos)], counts_ref, local_sem.at[4]),
        ]
    )
    for copy in local:
        copy.start()
    right, left = at_spot(y, (z + 1) % RING, core), at_spot(y, (z + RING - 1) % RING, core)
    peers = plane_peers(y, z, core)
    column = [at_spot(y, (z + k) % RING, core) for k in range(1, RING)]
    others = [(q + k) % modes for k in range(1, modes)]
    meet([(scan, q) for scan in column] + [(scan, q) for _, scan, _ in peers] + [(here, m) for m in others])

    def go(copy):
        copy.start()
        return copy

    def arrive(ref, sem):
        received(ref, sem, here, q)


    def pass_on(l, direction, step):
        rightward = chunk[l][0:4] + chunk[l][7:8]
        leftward = chunk[l][0:1] + chunk[l][4:8]
        lane = (rightward, leftward)[direction]
        scan = (right, left)[direction]
        src, dst = lane[step], lane[step + 1]
        if step == 3:
            part = pl.ds(direction * (tile_dev // 2), tile_dev // 2)
            src, dst = src.at[part], dst.at[part]
        return go(send(src, dst, zs.at[l], zr.at[l, direction, step], scan, q))

    moving = {}

    def step_on(l, step):
        for direction in (0, 1):
            if step > 0:
                moving[l, direction].wait_recv()
            moving[l, direction] = pass_on(l, direction, step)

    for l in range(2):
        local[l].wait()
        step_on(l, 0)
    for k, m in enumerate(others):
        go(send(probe_ref.at[0], pall_ref.at[q], ps.at[0], pr.at[0], here, m))

    lanes = lax.broadcasted_iota(jnp.int32, (RING, side), 1)
    depth = lax.broadcasted_iota(jnp.int32, (RING, side), 0)
    zero = jnp.zeros((RING, side), jnp.int32)
    owners = [owner_rows[n : n + 1, :] for n in range(owner_rows.shape[0])]
    my_first = first_ref[here, 0]
    span = first_ref.shape[0] // 2
    ring = at_spot(y, depth, core)
    owned = [jnp.where(row == ring, 1, 0) for row in owners]
    picks = []
    slots = zero
    for d in range(8):
        first = first_ref[at_spot(d // 2, z, d % 2), 0]
        before, slot = zero, zero
        ring = at_spot(d // 2, depth, d % 2)
        for n, row in enumerate(owners):
            tile = lanes + n * side
            before = before + jnp.where(tile < first, owned[n], 0)
            inside = (tile >= my_first) & (tile < my_first + 2 * span) & (row == ring)
            slot = jnp.maximum(slot, jnp.where(inside, tile - my_first, 0))
        picks.append(jnp.sum(before, axis=1, keepdims=True))
        slots = jnp.where(lanes == d, jnp.max(slot, axis=1, keepdims=True), slots)
    chosen, order, ends = zero, zero, zero
    for d in range(8):
        ahead = jnp.zeros_like(picks[d])
        for e in range(8):
            if e != d:
                ahead = ahead + jnp.where(picks[e] <= picks[d] if e < d else picks[e] < picks[d], 1, 0)
        chosen = jnp.where(lanes == d, picks[d], chosen)
        order = order + jnp.where(lanes == ahead, d, 0)
        ends = ends + jnp.where(picks[d] <= lanes, 1, 0)
    places = [pos_ref[1, j] >> 7 for j in range(batch)]
    ranks = [jnp.int32(0)] * batch
    for j in range(batch):
        for k in range(j):
            earlier = jnp.where(places[k] <= places[j], 1, 0)
            ranks[j] = ranks[j] + earlier
            ranks[k] = ranks[k] + (1 - earlier)
    queue, counted = zero, zero
    for j in range(batch):
        queue = queue + jnp.where(lanes == ranks[j], j, 0)
        counted = counted + jnp.where(places[j] < lanes - 1, 1, 0)
    for n, table in enumerate((chosen, order, ends, slots, jnp.where(depth == 0, queue, counted))):
        table_ref[n] = table
    pick_copy = pltpu.make_async_copy(table_ref, pick_ref, local_sem.at[5])
    pick_copy.start()
    pick_copy.wait()

    rounds = [0, -1, 1, -2, 2, -3, 3, 4]

    def offer(l, r):
        zi = (z + rounds[r] + RING) % RING
        buf = chunk[l][(0, 1, 4, 2, 5, 3, 6, 7)[r]]
        for n, scan, d in peers:
            ybuf[l, n, r] = buf[pick_ref[0, zi, d]]
            go(send(ybuf.at[l, n, r], win[l].at[mine * RING + zi], ys.at[l], yr.at[l], scan, q))
        win[l][mine * RING + zi] = buf[pick_ref[0, zi, mine]]

    shape = (2, quarter, side)
    rows = lax.broadcasted_iota(jnp.int32, shape, 1) + q * quarter
    cols = lax.broadcasted_iota(jnp.int32, shape, 2)

    def piece(l, j):
        row, col = pos_ref[0, j], pos_ref[1, j]
        near = my_first + (col >> 7)
        far = my_first + jnp.minimum((col >> 7) + 1, span - 1)
        tiles = [win[l][home(owner_ref[t])].astype(jnp.float32) for t in (near, far, near + span, far + span)]
        kept = cols >= (col & (side - 1))
        upper = jnp.where(kept, tiles[0], tiles[1])
        lower = jnp.where(kept, tiles[2], tiles[3])
        return jnp.where(rows >= row, upper, lower).astype(jnp.bfloat16)

    def x_copy(l, k, i, mode, target):
        return send(xbuf.at[l, k, i], x_ref.at[l, target, i], xs.at[l], xr.at[l, i], here, mode)

    def share(l):
        def pack(i, carry):
            for k in (1, 0, 2):
                xbuf[l, k, i] = piece(l, others[k] * npos + i)
                x_copy(l, k, i, others[k], q).start()
            x_ref[l, q, i] = piece(l, q * npos + i)
            return carry

        lax.fori_loop(0, npos, pack, 0)

    for l in range(2):
        offer(l, 0)
    step_on(0, 1)
    offer(0, 1)
    offer(0, 2)
    step_on(1, 1)
    offer(1, 1)
    offer(1, 2)
    step_on(0, 2)
    offer(0, 3)
    offer(0, 4)
    step_on(1, 2)
    offer(1, 3)
    step_on(0, 3)
    offer(0, 5)
    offer(0, 6)
    step_on(1, 3)
    offer(1, 4)
    for direction in (0, 1):
        moving[0, direction].wait_recv()
    offer(0, 7)
    offer(1, 5)
    for direction in (0, 1):
        moving[1, direction].wait_recv()
    offer(1, 6)
    offer(1, 7)
    for l in range(2):
        arrive(ybuf.at[l], yr.at[l])
        share(l)
    for copy in local[2:]:
        copy.wait()
    arrive(pall_ref.at[pl.ds(0, modes - 1)], pr.at[0])


    pair = 2
    count = pair * modes

    def block(m):
        return slice(m * side, (m + 1) * side)

    def load(hi_ref, lo_ref, fields):
        for m, (re, im) in enumerate(fields):
            rh, rl = split_parts(re)
            ih, il = split_parts(im)
            hi_ref[block(m), 0:side] = rh
            hi_ref[block(m), side : 2 * side] = ih
            lo_ref[block(m), 0:side] = rl
            lo_ref[block(m), side : 2 * side] = il

    def two_sided(right_table, left_table, hi_ref, lo_ref):
        for m in range(count):
            bh, bl = tab_ref[2 * right_table], tab_ref[2 * right_table + 1]
            whole = dot(hi_ref[block(m)], bh) + dot(lo_ref[block(m)], bh) + dot(hi_ref[block(m)], bl)
            hi, lo = split_parts(whole)
            c_hi[0:side, block(m)] = hi[:, 0:side]
            c_hi[side : 2 * side, block(m)] = hi[:, side : 2 * side]
            c_lo[0:side, block(m)] = lo[:, 0:side]
            c_lo[side : 2 * side, block(m)] = lo[:, side : 2 * side]
        lh, ll = tab_ref[2 * left_table], tab_ref[2 * left_table + 1]
        out = []
        for h in range(count // 2):
            cut = slice(h * 2 * side, (h + 1) * 2 * side)
            whole = dot(lh, c_hi[:, cut]) + dot(lh, c_lo[:, cut]) + dot(ll, c_hi[:, cut])
            for k in range(2):
                out.append((whole[0:side, block(k)], whole[side : 2 * side, block(k)]))
        return out

    def patch(l, p, n):
        arrive(x_ref.at[l, pl.ds(0, modes - 1), p], xr.at[l, p])
        row, col = pos_ref[0, q * npos + p], pos_ref[1, q * npos + p]
        for part in range(2):
            whole = jnp.concatenate([x_ref[l, k, p, part].astype(jnp.float32) for k in range(modes)], axis=0)
            whole = pltpu.roll(whole, (side - row) & (side - 1), 0)
            planes_ref[n, part] = pltpu.roll(whole, (side - (col & (side - 1))) & (side - 1), 1)

    def plane(n):
        return planes_ref[n, 0], planes_ref[n, 1]

    def wave(p, m):
        return wave_ref[p, m, 0], wave_ref[p, m, 1]

    def shone(m):
        return pall_ref[m, 0], pall_ref[m, 1]

    def times(wave, field):
        (wr, wi), (fr, fi) = wave, field
        return wr * fr - wi * fi, wr * fi + wi * fr

    def conj_times(wave, field):
        (wr, wi), (fr, fi) = wave, field
        return wr * fr + wi * fi, wr * fi - wi * fr

    def e_copy(l, k, p, mode, target):
        return send(ebuf.at[l, k, p], eq_ref[l].at[target, p], es.at[l], er.at[l], here, mode)

    def hand_out(l, p, n, total):
        row, col = pos_ref[0, q * npos + p], pos_ref[1, q * npos + p]
        for part in range(2):
            sum_ref[n, part] = pltpu.roll(pltpu.roll(total[part], row & (side - 1), 0), col & (side - 1), 1)
        def coded(mode):
            value = sum_ref[n, :, pl.ds(pl.multiple_of(mode * quarter, quarter), quarter)]
            step = column_scale(value)
            return encode(value, step), step

        for k in range(modes - 1):
            ebuf[l, k, p], e_out[l, k, pl.ds(p, 1)] = coded(others[k])
            e_copy(l, k, p, others[k], q).start()
        eq_ref[l][q, p], e_steps[l][q, pl.ds(p, 1)] = coded(q)

    def hand_out_steps(l):
        for k, m in enumerate(others):
            go(send(e_out.at[l, k], e_steps[l].at[q], ess.at[l], esr.at[l], here, m))

    def each(i):
        return [(n, i * pair + n, m) for n in range(pair) for m in range(modes)]

    def enter(i, carry):
        for n in range(pair):
            patch(0, i * pair + n, n)
            for part in range(2):
                xroll[i * pair + n, part] = planes_ref[n, part]
        load(a_hi, a_lo, [times(shone(m), plane(n)) for n, p, m in each(i)])
        for (n, p, m), (re, im) in zip(each(i), two_sided(2, 3, a_hi, a_lo)):
            wave_ref[p, m, 0] = re
            wave_ref[p, m, 1] = im
        return carry

    def summed(terms):
        return [functools.reduce(jnp.add, part) for part in zip(*terms)]

    def detect(i, carry):
        for n in range(pair):
            patch(1, i * pair + n, n)
        load(a_hi, a_lo, [times(wave(p, m), plane(n)) for n, p, m in each(i)])
        far = two_sided(0, 1, a_hi, a_lo)
        weighted = []
        for n in range(pair):
            mine_far = far[n * modes : (n + 1) * modes]
            intensity = background
            for re, im in mine_far:
                intensity = intensity + (re * re + im * im)
            weight = 1.0 - counts_ref[i * pair + n].astype(jnp.float32) / intensity
            weighted.extend((weight * re, weight * im) for re, im in mine_far)
        load(a_hi, a_lo, weighted)
        grads = two_sided(1, 0, a_hi, a_lo)
        load(b_hi.at[i], b_lo.at[i], [conj_times(plane(n), grad) for (n, p, m), grad in zip(each(i), grads)])
        terms = [conj_times(wave(p, m), grad) for (n, p, m), grad in zip(each(i), grads)]
        for n in range(pair):
            hand_out(1, i * pair + n, n, summed(terms[n * modes : (n + 1) * modes]))
        return carry

    def leave(i, carry):
        grads = two_sided(3, 2, b_hi.at[i], b_lo.at[i])
        for m in range(modes):
            terms = [conj_times((xroll[p, 0], xroll[p, 1]), grad) for (n, p, k), grad in zip(each(i), grads) if k == m]
            for part, term in enumerate(summed(terms)):
                pp_ref[m, part * side : (part + 1) * side] += term
        terms = [conj_times(shone(m), grad) for (n, p, m), grad in zip(each(i), grads)]
        for n in range(pair):
            hand_out(0, i * pair + n, n, summed(terms[n * modes : (n + 1) * modes]))
        return carry

    lax.fori_loop(0, npos // pair, enter, 0)
    e_out[...] = jnp.zeros_like(e_out)
    lax.fori_loop(0, npos // pair, detect, 0)
    hand_out_steps(1)
    pp_ref[...] = jnp.zeros_like(pp_ref)
    lax.fori_loop(0, npos // pair, leave, 0)
    hand_out_steps(0)


    def gather_e(l):
        arrive(eq_ref[l].at[pl.ds(0, modes - 1)], er.at[l])
        arrive(e_steps[l].at[pl.ds(0, modes - 1)], esr.at[l])

    def lay(l):
        blank = jnp.zeros(shape, jnp.float32)
        for u in range(2):
            left_sum[l][u, 0] = blank
            right_sum[l][u, 0] = blank

        def add(n, carry):
            j = pick_ref[4, 0, n]
            kept = cols >= (pos_ref[1, j] & (side - 1))
            upper = rows >= pos_ref[0, j]
            term = decode(eq_ref[l][j // npos, j % npos]) * e_steps[l][j // npos, pl.ds(j % npos, 1)]
            lefts, rights = jnp.where(kept, term, 0.0), jnp.where(kept, 0.0, term)
            for sums, part in ((left_sum[l], lefts), (right_sum[l], rights)):
                sums[0, n + 1] = sums[0, n] + jnp.where(upper, part, 0.0)
                sums[1, n + 1] = sums[1, n] + jnp.where(upper, 0.0, part)
            return carry

        lax.fori_loop(0, batch, add, 0)

    back = [4, 3, -3, 2, -2, 1, -1, 0]

    def zi(r):
        return (z + back[r] + RING) % RING

    def code(l):
        def one(place, carry):
            for d in range(8):
                slot = pick_ref[3, place, d]
                u, w = slot >> 5, slot & (span - 1)
                low, middle, high = pick_ref[4, 1, w], pick_ref[4, 1, w + 1], pick_ref[4, 1, w + 2]
                value = (left_sum[l][u, high] - left_sum[l][u, middle]) + (right_sum[l][u, middle] - right_sum[l][u, low])
                step = column_scale(value)
                cscale[l, d, pl.ds(place, 1)] = step
                codes[l, d, place] = encode(value, step)
            return carry

        lax.fori_loop(0, RING, one, 0)
        for n, scan, d in peers:
            go(send(cscale.at[l, d], rscale[l].at[mine], tcs.at[l], tcr.at[l], scan, q))
        rscale[l][mine] = cscale[l, mine]

    def yield_up(l, r):
        for n, scan, d in peers:
            go(send(codes.at[l, d, zi(r)], rbuf[l][r].at[mine], ts.at[l], tr.at[l, r], scan, q))
        rbuf[l][r][mine] = codes[l, mine, zi(r)]

    def await_up(l, r):
        arrive(rbuf[l][r].at[pl.ds(0, 7)], tr.at[l, r])

    def await_scales(l):
        arrive(rscale[l].at[pl.ds(0, 7)], tcr.at[l])

    given[0] = jnp.zeros(shape, jnp.float32)

    def combine(l, r, received, use):
        place = zi(r)
        total = jnp.zeros(shape, jnp.float32)
        for n in range(8):
            giver = pick_ref[1, place, n]
            total = total + decode(rbuf[l][r][giver]) * rscale[l][giver, pl.ds(place, 1)]
            given[n + 1] = total
        received = received()
        start = 0
        for k in range(tile_dev):
            end = pick_ref[2, place, k]
            value = given[end] - given[start]
            for ref, ref_scale, held in received:
                if k in held:
                    value = value + decode(ref[k]) * ref_scale[k : k + 1]
            use(k, value)
            start = end

    def ship(l, direction, step, tiles):
        at = (l, direction, step)
        buf, to = out_of[l][direction][step].at[tiles], into[l][direction][step].at[tiles]
        scan = (right, left)[direction]
        return (
            go(send(sscale.at[at], zscale.at[at], ucs.at[l], ucr.at[at], scan, q)),
            go(send(buf, to, us.at[l], ur.at[at], scan, q)),
        )

    def packer(l, direction, step):
        def pack(k, value):
            side_of = (k // half_dev) if direction is None else direction
            step_size = column_scale(value)
            sscale[l, side_of, step, k : k + 1] = step_size
            out_of[l][side_of][step][k] = encode(value, step_size)

        return pack

    flying = {}
    half_dev = tile_dev // 2
    halves = (pl.ds(0, half_dev), pl.ds(half_dev, half_dev))

    def arrived(l, direction, step):
        for copy in flying[l, direction]:
            copy.wait_recv()
        held = range(direction * half_dev, (direction + 1) * half_dev) if step == 1 else range(tile_dev)
        return [(into[l][direction][step - 1], zscale.at[l, direction, step - 1], held)]

    def turn(l, step):
        if step == 0:
            await_scales(l)
            await_up(l, 0)
            for scan_side in range(2):
                sscale[l, scan_side, 0] = jnp.zeros_like(sscale[l, scan_side, 0])
            combine(l, 0, lambda: [], packer(l, None, 0))
            for direction in (0, 1):
                flying[l, direction] = ship(l, direction, 0, halves[direction])
            return
        for direction in (0, 1):
            r = 2 * step - 1 + direction
            await_up(l, r)
            combine(l, r, lambda: arrived(l, direction, step), packer(l, direction, step))
            flying[l, direction] = ship(l, direction, step, pl.ds(0, tile_dev))

    def probe_over_modes():
        arrive(pxb, p0r.at[0])
        total = pp_ref[q]
        for k in range(modes - 1):
            total = total + pxb[k]
        pxs[...] = total.reshape(pxs.shape)
        for n, scan, d in peers:
            go(send(pxs.at[d], pyb.at[n], p1s.at[0], p1r.at[0], scan, q))

    def probe_over_plane():
        arrive(pyb, p1r.at[0])
        total = pxs[mine]
        for n in range(7):
            total = total + pyb[n]
        pzs[...] = total
        for k, scan in enumerate(column):
            go(send(pzs, pzb.at[k], p2s.at[0], p2r.at[0], scan, q))

    def probe_over_ring():
        arrive(pzb, p2r.at[0])
        total = pzs[...]
        for k in range(RING - 1):
            total = total + pzb[k]
        pg_ref[mine] = total * scale
        for n, scan, d in peers:
            go(send(pg_ref.at[mine], pg_ref.at[mine], p3s.at[0], p3r.at[0], scan, q))

    def keep(l):
        def put(k, value):
            out_ref[k, l] = value

        return put

    gather_e(1)
    lay(1)
    code(1)
    for r in range(3):
        yield_up(1, r)
    for k, m in enumerate(others):
        go(send(pp_ref.at[m], pxb.at[k], p0s.at[0], p0r.at[0], here, m))
    gather_e(0)
    lay(0)
    turn(1, 0)
    code(0)
    for r in range(3):
        yield_up(0, r)
    yield_up(1, 3)
    yield_up(1, 4)
    turn(1, 1)
    turn(0, 0)
    yield_up(0, 3)
    yield_up(0, 4)
    probe_over_modes()
    yield_up(1, 5)
    yield_up(1, 6)
    turn(0, 1)
    yield_up(0, 5)
    yield_up(0, 6)
    turn(1, 2)
    yield_up(1, 7)
    probe_over_plane()
    turn(0, 2)
    yield_up(0, 7)
    turn(1, 3)
    probe_over_ring()
    turn(0, 3)
    for l in (1, 0):
        await_up(l, 7)
        combine(l, 7, lambda: arrived(l, 0, 4) + arrived(l, 1, 4), keep(l))
    arrive(pg_ref.at[pl.ds(0, 7)], p3r.at[0])

    def departed(ref, sem):
        send(ref, ref, sem, sem, here, q).wait_send()

    for l in range(2):
        departed(ybuf.at[l], zs.at[l])
        departed(ybuf.at[l], ys.at[l])
        departed(xbuf.at[l], xs.at[l])
        departed(ebuf.at[l], es.at[l])
        departed(e_out.at[l], ess.at[l])
        departed(codes.at[l, pl.ds(0, 7)], ts.at[l])
        departed(cscale.at[l, pl.ds(0, 7)], tcs.at[l])
        departed(codes.at[l, pl.ds(0, 7)], us.at[l])
        departed(cscale.at[l], ucs.at[l])
    departed(pall_ref.at[pl.ds(0, modes - 1)], ps.at[0])
    departed(pxb, p0s.at[0])
    departed(pyb, p1s.at[0])
    departed(pzb, p2s.at[0])
    departed(pg_ref.at[pl.ds(0, 7)], p3s.at[0])


def gradients(tile_owner, block_tiles, positions, tiles, probe, counts, tables, modes, scale):
    tile_dev, slices, parts, side, _ = tiles.shape
    quarter = side // modes
    batch = positions.shape[0]
    npos = batch // modes
    dma = pltpu.SemaphoreType.DMA
    smem, anywhere, vmem = (pl.BlockSpec(memory_space=space) for space in (pltpu.SMEM, pl.ANY, pltpu.VMEM))
    tile = (parts, quarter, side)

    def wide(*dims):
        return pltpu.VMEM(dims, jnp.float32)

    def half(*dims):
        return pltpu.VMEM(dims, jnp.bfloat16)

    def short(*dims):
        return pltpu.VMEM(dims, jnp.int16)

    piece = (parts * side // 8, side)
    scratch = [half(tile_dev, *tile)] * 16 + [half(8 * RING, *tile)] * 2
    scratch += [
        half(slices, 7, RING, *tile),
        half(slices, modes - 1, npos, *tile),
        half(slices, modes, npos, *tile),
        wide(modes, parts, side, side),
        pltpu.VMEM((npos, side, side), counts.dtype),
        half(*tables.shape),
        short(slices, modes - 1, npos, *tile),
        short(modes, npos, *tile),
        short(modes, npos, *tile),
        wide(modes, 8, side),
        wide(modes, 8, side),
        wide(slices, modes - 1, 8, side),
        wide(modes, parts * side, side),
        half(2 * modes * side, 2 * side),
        half(2 * modes * side, 2 * side),
        half(npos // 2, 2 * modes * side, 2 * side),
        half(npos // 2, 2 * modes * side, 2 * side),
        half(2 * side, 2 * modes * side),
        half(2 * side, 2 * modes * side),
        wide(2, parts, side, side),
        wide(npos, parts, side, side),
        wide(npos, modes, parts, side, side),
        wide(2, parts, side, side),
    ]
    scratch += [wide(2, batch + 1, *tile)] * 4
    scratch += [short(8, *tile)] * 16 + [wide(8, RING, side)] * 2
    scratch += [short(tile_dev, *tile)] * 32
    scratch += [
        short(slices, 8, RING, *tile),
        wide(slices, 8, RING, side),
        wide(slices, 2, 4, tile_dev, side),
        wide(slices, 2, 4, tile_dev, side),
        wide(9, *tile),
        wide(modes - 1, parts * side, side),
        wide(8, *piece),
        wide(7, *piece),
        wide(*piece),
        wide(RING - 1, *piece),
        pltpu.VMEM((5, RING, side), jnp.int32),
        pltpu.SMEM((5, RING, side), jnp.int32),
    ]
    sizes = [(6,), (slices,), (slices, 2, 4), (slices,), (slices,), (slices,), (slices, npos)]
    sizes += [(1,), (1,), (slices,), (slices,), (slices,), (slices,)]
    sizes += [(slices,), (slices, RING), (slices,), (slices,), (slices,), (slices, 2, 4), (slices,), (slices, 2, 4)]
    sizes += [(1,)] * 8
    scratch += [dma(size) for size in sizes]
    return pl.pallas_call(
        functools.partial(kernel_body, scale=scale),
        in_specs=[smem, smem, smem, vmem, anywhere, anywhere, anywhere, anywhere],
        out_specs=[vmem, vmem],
        out_shape=[
            jax.ShapeDtypeStruct((tile_dev, slices) + tile, jnp.float32),
            jax.ShapeDtypeStruct((8,) + piece, jnp.float32),
        ],
        scratch_shapes=scratch,
        compiler_params=pltpu.CompilerParams(
            collective_id=0, has_side_effects=True, vmem_limit_bytes=60 * MIB
        ),
        name="gradients",
    )(tile_owner, block_tiles, positions.T, tile_owner.reshape(-1, side), tiles, probe, counts, tables)


def shards(object_tiles, tile_owner, block_tiles, positions, counts, probe):
    scan_count = lax.axis_size("scan")
    mode_count = lax.axis_size("mode")
    batch = positions.shape[0]
    tables = jnp.asarray(transform_tables(object_tiles.shape[3]))
    object_grad, probe_grad = gradients(
        tile_owner, block_tiles, positions, object_tiles, probe, counts, tables, mode_count, 1.0 / (batch * scan_count)
    )
    return (object_grad, probe_grad.reshape(probe.shape))


def solution(mesh):
    placed = (
        P("scan", None, None, None, None),
        P(),
        P(),
        P("scan", None),
        P("scan", None, None),
        P("mode", None, None, None),
    )
    return jax.shard_map(
        shards,
        mesh=mesh,
        in_specs=placed,
        out_specs=(P("scan", None, None, "mode", None), P("mode", None, None, None)),
        check_vma=False,
    )
```

```python
import functools

import jax
import jax.numpy as jnp
import ml_dtypes
import numpy as np
from jax import lax
from jax.experimental import pallas as pl
from jax.experimental.pallas import tpu as pltpu
from jax.sharding import PartitionSpec as P

background = 0.25
fresnel_number = 1.0
MIB = 1024 * 1024
RING = 8
STEPS = 32767.0


def split_const(matrix):
    hi = matrix.astype(ml_dtypes.bfloat16)
    lo = (matrix - hi.astype(np.float64)).astype(ml_dtypes.bfloat16)
    return hi, lo


def transform_tables(side):
    index = np.arange(side)
    four = np.exp(-2j * np.pi * (index[:, None] * index[None, :] % side) / side) / np.sqrt(side)
    frequency = np.where(index < side // 2, index, index - side) / side
    chirp = np.exp(-1j * np.pi * fresnel_number * frequency * frequency)
    prop = (four.conj() * chirp[None, :]) @ four
    blocks = []
    for matrix in (four, prop):
        re, im = matrix.real, matrix.imag
        blocks.append(np.block([[re, im], [-im, re]]))
        blocks.append(np.block([[re, -im], [im, re]]))
    parts = []
    for block in blocks:
        parts.extend(split_const(block))
    return np.stack(parts)


def split_parts(value):
    hi = value.astype(jnp.bfloat16)
    lo = (value - hi.astype(jnp.float32)).astype(jnp.bfloat16)
    return hi, lo


def dot(a, b):
    return jnp.dot(a, b, preferred_element_type=jnp.float32)


def spot(scan):
    return scan // (2 * RING), scan // 2 % RING, scan % 2


def at_spot(y, z, core):
    return (y * RING + z) * 2 + core


def plane_peers(y, z, core):
    peers = []
    for number in range(1, 8):
        there_y, there_core = (y + number // 2) % 4, (core + number % 2) % 2
        peers.append((number - 1, at_spot(there_y, z, there_core), there_y * 2 + there_core))
    return peers


def send(src, dst, send_sem, recv_sem, scan, mode):
    return pltpu.make_async_remote_copy(
        src_ref=src,
        dst_ref=dst,
        send_sem=send_sem,
        recv_sem=recv_sem,
        device_id={"scan": scan, "mode": mode},
        device_id_type=pl.DeviceIdType.MESH,
    )


def received(ref, sem, scan, mode):
    send(ref, ref, sem, sem, scan, mode).wait_recv()


def meet(partners):
    barrier = pltpu.get_barrier_semaphore()
    for scan, mode in partners:
        pl.semaphore_signal(
            barrier, inc=1, device_id={"scan": scan, "mode": mode}, device_id_type=pl.DeviceIdType.MESH
        )
    pl.semaphore_wait(barrier, len(partners))


def home(owner):
    y, z, core = owner >> 4, (owner >> 1) & (RING - 1), owner & 1
    return (y * 2 + core) * RING + z


def column_scale(value):
    most = jnp.max(jnp.max(jnp.abs(value), axis=0), axis=0, keepdims=True)
    return jnp.maximum(most, 1e-30) * (1.0 / STEPS)


def encode(value, scale):
    return jnp.round(value * (1.0 / scale)).astype(jnp.int32).astype(jnp.int16)


def decode(code):
    return code.astype(jnp.int32).astype(jnp.float32)


def kernel_body(owner_ref, first_ref, pos_ref, owner_rows, obj_ref, probe_ref, counts_any, tab_any, out_ref, pg_ref, *scratch, scale=1.0):
    names = iter(scratch)

    def several(count):
        return [next(names) for _ in range(count)]

    chunk = [several(8) for _ in range(2)]
    win = several(2)
    ybuf, xbuf, x_ref, pall_ref, counts_ref, tab_ref, ebuf = several(7)
    eq_ref, e_steps = several(2), several(2)
    e_out, pp_ref = several(2)
    a_hi, a_lo, b_hi, b_lo, c_hi, c_lo, planes_ref, xroll, wave_ref, sum_ref = several(10)
    left_sum, right_sum = several(2), several(2)
    rbuf = [several(8) for _ in range(2)]
    rscale = several(2)
    out_of = [[several(4) for _ in range(2)] for _ in range(2)]
    into = [[several(4) for _ in range(2)] for _ in range(2)]
    codes, cscale, sscale, zscale, given, pxb, pxs, pyb, pzs, pzb, table_ref, pick_ref = several(12)
    local_sem, zs, zr, ys, yr, xs, xr, ps, pr, es, er, ess, esr = several(13)
    ts, tr, tcs, tcr, us, ur, ucs, ucr, p0s, p0r, p1s, p1r, p2s, p2r, p3s, p3r = several(16)

    here, q = lax.axis_index("scan"), lax.axis_index("mode")
    y, z, core = spot(here)
    mine = y * 2 + core
    tile_dev, _, quarter, side = chunk[0][0].shape
    modes, npos = x_ref.shape[1:3]
    batch = modes * npos
    local = [
        pltpu.make_async_copy(
            obj_ref.at[:, l, :, pl.ds(q * quarter, quarter), :], chunk[l][0], local_sem.at[l]
        )
        for l in range(2)
    ]
    local.extend(
        [
            pltpu.make_async_copy(probe_ref.at[0], pall_ref.at[q], local_sem.at[2]),
            pltpu.make_async_copy(tab_any, tab_ref, local_sem.at[3]),
            pltpu.make_async_copy(counts_any.at[pl.ds(q * npos, npos)], counts_ref, local_sem.at[4]),
        ]
    )
    for copy in local:
        copy.start()
    right, left = at_spot(y, (z + 1) % RING, core), at_spot(y, (z + RING - 1) % RING, core)
    peers = plane_peers(y, z, core)
    column = [at_spot(y, (z + k) % RING, core) for k in range(1, RING)]
    others = [(q + k) % modes for k in range(1, modes)]
    meet([(scan, q) for scan in column] + [(scan, q) for _, scan, _ in peers] + [(here, m) for m in others])

    def go(copy):
        copy.start()
        return copy

    def arrive(ref, sem):
        received(ref, sem, here, q)


    def pass_on(l, direction, step):
        rightward = chunk[l][0:4] + chunk[l][7:8]
        leftward = chunk[l][0:1] + chunk[l][4:8]
        lane = (rightward, leftward)[direction]
        scan = (right, left)[direction]
        src, dst = lane[step], lane[step + 1]
        if step == 3:
            part = pl.ds(direction * (tile_dev // 2), tile_dev // 2)
            src, dst = src.at[part], dst.at[part]
        return go(send(src, dst, zs.at[l], zr.at[l, direction, step], scan, q))

    moving = {}

    def step_on(l, step):
        for direction in (0, 1):
            if step > 0:
                moving[l, direction].wait_recv()
            moving[l, direction] = pass_on(l, direction, step)

    for l in range(2):
        local[l].wait()
        step_on(l, 0)
    for k, m in enumerate(others):
        go(send(probe_ref.at[0], pall_ref.at[q], ps.at[0], pr.at[0], here, m))

    lanes = lax.broadcasted_iota(jnp.int32, (RING, side), 1)
    depth = lax.broadcasted_iota(jnp.int32, (RING, side), 0)
    zero = jnp.zeros((RING, side), jnp.int32)
    owners = [owner_rows[n : n + 1, :] for n in range(owner_rows.shape[0])]
    my_first = first_ref[here, 0]
    span = first_ref.shape[0] // 2
    ring = at_spot(y, depth, core)
    owned = [jnp.where(row == ring, 1, 0) for row in owners]
    picks = []
    slots = zero
    for d in range(8):
        first = first_ref[at_spot(d // 2, z, d % 2), 0]
        before, slot = zero, zero
        ring = at_spot(d // 2, depth, d % 2)
        for n, row in enumerate(owners):
            tile = lanes + n * side
            before = before + jnp.where(tile < first, owned[n], 0)
            inside = (tile >= my_first) & (tile < my_first + 2 * span) & (row == ring)
            slot = jnp.maximum(slot, jnp.where(inside, tile - my_first, 0))
        picks.append(jnp.sum(before, axis=1, keepdims=True))
        slots = jnp.where(lanes == d, jnp.max(slot, axis=1, keepdims=True), slots)
    chosen, order, ends = zero, zero, zero
    for d in range(8):
        ahead = jnp.zeros_like(picks[d])
        for e in range(8):
            if e != d:
                ahead = ahead + jnp.where(picks[e] <= picks[d] if e < d else picks[e] < picks[d], 1, 0)
        chosen = jnp.where(lanes == d, picks[d], chosen)
        order = order + jnp.where(lanes == ahead, d, 0)
        ends = ends + jnp.where(picks[d] <= lanes, 1, 0)
    places = [pos_ref[1, j] >> 7 for j in range(batch)]
    ranks = [jnp.int32(0)] * batch
    for j in range(batch):
        for k in range(j):
            earlier = jnp.where(places[k] <= places[j], 1, 0)
            ranks[j] = ranks[j] + earlier
            ranks[k] = ranks[k] + (1 - earlier)
    queue, counted = zero, zero
    for j in range(batch):
        queue = queue + jnp.where(lanes == ranks[j], j, 0)
        counted = counted + jnp.where(places[j] < lanes - 1, 1, 0)
    for n, table in enumerate((chosen, order, ends, slots, jnp.where(depth == 0, queue, counted))):
        table_ref[n] = table
    pick_copy = pltpu.make_async_copy(table_ref, pick_ref, local_sem.at[5])
    pick_copy.start()
    pick_copy.wait()

    rounds = [0, -1, 1, -2, 2, -3, 3, 4]

    def offer(l, r):
        zi = (z + rounds[r] + RING) % RING
        buf = chunk[l][(0, 1, 4, 2, 5, 3, 6, 7)[r]]
        for n, scan, d in peers:
            ybuf[l, n, r] = buf[pick_ref[0, zi, d]]
            go(send(ybuf.at[l, n, r], win[l].at[mine * RING + zi], ys.at[l], yr.at[l], scan, q))
        win[l][mine * RING + zi] = buf[pick_ref[0, zi, mine]]

    shape = (2, quarter, side)
    rows = lax.broadcasted_iota(jnp.int32, shape, 1) + q * quarter
    cols = lax.broadcasted_iota(jnp.int32, shape, 2)

    def piece(l, j):
        row, col = pos_ref[0, j], pos_ref[1, j]
        near = my_first + (col >> 7)
        far = my_first + jnp.minimum((col >> 7) + 1, span - 1)
        tiles = [win[l][home(owner_ref[t])].astype(jnp.float32) for t in (near, far, near + span, far + span)]
        kept = cols >= (col & (side - 1))
        upper = jnp.where(kept, tiles[0], tiles[1])
        lower = jnp.where(kept, tiles[2], tiles[3])
        return jnp.where(rows >= row, upper, lower).astype(jnp.bfloat16)

    def x_copy(l, k, i, mode, target):
        return send(xbuf.at[l, k, i], x_ref.at[l, target, i], xs.at[l], xr.at[l, i], here, mode)

    def share(l):
        def pack(i, carry):
            for k in (1, 0, 2):
                xbuf[l, k, i] = piece(l, others[k] * npos + i)
                x_copy(l, k, i, others[k], q).start()
            x_ref[l, q, i] = piece(l, q * npos + i)
            return carry

        lax.fori_loop(0, npos, pack, 0)

    for l in range(2):
        offer(l, 0)
    step_on(0, 1)
    offer(0, 1)
    offer(0, 2)
    step_on(1, 1)
    offer(1, 1)
    offer(1, 2)
    step_on(0, 2)
    offer(0, 3)
    offer(0, 4)
    step_on(1, 2)
    offer(1, 3)
    step_on(0, 3)
    offer(0, 5)
    offer(0, 6)
    step_on(1, 3)
    offer(1, 4)
    for direction in (0, 1):
        moving[0, direction].wait_recv()
    offer(0, 7)
    offer(1, 5)
    for direction in (0, 1):
        moving[1, direction].wait_recv()
    offer(1, 6)
    offer(1, 7)
    for l in range(2):
        arrive(ybuf.at[l], yr.at[l])
        share(l)
    for copy in local[2:]:
        copy.wait()
    arrive(pall_ref.at[pl.ds(0, modes - 1)], pr.at[0])


    pair = 2
    count = pair * modes

    def block(m):
        return slice(m * side, (m + 1) * side)

    def load(hi_ref, lo_ref, fields):
        for m, (re, im) in enumerate(fields):
            rh, rl = split_parts(re)
            ih, il = split_parts(im)
            hi_ref[block(m), 0:side] = rh
            hi_ref[block(m), side : 2 * side] = ih
            lo_ref[block(m), 0:side] = rl
            lo_ref[block(m), side : 2 * side] = il

    def two_sided(right_table, left_table, hi_ref, lo_ref):
        for m in range(count):
            bh, bl = tab_ref[2 * right_table], tab_ref[2 * right_table + 1]
            whole = dot(hi_ref[block(m)], bh) + dot(lo_ref[block(m)], bh) + dot(hi_ref[block(m)], bl)
            hi, lo = split_parts(whole)
            c_hi[0:side, block(m)] = hi[:, 0:side]
            c_hi[side : 2 * side, block(m)] = hi[:, side : 2 * side]
            c_lo[0:side, block(m)] = lo[:, 0:side]
            c_lo[side : 2 * side, block(m)] = lo[:, side : 2 * side]
        lh, ll = tab_ref[2 * left_table], tab_ref[2 * left_table + 1]
        out = []
        for h in range(count // 2):
            cut = slice(h * 2 * side, (h + 1) * 2 * side)
            whole = dot(lh, c_hi[:, cut]) + dot(lh, c_lo[:, cut]) + dot(ll, c_hi[:, cut])
            for k in range(2):
                out.append((whole[0:side, block(k)], whole[side : 2 * side, block(k)]))
        return out

    def patch(l, p, n):
        arrive(x_ref.at[l, pl.ds(0, modes - 1), p], xr.at[l, p])
        row, col = pos_ref[0, q * npos + p], pos_ref[1, q * npos + p]
        for part in range(2):
            whole = jnp.concatenate([x_ref[l, k, p, part].astype(jnp.float32) for k in range(modes)], axis=0)
            whole = pltpu.roll(whole, (side - row) & (side - 1), 0)
            planes_ref[n, part] = pltpu.roll(whole, (side - (col & (side - 1))) & (side - 1), 1)

    def plane(n):
        return planes_ref[n, 0], planes_ref[n, 1]

    def wave(p, m):
        return wave_ref[p, m, 0], wave_ref[p, m, 1]

    def shone(m):
        return pall_ref[m, 0], pall_ref[m, 1]

    def times(wave, field):
        (wr, wi), (fr, fi) = wave, field
        return wr * fr - wi * fi, wr * fi + wi * fr

    def conj_times(wave, field):
        (wr, wi), (fr, fi) = wave, field
        return wr * fr + wi * fi, wr * fi - wi * fr

    def e_copy(l, k, p, mode, target):
        return send(ebuf.at[l, k, p], eq_ref[l].at[target, p], es.at[l], er.at[l], here, mode)

    def hand_out(l, p, n, total):
        row, col = pos_ref[0, q * npos + p], pos_ref[1, q * npos + p]
        for part in range(2):
            sum_ref[n, part] = pltpu.roll(pltpu.roll(total[part], row & (side - 1), 0), col & (side - 1), 1)
        def coded(mode):
            value = sum_ref[n, :, pl.ds(pl.multiple_of(mode * quarter, quarter), quarter)]
            step = column_scale(value)
            return encode(value, step), step

        for k in range(modes - 1):
            ebuf[l, k, p], e_out[l, k, pl.ds(p, 1)] = coded(others[k])
            e_copy(l, k, p, others[k], q).start()
        eq_ref[l][q, p], e_steps[l][q, pl.ds(p, 1)] = coded(q)

    def hand_out_steps(l):
        for k, m in enumerate(others):
            go(send(e_out.at[l, k], e_steps[l].at[q], ess.at[l], esr.at[l], here, m))

    def each(i):
        return [(n, i * pair + n, m) for n in range(pair) for m in range(modes)]

    def enter(i, carry):
        for n in range(pair):
            patch(0, i * pair + n, n)
            for part in range(2):
                xroll[i * pair + n, part] = planes_ref[n, part]
        load(a_hi, a_lo, [times(shone(m), plane(n)) for n, p, m in each(i)])
        for (n, p, m), (re, im) in zip(each(i), two_sided(2, 3, a_hi, a_lo)):
            wave_ref[p, m, 0] = re
            wave_ref[p, m, 1] = im
        return carry

    def summed(terms):
        return [functools.reduce(jnp.add, part) for part in zip(*terms)]

    def detect(i, carry):
        for n in range(pair):
            patch(1, i * pair + n, n)
        load(a_hi, a_lo, [times(wave(p, m), plane(n)) for n, p, m in each(i)])
        far = two_sided(0, 1, a_hi, a_lo)
        weighted = []
        for n in range(pair):
            mine_far = far[n * modes : (n + 1) * modes]
            intensity = background
            for re, im in mine_far:
                intensity = intensity + (re * re + im * im)
            weight = 1.0 - counts_ref[i * pair + n].astype(jnp.float32) / intensity
            weighted.extend((weight * re, weight * im) for re, im in mine_far)
        load(a_hi, a_lo, weighted)
        grads = two_sided(1, 0, a_hi, a_lo)
        load(b_hi.at[i], b_lo.at[i], [conj_times(plane(n), grad) for (n, p, m), grad in zip(each(i), grads)])
        terms = [conj_times(wave(p, m), grad) for (n, p, m), grad in zip(each(i), grads)]
        for n in range(pair):
            hand_out(1, i * pair + n, n, summed(terms[n * modes : (n + 1) * modes]))
        return carry

    def leave(i, carry):
        grads = two_sided(3, 2, b_hi.at[i], b_lo.at[i])
        for m in range(modes):
            terms = [conj_times((xroll[p, 0], xroll[p, 1]), grad) for (n, p, k), grad in zip(each(i), grads) if k == m]
            for part, term in enumerate(summed(terms)):
                pp_ref[m, part * side : (part + 1) * side] += term
        terms = [conj_times(shone(m), grad) for (n, p, m), grad in zip(each(i), grads)]
        for n in range(pair):
            hand_out(0, i * pair + n, n, summed(terms[n * modes : (n + 1) * modes]))
        return carry

    lax.fori_loop(0, npos // pair, enter, 0)
    e_out[...] = jnp.zeros_like(e_out)
    lax.fori_loop(0, npos // pair, detect, 0)
    hand_out_steps(1)
    pp_ref[...] = jnp.zeros_like(pp_ref)
    lax.fori_loop(0, npos // pair, leave, 0)
    hand_out_steps(0)


    def gather_e(l):
        arrive(eq_ref[l].at[pl.ds(0, modes - 1)], er.at[l])
        arrive(e_steps[l].at[pl.ds(0, modes - 1)], esr.at[l])

    def lay(l):
        blank = jnp.zeros(shape, jnp.float32)
        for u in range(2):
            left_sum[l][u, 0] = blank
            right_sum[l][u, 0] = blank

        def add(n, carry):
            j = pick_ref[4, 0, n]
            kept = cols >= (pos_ref[1, j] & (side - 1))
            upper = rows >= pos_ref[0, j]
            term = decode(eq_ref[l][j // npos, j % npos]) * e_steps[l][j // npos, pl.ds(j % npos, 1)]
            lefts, rights = jnp.where(kept, term, 0.0), jnp.where(kept, 0.0, term)
            for sums, part in ((left_sum[l], lefts), (right_sum[l], rights)):
                sums[0, n + 1] = sums[0, n] + jnp.where(upper, part, 0.0)
                sums[1, n + 1] = sums[1, n] + jnp.where(upper, 0.0, part)
            return carry

        lax.fori_loop(0, batch, add, 0)

    back = [4, 3, -3, 2, -2, 1, -1, 0]

    def zi(r):
        return (z + back[r] + RING) % RING

    def code(l):
        def one(place, carry):
            for d in range(8):
                slot = pick_ref[3, place, d]
                u, w = slot >> 5, slot & (span - 1)
                low, middle, high = pick_ref[4, 1, w], pick_ref[4, 1, w + 1], pick_ref[4, 1, w + 2]
                value = (left_sum[l][u, high] - left_sum[l][u, middle]) + (right_sum[l][u, middle] - right_sum[l][u, low])
                step = column_scale(value)
                cscale[l, d, pl.ds(place, 1)] = step
                codes[l, d, place] = encode(value, step)
            return carry

        lax.fori_loop(0, RING, one, 0)
        for n, scan, d in peers:
            go(send(cscale.at[l, d], rscale[l].at[mine], tcs.at[l], tcr.at[l], scan, q))
        rscale[l][mine] = cscale[l, mine]

    def yield_up(l, r):
        for n, scan, d in peers:
            go(send(codes.at[l, d, zi(r)], rbuf[l][r].at[mine], ts.at[l], tr.at[l, r], scan, q))
        rbuf[l][r][mine] = codes[l, mine, zi(r)]

    def await_up(l, r):
        arrive(rbuf[l][r].at[pl.ds(0, 7)], tr.at[l, r])

    def await_scales(l):
        arrive(rscale[l].at[pl.ds(0, 7)], tcr.at[l])

    given[0] = jnp.zeros(shape, jnp.float32)

    def combine(l, r, received, use):
        place = zi(r)
        total = jnp.zeros(shape, jnp.float32)
        for n in range(8):
            giver = pick_ref[1, place, n]
            total = total + decode(rbuf[l][r][giver]) * rscale[l][giver, pl.ds(place, 1)]
            given[n + 1] = total
        received = received()
        start = 0
        for k in range(tile_dev):
            end = pick_ref[2, place, k]
            value = given[end] - given[start]
            for ref, ref_scale, held in received:
                if k in held:
                    value = value + decode(ref[k]) * ref_scale[k : k + 1]
            use(k, value)
            start = end

    def ship(l, direction, step, tiles):
        at = (l, direction, step)
        buf, to = out_of[l][direction][step].at[tiles], into[l][direction][step].at[tiles]
        scan = (right, left)[direction]
        return (
            go(send(sscale.at[at], zscale.at[at], ucs.at[l], ucr.at[at], scan, q)),
            go(send(buf, to, us.at[l], ur.at[at], scan, q)),
        )

    def packer(l, direction, step):
        def pack(k, value):
            side_of = (k // half_dev) if direction is None else direction
            step_size = column_scale(value)
            sscale[l, side_of, step, k : k + 1] = step_size
            out_of[l][side_of][step][k] = encode(value, step_size)

        return pack

    flying = {}
    half_dev = tile_dev // 2
    halves = (pl.ds(0, half_dev), pl.ds(half_dev, half_dev))

    def arrived(l, direction, step):
        for copy in flying[l, direction]:
            copy.wait_recv()
        held = range(direction * half_dev, (direction + 1) * half_dev) if step == 1 else range(tile_dev)
        return [(into[l][direction][step - 1], zscale.at[l, direction, step - 1], held)]

    def turn(l, step):
        if step == 0:
            await_scales(l)
            await_up(l, 0)
            for scan_side in range(2):
                sscale[l, scan_side, 0] = jnp.zeros_like(sscale[l, scan_side, 0])
            combine(l, 0, lambda: [], packer(l, None, 0))
            for direction in (0, 1):
                flying[l, direction] = ship(l, direction, 0, halves[direction])
            return
        for direction in (0, 1):
            r = 2 * step - 1 + direction
            await_up(l, r)
            combine(l, r, lambda: arrived(l, direction, step), packer(l, direction, step))
            flying[l, direction] = ship(l, direction, step, pl.ds(0, tile_dev))

    def probe_over_modes():
        arrive(pxb, p0r.at[0])
        total = pp_ref[q]
        for k in range(modes - 1):
            total = total + pxb[k]
        pxs[...] = total.reshape(pxs.shape)
        for n, scan, d in peers:
            go(send(pxs.at[d], pyb.at[n], p1s.at[0], p1r.at[0], scan, q))

    def probe_over_plane():
        arrive(pyb, p1r.at[0])
        total = pxs[mine]
        for n in range(7):
            total = total + pyb[n]
        pzs[...] = total
        for k, scan in enumerate(column):
            go(send(pzs, pzb.at[k], p2s.at[0], p2r.at[0], scan, q))

    def probe_over_ring():
        arrive(pzb, p2r.at[0])
        total = pzs[...]
        for k in range(RING - 1):
            total = total + pzb[k]
        pg_ref[mine] = total * scale
        for n, scan, d in peers:
            go(send(pg_ref.at[mine], pg_ref.at[mine], p3s.at[0], p3r.at[0], scan, q))

    def keep(l):
        def put(k, value):
            out_ref[k, l] = value

        return put

    gather_e(1)
    lay(1)
    code(1)
    for r in range(3):
        yield_up(1, r)
    for k, m in enumerate(others):
        go(send(pp_ref.at[m], pxb.at[k], p0s.at[0], p0r.at[0], here, m))
    gather_e(0)
    lay(0)
    turn(1, 0)
    code(0)
    for r in range(3):
        yield_up(0, r)
    yield_up(1, 3)
    yield_up(1, 4)
    turn(1, 1)
    turn(0, 0)
    yield_up(0, 3)
    yield_up(0, 4)
    probe_over_modes()
    yield_up(1, 5)
    yield_up(1, 6)
    turn(0, 1)
    yield_up(0, 5)
    yield_up(0, 6)
    turn(1, 2)
    yield_up(1, 7)
    probe_over_plane()
    yield_up(0, 7)
    turn(0, 2)
    probe_over_ring()
    turn(1, 3)
    turn(0, 3)
    for l in (1, 0):
        await_up(l, 7)
        combine(l, 7, lambda: arrived(l, 0, 4) + arrived(l, 1, 4), keep(l))
    arrive(pg_ref.at[pl.ds(0, 7)], p3r.at[0])

    def departed(ref, sem):
        send(ref, ref, sem, sem, here, q).wait_send()

    for l in range(2):
        departed(ybuf.at[l], zs.at[l])
        departed(ybuf.at[l], ys.at[l])
        departed(xbuf.at[l], xs.at[l])
        departed(ebuf.at[l], es.at[l])
        departed(e_out.at[l], ess.at[l])
        departed(codes.at[l, pl.ds(0, 7)], ts.at[l])
        departed(cscale.at[l, pl.ds(0, 7)], tcs.at[l])
        departed(codes.at[l, pl.ds(0, 7)], us.at[l])
        departed(cscale.at[l], ucs.at[l])
    departed(pall_ref.at[pl.ds(0, modes - 1)], ps.at[0])
    departed(pxb, p0s.at[0])
    departed(pyb, p1s.at[0])
    departed(pzb, p2s.at[0])
    departed(pg_ref.at[pl.ds(0, 7)], p3s.at[0])


def gradients(tile_owner, block_tiles, positions, tiles, probe, counts, tables, modes, scale):
    tile_dev, slices, parts, side, _ = tiles.shape
    quarter = side // modes
    batch = positions.shape[0]
    npos = batch // modes
    dma = pltpu.SemaphoreType.DMA
    smem, anywhere, vmem = (pl.BlockSpec(memory_space=space) for space in (pltpu.SMEM, pl.ANY, pltpu.VMEM))
    tile = (parts, quarter, side)

    def wide(*dims):
        return pltpu.VMEM(dims, jnp.float32)

    def half(*dims):
        return pltpu.VMEM(dims, jnp.bfloat16)

    def short(*dims):
        return pltpu.VMEM(dims, jnp.int16)

    piece = (parts * side // 8, side)
    scratch = [half(tile_dev, *tile)] * 16 + [half(8 * RING, *tile)] * 2
    scratch += [
        half(slices, 7, RING, *tile),
        half(slices, modes - 1, npos, *tile),
        half(slices, modes, npos, *tile),
        wide(modes, parts, side, side),
        pltpu.VMEM((npos, side, side), counts.dtype),
        half(*tables.shape),
        short(slices, modes - 1, npos, *tile),
        short(modes, npos, *tile),
        short(modes, npos, *tile),
        wide(modes, 8, side),
        wide(modes, 8, side),
        wide(slices, modes - 1, 8, side),
        wide(modes, parts * side, side),
        half(2 * modes * side, 2 * side),
        half(2 * modes * side, 2 * side),
        half(npos // 2, 2 * modes * side, 2 * side),
        half(npos // 2, 2 * modes * side, 2 * side),
        half(2 * side, 2 * modes * side),
        half(2 * side, 2 * modes * side),
        wide(2, parts, side, side),
        wide(npos, parts, side, side),
        wide(npos, modes, parts, side, side),
        wide(2, parts, side, side),
    ]
    scratch += [wide(2, batch + 1, *tile)] * 4
    scratch += [short(8, *tile)] * 16 + [wide(8, RING, side)] * 2
    scratch += [short(tile_dev, *tile)] * 32
    scratch += [
        short(slices, 8, RING, *tile),
        wide(slices, 8, RING, side),
        wide(slices, 2, 4, tile_dev, side),
        wide(slices, 2, 4, tile_dev, side),
        wide(9, *tile),
        wide(modes - 1, parts * side, side),
        wide(8, *piece),
        wide(7, *piece),
        wide(*piece),
        wide(RING - 1, *piece),
        pltpu.VMEM((5, RING, side), jnp.int32),
        pltpu.SMEM((5, RING, side), jnp.int32),
    ]
    sizes = [(6,), (slices,), (slices, 2, 4), (slices,), (slices,), (slices,), (slices, npos)]
    sizes += [(1,), (1,), (slices,), (slices,), (slices,), (slices,)]
    sizes += [(slices,), (slices, RING), (slices,), (slices,), (slices,), (slices, 2, 4), (slices,), (slices, 2, 4)]
    sizes += [(1,)] * 8
    scratch += [dma(size) for size in sizes]
    return pl.pallas_call(
        functools.partial(kernel_body, scale=scale),
        in_specs=[smem, smem, smem, vmem, anywhere, anywhere, anywhere, anywhere],
        out_specs=[vmem, vmem],
        out_shape=[
            jax.ShapeDtypeStruct((tile_dev, slices) + tile, jnp.float32),
            jax.ShapeDtypeStruct((8,) + piece, jnp.float32),
        ],
        scratch_shapes=scratch,
        compiler_params=pltpu.CompilerParams(
            collective_id=0, has_side_effects=True, vmem_limit_bytes=60 * MIB
        ),
        name="gradients",
    )(tile_owner, block_tiles, positions.T, tile_owner.reshape(-1, side), tiles, probe, counts, tables)


def shards(object_tiles, tile_owner, block_tiles, positions, counts, probe):
    scan_count = lax.axis_size("scan")
    mode_count = lax.axis_size("mode")
    batch = positions.shape[0]
    tables = jnp.asarray(transform_tables(object_tiles.shape[3]))
    object_grad, probe_grad = gradients(
        tile_owner, block_tiles, positions, object_tiles, probe, counts, tables, mode_count, 1.0 / (batch * scan_count)
    )
    return (object_grad, probe_grad.reshape(probe.shape))


def solution(mesh):
    placed = (
        P("scan", None, None, None, None),
        P(),
        P(),
        P("scan", None),
        P("scan", None, None),
        P("mode", None, None, None),
    )
    return jax.shard_map(
        shards,
        mesh=mesh,
        in_specs=placed,
        out_specs=(P("scan", None, None, "mode", None), P("mode", None, None, None)),
        check_vma=False,
    )
```
